32 devices in a mesh: dp: 4 (over z), seq: 8 (over y, x, core).
Axes of the slice: x: 2, y: 2, z: 4, core: 2. Of those that a mesh axis runs over, the one named last changes fastest.
Arguments:
- inputs: bfloat16 [8, 1536, 1600], P('dp', 'seq'), may hold values from -6 to 6
- segments: int32 [8, 1536], P('dp'), may hold values from 0 to 7, as said below
- cotangent: bfloat16 [8, 1536, 1600], P('dp', 'seq'), may hold values from -6 to 6
- mix_weight: bfloat16 [1600, 4800], P('seq', 'dp'), may hold values from -0.15625 to 0.15625
- merge_weight: bfloat16 [1600, 1600], P('seq', 'dp'), may hold values from -1.25 to 1.25
- expand_weight: bfloat16 [1600, 6400], P('seq', 'dp'), may hold values from -0.15625 to 0.15625
- shrink_weight: bfloat16 [6400, 1600], P('seq', 'dp'), may hold values from -0.078125 to 0.078125
- first_gain: bfloat16 [1600], P('seq'), may hold values from 0.5 to 1.5
- first_bias: bfloat16 [1600], P('seq'), may hold values from -3 to 3
- query_bias: bfloat16 [1600], P('seq'), may hold values from -3 to 3
- value_bias: bfloat16 [1600], P('seq'), may hold values from -3 to 3
- merge_bias: bfloat16 [1600], P('seq'), may hold values from -3 to 3
- second_gain: bfloat16 [1600], P('seq'), may hold values from 0.5 to 1.5
- second_bias: bfloat16 [1600], P('seq'), may hold values from -3 to 3
- expand_bias: bfloat16 [6400], P('seq'), may hold values from -3 to 3
- shrink_bias: bfloat16 [1600], P('seq'), may hold values from -3 to 3
Outputs:
- block_out: bfloat16 [8, 1536, 1600], P('dp', 'seq')
- input_grad: float32 [8, 1536, 1600], P('dp', 'seq')
- grad_mix: float32 [1600, 4800], P('seq', 'dp')
- grad_merge: float32 [1600, 1600], P('seq', 'dp')
- grad_expand: float32 [1600, 6400], P('seq', 'dp')
- grad_shrink: float32 [6400, 1600], P('seq', 'dp')
- grad_first_gain: float32 [1600], P('seq')
- grad_first_bias: float32 [1600], P('seq')
- grad_query_bias: float32 [1600], P('seq')
- grad_value_bias: float32 [1600], P('seq')
- grad_merge_bias: float32 [1600], P('seq')
- grad_second_gain: float32 [1600], P('seq')
- grad_second_bias: float32 [1600], P('seq')
- grad_expand_bias: float32 [6400], P('seq')
- grad_shrink_bias: float32 [1600], P('seq')
The draws below stay inside these ranges and needn't reach their ends.
Inputs may be any that keep to these rules, and one draw needn't show every extreme that they name: `segments`: document numbers of a packed sequence start at 0 and never fall; a packed sequence holds at most eight documents; among the 2 packed sequences of each dp index, one has a document that starts before position 192 and ends within the last 192 positions.
All inputs are finite; a program needn't handle non-finite values.
Results may differ from the reference program's by a relative error of at most 0.011.
Values may be sent and summed in bfloat16 or wider, within the bound.
No kernel may reach another device: no remote copies, remote signals or barrier semaphores. Data moves between devices by JAX's collectives and lax.ppermute only.
A program may use at most 384 MiB of HBM per device.

```python
import jax
import jax.numpy as jnp
from jax import lax

D = 1600
HEADS = 25
HEAD_DIM = 64
FF = 6400
SEQ_DEV = 192
MICRO = 2
LENGTH = 1536
SEQS = 8


def draw_segments(key, part):
    key = jax.random.fold_in(key, 7)
    key_start, key_end, key_first, key_last, key_pick, key_cuts = jax.random.split(key, 6)
    opening = jax.random.randint(key_start, (SEQS, 1), 2, SEQ_DEV)
    tail = jax.random.randint(key_end, (SEQS, 1), 2, SEQ_DEV)
    closing = LENGTH - tail
    early = jax.random.randint(key_first, (SEQS, 1), 1, opening)
    late = closing + jax.random.randint(key_last, (SEQS, 1), 1, tail)
    positions = jnp.arange(LENGTH, dtype=jnp.int32)[None, :]
    spanning = (positions == opening) | (positions == closing) | (positions == early) | (positions == late)
    scores = jax.random.randint(key_cuts, (SEQS, LENGTH - 1), 0, 262144) * LENGTH + jnp.arange(LENGTH - 1, dtype=jnp.int32)[None, :]
    order = jnp.argsort(scores, axis=1, stable=True).astype(jnp.int32)
    cuts = order[:, :7] + 1
    spread_begins = jnp.any(positions[:, :, None] == cuts[:, None, :], axis=2)
    pick = jax.random.randint(key_pick, (SEQS // MICRO, 1), 0, MICRO)
    chosen = jnp.repeat(pick, MICRO, axis=0)
    within = (jnp.arange(SEQS, dtype=jnp.int32) % MICRO)[:, None]
    begins = jnp.where(within == chosen, spanning, spread_begins)
    return jnp.cumsum(begins.astype(jnp.int32), axis=1).astype(jnp.int32)


def level_of(own_key, extent, pieces, least, top_value):
    def one(dim, parts):
        steps = jax.random.uniform(jax.random.fold_in(jax.random.fold_in(own_key, 6), dim), (parts,), jnp.float32, least / len(pieces), top_value / len(pieces))
        return jnp.repeat(jnp.exp(steps), extent[dim] // parts).reshape((-1,) + (1,) * (len(extent) - dim - 1))

    loudness = one(*pieces[0])
    for cut in pieces[1:]:
        loudness = loudness * one(*cut)
    return loudness


def normal_values(key, shape, deviation, reach, pieces=(), kind=jnp.bfloat16):
    level = level_of(key, shape, pieces, -0.22, 0.18) if pieces else 1.0
    drawn = jax.random.normal(key, shape, jnp.float32) * deviation * level
    return jnp.minimum(jnp.maximum(drawn, -reach), reach).astype(kind)


def setup_inputs(seed: int = 0) -> dict:
    key_list = jax.random.split(jax.random.key(seed), 17)
    inputs = normal_values(key_list[0], (SEQS, LENGTH, D), 1.0, 6.0, ((0, 4), (1, 8)))
    segments = draw_segments(jax.random.fold_in(key_list[16], 71), 0)
    cotangent = normal_values(key_list[2], (SEQS, LENGTH, D), 1.0, 6.0, ((0, 4), (1, 8)))
    mix_weight = normal_values(key_list[3], (D, 3 * D), D ** -0.5, 0.15625, ((0, 8), (1, 4)))
    merge_weight = normal_values(key_list[4], (D, D), (D // 64) ** -0.5, 1.25, ((0, 8), (1, 4)))
    expand_weight = normal_values(key_list[5], (D, FF), D ** -0.5, 0.15625, ((0, 8), (1, 4)))
    shrink_weight = normal_values(key_list[6], (FF, D), FF ** -0.5, 0.078125, ((0, 8), (1, 4)))
    first_gain = jnp.clip(1.0 + 0.1 * jax.random.normal(key_list[7], (D,), jnp.float32), 0.5, 1.5).astype(jnp.bfloat16)
    first_bias = normal_values(key_list[8], (D,), 0.5, 3.0, ((0, 8),))
    query_bias = normal_values(key_list[9], (D,), 0.5, 3.0, ((0, 8),))
    value_bias = normal_values(key_list[10], (D,), 0.5, 3.0, ((0, 8),))
    merge_bias = normal_values(key_list[11], (D,), 0.5, 3.0, ((0, 8),))
    second_gain = jnp.clip(1.0 + 0.1 * jax.random.normal(key_list[12], (D,), jnp.float32), 0.5, 1.5).astype(jnp.bfloat16)
    second_bias = normal_values(key_list[13], (D,), 0.5, 3.0, ((0, 8),))
    expand_bias = normal_values(key_list[14], (FF,), 0.5, 3.0, ((0, 8),))
    shrink_bias = normal_values(key_list[15], (D,), 0.5, 3.0, ((0, 8),))
    return dict(inputs=inputs, segments=segments, cotangent=cotangent, mix_weight=mix_weight, merge_weight=merge_weight, expand_weight=expand_weight, shrink_weight=shrink_weight, first_gain=first_gain, first_bias=first_bias, query_bias=query_bias, value_bias=value_bias, merge_bias=merge_bias, second_gain=second_gain, second_bias=second_bias, expand_bias=expand_bias, shrink_bias=shrink_bias)


@jax.custom_vjp
def low(v):
    return lax.optimization_barrier(v.astype(jnp.bfloat16)).astype(jnp.float32)

@jax.custom_vjp
def low_back(v):
    return v

def low_keep(v):
    return (low(v), None)

def low_pass(kept, grad):
    return (grad,)

def back_keep(v):
    return (v, None)

def back_low(kept, grad):
    return (low(grad),)
low.defvjp(low_keep, low_pass)
low_back.defvjp(back_keep, back_low)

def layer_norm(v, gain, bias):
    center = v - lax.optimization_barrier(jnp.mean(v, axis=-1, keepdims=True))
    spread = lax.optimization_barrier(jnp.mean(center * center, axis=-1, keepdims=True))
    return center * lax.rsqrt(spread + 1e-05) * gain + bias

def gelu_tanh(v):
    return 0.5 * v * (1.0 + jnp.tanh(0.7978845608028654 * (v + 0.044715 * v * v * v)))

def attend(query, key, value, segs):
    block = min(512, LENGTH)
    count = LENGTH // block
    heads_key = key.reshape(LENGTH, HEADS, HEAD_DIM)
    heads_value = value.reshape(LENGTH, HEADS, HEAD_DIM)
    positions = jnp.arange(LENGTH, dtype=jnp.int32)

    def one_block(start):
        rows_q = lax.dynamic_slice_in_dim(query, start, block, 0).reshape(block, HEADS, HEAD_DIM)
        seg_q = lax.dynamic_slice_in_dim(segs, start, block, 0)
        pos_q = start + jnp.arange(block, dtype=jnp.int32)
        visible = (seg_q[:, None] == segs[None, :]) & (positions[None, :] <= pos_q[:, None])
        scores = jnp.einsum('qhd,khd->hqk', rows_q, heads_key, precision=lax.Precision.HIGHEST) * HEAD_DIM ** (-0.5)
        scores = low_back(scores)
        scores = jnp.where(visible[None], scores, -1e+30)
        top = lax.optimization_barrier(jnp.max(scores, axis=-1, keepdims=True))
        expo = jnp.exp(scores - top)
        probs = expo / lax.optimization_barrier(jnp.sum(expo, axis=-1, keepdims=True))
        mixed = jnp.einsum('hqk,khd->qhd', low(probs), heads_value, precision=lax.Precision.HIGHEST)
        return mixed.reshape(block, D)
    starts = (jnp.arange(count, dtype=jnp.int32) * block).astype(jnp.int32)
    return lax.map(jax.checkpoint(one_block), starts).reshape(LENGTH, D)

def forward(x, params, segs):
    mix, merge, expand, shrink, gain_one, bias_one, q_bias, v_bias, m_bias, gain_two, bias_two, e_bias, s_bias = params
    first = low(layer_norm(x, gain_one, bias_one))
    mixed = jnp.dot(first, mix, precision=lax.Precision.HIGHEST)
    query = low_back(low(mixed[:, :D] + q_bias))
    key = low_back(low(mixed[:, D:2 * D]))
    value = low_back(low(mixed[:, 2 * D:] + v_bias))
    attended = low_back(low(attend(query, key, value, segs)))
    hidden = x + low_back(jnp.dot(attended, merge, precision=lax.Precision.HIGHEST) + m_bias)
    second = low(layer_norm(hidden, gain_two, bias_two))
    pre = low_back(jnp.dot(second, expand, precision=lax.Precision.HIGHEST) + e_bias)
    act = low(gelu_tanh(pre))
    return hidden + jnp.dot(act, shrink, precision=lax.Precision.HIGHEST) + s_bias

def reference(inputs, segments, cotangent, mix_weight, merge_weight, expand_weight, shrink_weight, first_gain, first_bias, query_bias, value_bias, merge_bias, second_gain, second_bias, expand_bias, shrink_bias):
    params = tuple((p.astype(jnp.float32) for p in (mix_weight, merge_weight, expand_weight, shrink_weight, first_gain, first_bias, query_bias, value_bias, merge_bias, second_gain, second_bias, expand_bias, shrink_bias)))
    zeros = tuple((jnp.zeros(p.shape, jnp.float32) for p in params))

    def step(totals, row):
        x_row, seg_row, cot_row = row

        def local(xx, *ps):
            return forward(xx, ps, seg_row)
        result, pull = jax.vjp(local, x_row.astype(jnp.float32), *params)
        grads = pull(cot_row.astype(jnp.float32))
        totals = tuple((a + b for a, b in zip(totals, grads[1:])))
        return (totals, (result.astype(jnp.bfloat16), grads[0]))
    totals, (outputs, input_grad) = lax.scan(step, zeros, (inputs, segments, cotangent))
    return (outputs, input_grad, totals[0], totals[1], totals[2], totals[3], totals[4], totals[5], totals[6], totals[7], totals[8], totals[9], totals[10], totals[11], totals[12])
```

```python
import functools

import jax
import jax.numpy as jnp
from jax import lax
from jax.experimental import pallas as pl
from jax.experimental.pallas import tpu as pltpu
from jax.sharding import PartitionSpec as P

HEADS = 25
LANES = 128
LOW = jnp.bfloat16
FULL = jnp.float32
VMEM_BYTES = 50 * 1024 * 1024


def layer_norm(v, gain, bias):
    center = v - jnp.mean(v, axis=-1, keepdims=True)
    spread = jnp.mean(center * center, axis=-1, keepdims=True)
    return center * lax.rsqrt(spread + 1e-05) * gain + bias


def gelu_tanh(v):
    return 0.5 * v * (1.0 + jnp.tanh(0.7978845608028654 * (v + 0.044715 * v * v * v)))


def dot_nn(left, right):
    return lax.dot_general(left, right, (((1,), (0,)), ((), ())), preferred_element_type=FULL)


def dot_tn(left, right):
    return lax.dot_general(left, right, (((0,), (0,)), ((), ())), preferred_element_type=FULL)


def dot_nt(left, right):
    return lax.dot_general(left, right, (((1,), (1,)), ((), ())), preferred_element_type=FULL)


def softmax_pieces(query, keys, seg_col, seg_row, index, block):
    scores = []
    for j in range(index + 1):
        piece = dot_nt(query, keys[j])
        seen = seg_col == seg_row[:, j * block : (j + 1) * block]
        if j == index:
            row_id = lax.broadcasted_iota(jnp.int32, (block, block), 0)
            col_id = lax.broadcasted_iota(jnp.int32, (block, block), 1)
            seen = seen & (col_id <= row_id)
        scores.append(jnp.where(seen, piece, -1e30))
    top = functools.reduce(jnp.maximum, [jnp.max(p, axis=1, keepdims=True) for p in scores])
    expo = [jnp.exp(p - top) for p in scores]
    total = functools.reduce(jnp.add, [jnp.sum(p, axis=1, keepdims=True) for p in expo])
    return expo, total


def attend_forward_kernel(count, block, dim, heads, *refs):
    q_refs, k_refs, v_refs = refs[:count], refs[count : 2 * count], refs[2 * count : 3 * count]
    col_ref, row_ref, out_ref = refs[3 * count :]
    pair = pl.program_id(0)
    out_ref[...] = jnp.zeros_like(out_ref)
    for sub in range(LANES // dim):

        @pl.when(pair * (LANES // dim) + sub < heads)
        def _():
            lanes = slice(sub * dim, (sub + 1) * dim)
            keys = [r[:, lanes] for r in k_refs]
            values = [r[:, lanes] for r in v_refs]
            for i in range(count):
                rows = slice(i * block, (i + 1) * block)
                query = q_refs[i][:, lanes]
                expo, total = softmax_pieces(
                    query, keys, col_ref[rows, :], row_ref[...], i, block
                )
                mixed = functools.reduce(
                    jnp.add, [dot_nn(e.astype(LOW), v) for e, v in zip(expo, values)]
                )
                out_ref[rows, lanes] = (mixed / total).astype(LOW)


def attend_backward_kernel(count, block, dim, heads, *refs):
    q_refs, k_refs, v_refs = refs[:count], refs[count : 2 * count], refs[2 * count : 3 * count]
    g_ref, col_ref, row_ref, dq_ref, dk_ref, dv_ref, acc_k, acc_v = refs[3 * count :]
    pair = pl.program_id(0)
    scale = dim**-0.5
    dq_ref[...] = jnp.zeros_like(dq_ref)
    dk_ref[...] = jnp.zeros_like(dk_ref)
    dv_ref[...] = jnp.zeros_like(dv_ref)
    for sub in range(LANES // dim):

        @pl.when(pair * (LANES // dim) + sub < heads)
        def _():
            lanes = slice(sub * dim, (sub + 1) * dim)
            keys = [r[:, lanes] for r in k_refs]
            values = [r[:, lanes] for r in v_refs]
            acc_k[...] = jnp.zeros_like(acc_k)
            acc_v[...] = jnp.zeros_like(acc_v)
            for i in range(count):
                rows = slice(i * block, (i + 1) * block)
                query = q_refs[i][:, lanes]
                grad = g_ref[rows, lanes]
                expo, total = softmax_pieces(
                    query, keys, col_ref[rows, :], row_ref[...], i, block
                )
                inverse = 1.0 / total
                probs = [e * inverse for e in expo]
                d_weights = [dot_nt(grad, v) for v in values[: i + 1]]
                delta = functools.reduce(
                    jnp.add,
                    [jnp.sum(p * d, axis=1, keepdims=True) for p, d in zip(probs, d_weights)],
                )
                d_query = jnp.zeros((block, dim), FULL)
                for j in range(i + 1):
                    cols = slice(j * block, (j + 1) * block)
                    d_scores = (probs[j] * (d_weights[j] - delta)).astype(LOW)
                    d_query = d_query + dot_nn(d_scores, keys[j])
                    acc_k[cols, :] += dot_tn(d_scores, query)
                    acc_v[cols, :] += dot_tn(probs[j].astype(LOW), grad)
                dq_ref[rows, lanes] = (d_query * scale).astype(LOW)
            dk_ref[:, lanes] = acc_k[...].astype(LOW)
            dv_ref[:, lanes] = acc_v[...].astype(LOW)


def attend_specs(count, block, span):
    per = span // LANES
    specs = []
    for part in range(3):
        for j in range(count):
            specs.append(
                pl.BlockSpec(
                    (block, LANES), lambda p, j=j, part=part: (j, part * per + p)
                )
            )
    return specs


def attend_forward(mixed, seg, count, dim, heads):
    length, wide = mixed.shape
    span = wide // 3
    block = length // count
    whole = lambda shape: pl.BlockSpec(shape, lambda p: (0, 0))
    return pl.pallas_call(
        functools.partial(attend_forward_kernel, count, block, dim, heads),
        grid=(span // LANES,),
        in_specs=attend_specs(count, block, span) + [whole((length, 1)), whole((1, length))],
        out_specs=pl.BlockSpec((length, LANES), lambda p: (0, p)),
        out_shape=jax.ShapeDtypeStruct((length, span), LOW),
        compiler_params=pltpu.CompilerParams(vmem_limit_bytes=VMEM_BYTES),
        cost_estimate=pl.CostEstimate(
            flops=2 * length * length * dim * heads * 2,
            bytes_accessed=4 * length * span * 2,
            transcendentals=length * length * heads // 2,
        ),
        name="attend_forward",
    )(*([mixed] * (3 * count)), seg.reshape(length, 1), seg.reshape(1, length))


def attend_backward(mixed, grad, seg, count, dim, heads):
    length, wide = mixed.shape
    span = wide // 3
    block = length // count
    whole = lambda shape: pl.BlockSpec(shape, lambda p: (0, 0))
    column = pl.BlockSpec((length, LANES), lambda p: (0, p))
    shape = jax.ShapeDtypeStruct((length, span), LOW)
    return pl.pallas_call(
        functools.partial(attend_backward_kernel, count, block, dim, heads),
        grid=(span // LANES,),
        in_specs=attend_specs(count, block, span)
        + [column, whole((length, 1)), whole((1, length))],
        out_specs=[column, column, column],
        out_shape=[shape, shape, shape],
        scratch_shapes=[pltpu.VMEM((length, dim), FULL), pltpu.VMEM((length, dim), FULL)],
        compiler_params=pltpu.CompilerParams(vmem_limit_bytes=VMEM_BYTES),
        cost_estimate=pl.CostEstimate(
            flops=5 * length * length * dim * heads * 2,
            bytes_accessed=8 * length * span * 2,
            transcendentals=length * length * heads // 2,
        ),
        name="attend_backward",
    )(*([mixed] * (3 * count)), grad, seg.reshape(length, 1), seg.reshape(1, length))


def body(
    seq_n,
    dp_n,
    inputs,
    segments,
    cotangent,
    mix_weight,
    merge_weight,
    expand_weight,
    shrink_weight,
    first_gain,
    first_bias,
    query_bias,
    value_bias,
    merge_bias,
    second_gain,
    second_bias,
    expand_bias,
    shrink_bias,
):
    micro, rows, width = inputs.shape
    length = segments.shape[1]
    dim = width // HEADS
    teams = seq_n // 2
    bits = teams.bit_length() - 1
    own_rows = 2 * rows
    feats = width // seq_n
    share = width // teams
    starts_exact = [share * t // dim for t in range(teams)]
    heads = max(-(-share * (t + 1) // dim) - starts_exact[t] for t in range(teams))
    starts = [dim * min(h, HEADS - heads) for h in starts_exact]
    window = heads * dim
    span = -(-window // LANES) * LANES
    hidden_units = expand_weight.shape[1] * dp_n
    per_team = hidden_units // dp_n // teams
    half_team = per_team // 2

    place = lax.axis_index("seq")
    core = place % 2
    team = place // 2

    def hop(v, mask):
        return lax.ppermute(v, "seq", [(i, i ^ mask) for i in range(seq_n)])

    def pick(v, index):
        return lax.dynamic_index_in_dim(v, index, 0, keepdims=False)

    def reorder(v):
        return jnp.stack([pick(v, team ^ j) for j in range(teams)])

    def by_core(mine, other):
        return jnp.where(core == 0, jnp.stack([mine, other]), jnp.stack([other, mine]))

    def part_rows(total):
        edges = [total * p // bits for p in range(bits + 1)]
        return list(zip(edges[:-1], edges[1:]))

    def gather_team(v):
        done = []
        for p, (low, high) in enumerate(part_rows(v.shape[0])):
            cur = v[low:high][None]
            order = [(p + i) % bits for i in range(bits)]
            for b in order:
                cur = jnp.concatenate([cur, hop(cur, 2 << b)], axis=0)
            cur = cur.reshape((2,) * bits + cur.shape[1:])
            axes = [bits - 1 - order.index(bits - 1 - a) for a in range(bits)]
            cur = cur.transpose(axes + list(range(bits, cur.ndim)))
            done.append(cur.reshape((teams,) + cur.shape[bits:]))
        return jnp.concatenate(done, axis=1)

    def reduce_team(v):
        done = []
        for p, (low, high) in enumerate(part_rows(v.shape[1])):
            cur = v[:, low:high]
            cur = cur.reshape((2,) * bits + cur.shape[1:])
            left = list(range(bits - 1, -1, -1))
            order = [(p + i) % bits for i in range(bits)]
            for b in reversed(order):
                axis = left.index(b)
                keep = lax.index_in_dim(cur, 0, axis, keepdims=False)
                give = lax.index_in_dim(cur, 1, axis, keepdims=False)
                left.remove(b)
                cur = keep.astype(FULL) + hop(give, 2 << b).astype(FULL)
                if left:
                    cur = cur.astype(LOW)
            done.append(cur)
        return jnp.concatenate(done, axis=0)

    def exchange_team(v):
        return jnp.stack([v[0]] + [hop(v[k], 2 * k) for k in range(1, teams)])

    def swap_in(v):
        got = hop(pick(v, 1 - core), 1)
        return by_core(pick(v, core), got).reshape(own_rows, width)

    def swap_out(v):
        v = v.reshape(2, rows, width)
        got = hop(pick(v, 1 - core), 1)
        return by_core(pick(v, core), got)

    def gather_small(v):
        cur = v[None]
        for b in range(bits + 1):
            got = hop(cur, 1 << b)
            bit = (place >> b) & 1
            cur = jnp.where(
                bit == 0, jnp.concatenate([cur, got]), jnp.concatenate([got, cur])
            )
        return cur

    def reduce_small(v):
        for b in reversed(range(bits + 1)):
            half = v.shape[0] // 2
            bit = (place >> b) & 1
            mine = jnp.where(bit == 0, v[:half], v[half:])
            give = jnp.where(bit == 0, v[half:], v[:half])
            v = mine + hop(give, 1 << b)
        v = v[0]
        for b in range(dp_n.bit_length() - 1):
            v = v + lax.ppermute(v, "dp", [(i, i ^ (1 << b)) for i in range(dp_n)])
        return v

    small = (
        first_gain,
        first_bias,
        query_bias,
        value_bias,
        merge_bias,
        second_gain,
        second_bias,
        expand_bias,
        shrink_bias,
    )
    sizes = [v.shape[0] for v in small]
    offsets = [sum(sizes[:i]) for i in range(len(sizes) + 1)]

    x_own_low = swap_in(inputs)
    x_own = x_own_low.astype(FULL)
    packed = gather_small(jnp.concatenate(small))
    gain_one, bias_one, q_bias, v_bias, m_bias, gain_two, bias_two, e_bias, s_bias = [
        packed[:, offsets[i] : offsets[i + 1]].reshape(-1).astype(FULL) for i in range(9)
    ]
    start = jnp.asarray(starts, jnp.int32)[team]

    mix_rows = lax.all_gather(mix_weight, "dp", axis=0)
    mix_rows = mix_rows.transpose(1, 0, 2).reshape(feats, 3, width)
    mix_cuts = jnp.stack(
        [mix_rows[:, :, s : s + window].reshape(feats, 3 * window) for s in starts]
    )
    mix_got = exchange_team(reorder(mix_cuts))
    mix_other = hop(mix_got, 1)
    mix_mine = reorder(mix_got)
    mix_other = reorder(mix_other)
    mix = by_core(mix_mine, mix_other).transpose(1, 0, 2, 3)
    mix = mix.reshape(width, 3, window)
    mix = jnp.pad(mix, ((0, 0), (0, 0), (0, span - window))).reshape(width, 3 * span)

    merge_rows = lax.all_gather(merge_weight, "dp", axis=0)
    merge_rows = merge_rows.transpose(1, 0, 2).reshape(feats, width)
    merge_got = gather_team(merge_rows)
    merge_other = reorder(hop(merge_got, 1))
    merge = by_core(reorder(merge_got), merge_other).transpose(1, 0, 2, 3)
    merge = merge.reshape(width, width)

    cut = expand_weight.reshape(feats, teams, 2, half_team).transpose(2, 1, 3, 0)
    cut = by_core(pick(cut, core), hop(pick(cut, 1 - core), 1))
    cut = cut.transpose(1, 2, 0, 3).reshape(teams, half_team, 2 * feats)
    cut = reorder(exchange_team(reorder(cut))).transpose(1, 0, 2).reshape(half_team, width)
    expand_mine = lax.all_gather(cut, "dp", axis=0, tiled=True)
    expand_other = hop(expand_mine, 1)

    cut = shrink_weight.reshape(teams // 2, 2, half_team, -1).transpose(1, 0, 2, 3)
    cut = by_core(pick(cut, core), hop(pick(cut, 1 - core), 1))
    cut = cut.reshape((teams, half_team) + cut.shape[3:])
    cut = reorder(exchange_team(reorder(cut))).transpose(2, 0, 1).reshape(-1, teams * half_team)
    shrink_mine = lax.all_gather(cut, "dp", axis=0, tiled=True)
    shrink_other = hop(shrink_mine, 1)

    x_all = reorder(gather_team(x_own_low)).reshape(length, width)
    first = layer_norm(x_all.astype(FULL), gain_one, bias_one).astype(LOW)

    def windowed(v):
        return jnp.pad(lax.dynamic_slice_in_dim(v, start, window, 0), (0, span - window))

    mix_bias = jnp.concatenate([windowed(q_bias), jnp.zeros((span,), FULL), windowed(v_bias)])
    mixed = (dot_nn(first, mix) + mix_bias).astype(LOW)
    shrinking = jnp.where(jnp.arange(3 * span) < span, dim**-0.5, 1.0).astype(LOW)
    mixed = mixed * shrinking
    seg = pick(segments, core)
    attended_win = attend_forward(mixed, seg, teams, dim, heads)
    pieces = reorder(exchange_team(reorder(attended_win.reshape(teams, own_rows, span))))
    attended = jnp.concatenate(
        [
            pieces[t][:, share * t - starts[t] : share * (t + 1) - starts[t]]
            for t in range(teams)
        ],
        axis=1,
    )
    hidden = x_own + dot_nn(attended, merge) + m_bias
    second_own, second_pull = jax.vjp(layer_norm, hidden, gain_two, bias_two)
    second = gather_team(second_own.astype(LOW)).reshape(length, width)

    g_own_low = swap_in(cotangent)
    g_own = g_own_low.astype(FULL)
    g_all = gather_team(g_own_low).reshape(length, width)

    e_cut = e_bias.reshape(dp_n, teams, 2, half_team).transpose(1, 2, 0, 3)
    e_cut = pick(e_cut, team).reshape(2, dp_n * half_team)
    e_mine, e_other = pick(e_cut, core), pick(e_cut, 1 - core)

    def feed(expand_t, shrink_t, bias):
        pre = dot_nt(second, expand_t) + bias
        act, pull = jax.vjp(gelu_tanh, pre)
        act = act.astype(LOW)
        d_act = dot_nn(g_all, shrink_t)
        d_pre = pull(d_act)[0].astype(LOW)
        return act, d_pre

    act_mine, d_pre_mine = feed(expand_mine, shrink_mine, e_mine)
    act_other, d_pre_other = feed(expand_other, shrink_other, e_other)
    d_second = dot_nn(d_pre_mine, expand_mine) + dot_nn(d_pre_other, expand_other)
    d_second = reduce_team(d_second.astype(LOW).reshape(teams, own_rows, width))
    out = dot_nt(act_mine, shrink_mine) + dot_nt(act_other, shrink_other)
    out = reduce_team(out.astype(LOW).reshape(teams, own_rows, width))
    block_out = swap_out((hidden + out + s_bias).astype(LOW))

    def core_sum(mine, other):
        return (mine + hop(other.astype(LOW), 1).astype(FULL)).astype(LOW)

    g_shrink = core_sum(dot_tn(g_all, act_mine), dot_tn(g_all, act_other))
    g_shrink = lax.psum_scatter(g_shrink, "dp", scatter_dimension=0, tiled=True)
    g_expand = core_sum(dot_tn(d_pre_mine, second), dot_tn(d_pre_other, second))
    g_expand = lax.psum_scatter(g_expand, "dp", scatter_dimension=0, tiled=True)

    cut = g_shrink.reshape(-1, teams, half_team).transpose(1, 2, 0)
    cut = reorder(exchange_team(reorder(cut)))
    cut = cut.reshape((2, teams // 2) + cut.shape[1:])
    cut = by_core(pick(cut, core), hop(pick(cut, 1 - core), 1))
    grad_shrink = cut.transpose(1, 0, 2, 3).reshape(shrink_weight.shape).astype(FULL)

    cut = g_expand.reshape(half_team, teams, 2 * feats).transpose(1, 0, 2)
    cut = reorder(exchange_team(reorder(cut)))
    cut = cut.reshape(teams, half_team, 2, feats).transpose(2, 3, 0, 1)
    cut = by_core(pick(cut, core), hop(pick(cut, 1 - core), 1))
    grad_expand = cut.transpose(1, 2, 0, 3).reshape(expand_weight.shape).astype(FULL)

    d_norm_two, d_gain_two, d_bias_two = second_pull(d_second)
    d_hidden = g_own + d_norm_two
    d_branch = d_hidden.astype(LOW)
    d_attended = dot_nt(d_branch, merge).astype(LOW)
    pieces = jnp.stack(
        [
            jnp.pad(d_attended[:, s : s + window], ((0, 0), (0, span - window)))
            for s in starts
        ]
    )
    d_attended_win = reorder(exchange_team(reorder(pieces))).reshape(length, span)
    d_parts = attend_backward(mixed, d_attended_win, seg, teams, dim, heads)

    column = jnp.arange(span, dtype=jnp.int32) + start
    owned = (column >= share * team) & (column < share * (team + 1))
    d_parts = [jnp.where(owned, d, jnp.zeros((), LOW)) for d in d_parts]
    d_first = functools.reduce(
        jnp.add,
        [dot_nt(d_parts[m], mix[:, m * span : (m + 1) * span]) for m in range(3)],
    )
    d_first = reduce_team(reorder(d_first.astype(LOW).reshape(teams, own_rows, width)))

    def core_halves(v):
        v = v.reshape((teams, 2, feats) + v.shape[1:]).transpose((1, 0, 2, 3))
        return core_sum(pick(v, core), pick(v, 1 - core))

    g_merge = core_halves(dot_tn(attended, d_branch))
    g_merge = g_merge.reshape(teams, feats, dp_n, -1).transpose(2, 0, 1, 3)
    g_merge = lax.psum_scatter(g_merge, "dp", scatter_dimension=0, tiled=True)[0]
    grad_merge = reduce_team(reorder(g_merge))

    g_mix = jnp.concatenate([dot_tn(first, d)[:, :window] for d in d_parts], axis=1)
    g_mix = reorder(exchange_team(reorder(core_halves(g_mix))))
    g_mix = g_mix.reshape(teams, feats, 3, window)
    g_mix = jnp.concatenate(
        [
            g_mix[t, :, :, share * t - starts[t] : share * (t + 1) - starts[t]]
            for t in range(teams)
        ],
        axis=-1,
    )
    g_mix = g_mix.reshape(feats, dp_n, -1).transpose(1, 0, 2)
    grad_mix = lax.psum_scatter(g_mix, "dp", scatter_dimension=0, tiled=True)[0].astype(FULL)

    x_again, first_pull = jax.vjp(layer_norm, x_own, gain_one, bias_one)
    d_norm_one, d_gain_one, d_bias_one = first_pull(d_first)
    input_grad = swap_out(d_hidden + d_norm_one)

    def spread(v):
        return lax.dynamic_update_slice_in_dim(
            jnp.zeros((width + span,), FULL), v, start, 0
        )[:width]

    d_e = jnp.stack([jnp.sum(d.astype(FULL), axis=0) for d in (d_pre_mine, d_pre_other)])
    d_e = jnp.where(core == 0, d_e, d_e[::-1]).reshape(2, dp_n, half_team).transpose(1, 0, 2)
    d_e = lax.dynamic_update_slice_in_dim(
        jnp.zeros((dp_n, teams, 2, half_team), FULL), d_e[:, None], team, 1
    )
    partial = (
        d_gain_one,
        d_bias_one,
        spread(jnp.sum(d_parts[0].astype(FULL), axis=0)),
        spread(jnp.sum(d_parts[2].astype(FULL), axis=0)),
        jnp.sum(d_branch.astype(FULL), axis=0),
        d_gain_two,
        d_bias_two,
        d_e.reshape(-1),
        jnp.sum(g_own, axis=0),
    )
    total = reduce_small(
        jnp.concatenate([v.reshape(seq_n, -1) for v in partial], axis=1)
    )
    vectors = [total[offsets[i] : offsets[i + 1]] for i in range(9)]
    return (block_out, input_grad, grad_mix, grad_merge, grad_expand, grad_shrink, *vectors)


def solution(mesh):
    rows = P("dp", "seq", None)
    matrix = P("seq", "dp")
    vector = P("seq")
    return jax.shard_map(
        functools.partial(body, mesh.shape["seq"], mesh.shape["dp"]),
        mesh=mesh,
        in_specs=(rows, P("dp", None), rows) + (matrix,) * 4 + (vector,) * 9,
        out_specs=(rows, rows) + (matrix,) * 4 + (vector,) * 9,
        check_vma=False,
    )
```

```python
import functools

import jax
import jax.numpy as jnp
from jax import lax
from jax.experimental import pallas as pl
from jax.experimental.pallas import tpu as pltpu
from jax.sharding import PartitionSpec as P

HEADS = 25
COST = 0.25
LANES = 128
CHUNK = 256
LOW = jnp.bfloat16
FULL = jnp.float32
VMEM_BYTES = 60 * 1024 * 1024


def dot_nn(left, right):
    return lax.dot_general(left, right, (((1,), (0,)), ((), ())), preferred_element_type=FULL)


def dot_tn(left, right):
    return lax.dot_general(left, right, (((0,), (0,)), ((), ())), preferred_element_type=FULL)


def dot_nt(left, right):
    return lax.dot_general(left, right, (((1,), (1,)), ((), ())), preferred_element_type=FULL)


def norm_parts(v):
    center = v - jnp.mean(v, axis=-1, keepdims=True)
    spread = jnp.mean(center * center, axis=-1, keepdims=True)
    inverse = lax.rsqrt(spread + 1e-05)
    return center * inverse, inverse


def norm_back(grad, gain, normal, inverse):
    e = grad * gain
    mean_e = jnp.mean(e, axis=-1, keepdims=True)
    mean_en = jnp.mean(e * normal, axis=-1, keepdims=True)
    return inverse * (e - mean_e - normal * mean_en)


def total_rows(v):
    return jnp.sum(v, axis=0, keepdims=True)


def fixed(shape):
    return pl.BlockSpec(shape, lambda *_: (0,) * len(shape), pipeline_mode=pl.Buffered(1))


def call(
    kernel, name, grid, at, operands, in_specs, outs, out_specs, scratch, flops, nbytes, exps=0, after=()
):
    if after:
        count, inner = len(operands), kernel
        kernel = lambda at_ref, *refs: inner(at_ref, *refs[:count], *refs[count + len(after) :])
        operands = (*operands, *after)
        in_specs = list(in_specs) + [pl.BlockSpec(memory_space=pl.ANY)] * len(after)
    spec = pltpu.PrefetchScalarGridSpec(
        num_scalar_prefetch=1,
        grid=grid,
        in_specs=in_specs,
        out_specs=out_specs,
        scratch_shapes=scratch,
    )
    return pl.pallas_call(
        kernel,
        grid_spec=spec,
        out_shape=[jax.ShapeDtypeStruct(s, d) for s, d in outs],
        compiler_params=pltpu.CompilerParams(vmem_limit_bytes=VMEM_BYTES),
        cost_estimate=pl.CostEstimate(
            flops=int(COST * flops),
            bytes_accessed=int(COST * nbytes),
            transcendentals=int(COST * exps),
        ),
        name=name,
    )(at, *operands)


def row_slot(half, core, rows):
    slot = core if half == 0 else 1 - core
    return pl.ds(pl.multiple_of(slot * rows, rows), rows)


def load_pair(step, sizes, refs, buf, core, rows):
    low = 0
    for size, ref in zip(sizes, refs):
        for i in range(size // rows):
            r = low // rows + i

            @pl.when(step == r // 2)
            def _():
                buf[row_slot(r % 2, core, rows), :] = ref[i * rows : (i + 1) * rows, :]

        low += size


def pair_rows(refs, core, rows, buf):
    for half in range(2):
        here = slice(half * rows, (half + 1) * rows)
        value = functools.reduce(jnp.add, [ref[here, :].astype(FULL) for ref in refs])
        buf[row_slot(half, core, rows), :] = value.astype(buf.dtype)


def fold_kernel(at_ref, x_ref, y_ref, far0_ref, far1_ref, xo_ref, yo_ref):
    rows = far0_ref.shape[0]
    xo_ref[:rows, :] = x_ref[:rows, :]
    xo_ref[rows:, :] = (x_ref[rows:, :].astype(FULL) + far1_ref[...].astype(FULL)).astype(LOW)
    yo_ref[:rows, :] = (y_ref[:rows, :].astype(FULL) + far0_ref[...].astype(FULL)).astype(LOW)
    yo_ref[rows:, :] = y_ref[rows:, :]


def place_rows(place, refs, wide, out):
    each = refs[0].shape[0]
    if len(refs) == 1:
        out[...] = refs[0][...]
        return
    for r, ref in enumerate(refs):
        begin = pl.multiple_of((place ^ r) * each, each)
        wide[pl.ds(begin, each), :] = ref[...].astype(FULL)
    filled = each * len(refs)
    if filled < wide.shape[0]:
        wide[filled:, :] = jnp.zeros((wide.shape[0] - filled, wide.shape[1]), FULL)
    block = 16
    for size in range(16, 129, 16):
        block = size if out.shape[0] % size == 0 else block

    def narrow(i, carry):
        span = pl.ds(pl.multiple_of(i * block, block), block)
        out[span, :] = wide[span, :].astype(LOW)
        return carry

    lax.fori_loop(0, out.shape[0] // block, narrow, 0)


def flip(v):
    rows, cols = v.shape
    v = jnp.pad(v.astype(FULL), ((0, -rows % LANES), (0, -cols % LANES)))
    return v.T[:cols, :rows]


def cut_feed_kernel(at_ref, e_ref, s_ref, ek_ref, eg_ref, sk_ref, sg_ref, *, teams, hr):
    first = at_ref[0] % 2 == 0
    cols = s_ref.shape[1]
    e, s = e_ref[...].astype(FULL), s_ref[...].astype(FULL)
    for t in range(teams):
        a, b = e[:, 2 * t * hr : (2 * t + 1) * hr], e[:, (2 * t + 1) * hr : (2 * t + 2) * hr]
        ek_ref[:, t * hr : (t + 1) * hr] = jnp.where(first, a, b).astype(LOW)
        eg_ref[:, t * hr : (t + 1) * hr] = jnp.where(first, b, a).astype(LOW)
    for t in range(teams // 2):
        a, b = s[2 * t * hr : (2 * t + 1) * hr], s[(2 * t + 1) * hr : (2 * t + 2) * hr]
        sk_ref[:, t * cols : (t + 1) * cols] = jnp.where(first, a, b).astype(LOW)
        sg_ref[:, t * cols : (t + 1) * cols] = jnp.where(first, b, a).astype(LOW)


def join_feed_kernel(at_ref, ek_ref, eo_ref, sk_ref, so_ref, *out_refs, teams, hr):
    first, team = at_ref[0] % 2 == 0, at_ref[0] // 2
    feats = ek_ref.shape[0]
    cols = 2 * feats
    mine, other = flip(ek_ref[...]), flip(eo_ref[...])
    low = jnp.where(first, mine, other).astype(LOW)
    high = jnp.where(first, other, mine).astype(LOW)
    for t in range(teams):
        part = slice((t % (teams // 2)) * cols, (t % (teams // 2) + 1) * cols)
        here = first if t < teams // 2 else jnp.logical_not(first)
        piece = jnp.where(here, sk_ref[:, part], so_ref[:, part])
        for k, ref in enumerate(out_refs):

            @pl.when((team ^ t) == k)
            def _():
                ref[0, :, :feats] = low[t * hr : (t + 1) * hr, :]
                ref[0, :, feats:] = high[t * hr : (t + 1) * hr, :]
                ref[1] = piece


def lay_feed_kernel(at_ref, *refs, teams, hp):
    part_refs, e_ref, s_ref, whole = refs[:teams], *refs[teams:]
    team = at_ref[0] // 2
    for k, ref in enumerate(part_refs):
        whole[team ^ k] = ref[...]
    hr, cols = whole.shape[2:]
    e_ref[hr:, :] = jnp.zeros((hp - hr, e_ref.shape[1]), LOW)
    s_ref[...] = jnp.zeros_like(s_ref)
    for t in range(teams):
        e_ref[:hr, t * cols : (t + 1) * cols] = whole[t, 0]
        s_ref[:, t * hp : t * hp + hr] = flip(whole[t, 1]).astype(LOW)


def split_feed_kernel(at_ref, e_ref, s_ref, *out_refs, teams, hp):
    team = at_ref[0] // 2
    hr, cols = out_refs[0].shape[1:]
    for t in range(teams):
        piece = flip(s_ref[:, t * hp : t * hp + hr]).astype(LOW)
        for k, ref in enumerate(out_refs):

            @pl.when((team ^ t) == k)
            def _():
                ref[0] = e_ref[:hr, t * cols : (t + 1) * cols]
                ref[1] = piece


def part_feed_kernel(at_ref, *refs, teams):
    part_refs, ek_ref, eg_ref, sk_ref, sg_ref, whole = refs[:teams], *refs[teams:]
    first, team = at_ref[0] % 2 == 0, at_ref[0] // 2
    for k, ref in enumerate(part_refs):
        whole[team ^ k] = ref[...]
    hr, cols = whole.shape[2:]
    feats = cols // 2
    for t in range(teams):
        e = flip(whole[t, 0])
        a, b = e[:feats, :], e[feats:, :]
        ek_ref[:, t * hr : (t + 1) * hr] = jnp.where(first, a, b).astype(LOW)
        eg_ref[:, t * hr : (t + 1) * hr] = jnp.where(first, b, a).astype(LOW)
    for t in range(teams // 2):
        a, b = whole[t, 1], whole[teams // 2 + t, 1]
        sk_ref[:, t * cols : (t + 1) * cols] = jnp.where(first, a, b)
        sg_ref[:, t * cols : (t + 1) * cols] = jnp.where(first, b, a)


def end_feed_kernel(at_ref, ek_ref, eo_ref, sk_ref, so_ref, e_ref, s_ref, *, teams, hr):
    first = at_ref[0] % 2 == 0
    cols = s_ref.shape[1]
    mine, other = ek_ref[...].astype(FULL), eo_ref[...].astype(FULL)
    low, high = jnp.where(first, mine, other), jnp.where(first, other, mine)
    for t in range(teams):
        e_ref[:, 2 * t * hr : (2 * t + 1) * hr] = low[:, t * hr : (t + 1) * hr]
        e_ref[:, (2 * t + 1) * hr : (2 * t + 2) * hr] = high[:, t * hr : (t + 1) * hr]
    mine, other = sk_ref[...].astype(FULL), so_ref[...].astype(FULL)
    low, high = jnp.where(first, mine, other), jnp.where(first, other, mine)
    for t in range(teams // 2):
        s_ref[2 * t * hr : (2 * t + 1) * hr, :] = low[:, t * cols : (t + 1) * cols]
        s_ref[(2 * t + 1) * hr : (2 * t + 2) * hr, :] = high[:, t * cols : (t + 1) * cols]


def cut_mix_kernel(at_ref, rows_ref, *refs, teams, dp_n, each, span, starts, width):
    out_refs, merge_ref, full = refs[:teams], refs[teams], refs[teams + 1]
    team = at_ref[0] // 2
    part = width // dp_n
    for d in range(dp_n):
        full[:, d * each : (d + 1) * each] = rows_ref[d, :, :each]
        merge_ref[:, d * part : (d + 1) * part] = rows_ref[d, :, each:]
    full[:, dp_n * each :] = jnp.zeros((full.shape[0], full.shape[1] - dp_n * each), LOW)
    for t in range(teams):
        for k, ref in enumerate(out_refs):

            @pl.when((team ^ t) == k)
            def _():
                for m in range(3):
                    begin = m * width + starts[t]
                    ref[:, m * span : (m + 1) * span] = full[:, begin : begin + span]


def join_mix_kernel(at_ref, *refs, teams, dp_n, each, span, starts, width):
    part_refs, out_ref, whole, flat = refs[: 2 * teams], *refs[2 * teams :]
    team = at_ref[0] // 2
    share, half = width // teams, span // 2
    for i, ref in enumerate(part_refs):
        for m in range(3):
            low = m * span + (i // teams) * half
            whole[team ^ (i % teams), :, low : low + half] = ref[:, m * half : (m + 1) * half]
    for m in range(3):
        for t in range(teams):
            low = m * span + share * t - starts[t]
            begin = m * width + share * t
            flat[:, begin : begin + share] = whole[t, :, low : low + share]
    for d in range(dp_n):
        out_ref[d] = flat[:, d * each : (d + 1) * each]


def norm_kernel(sizes, rows, at_ref, *refs):
    count = len(sizes)
    vec_ref, first_ref, buf = refs[count:]
    load_pair(pl.program_id(0), sizes, refs[:count], buf, at_ref[0] % 2, rows)
    normal, _ = norm_parts(buf[...].astype(FULL))
    first_ref[...] = (normal * vec_ref[0:1, :] + vec_ref[1:2, :]).astype(LOW)


def mix_kernel(parts, at_ref, *refs):
    first_ref, bias_ref, mixed_ref, mix_ref, wide = refs[parts:]

    @pl.when(pl.program_id(0) == 0)
    def _():
        place_rows(at_ref[0], refs[:parts], wide, mix_ref)

    mixed = dot_nn(first_ref[...], mix_ref[...]) + bias_ref[0:1, :]
    mixed_ref[...] = (mixed * bias_ref[1:2, :]).astype(LOW)


def softmax_pieces(query, keys, seg_col, seg_row, index, block):
    scores = []
    for j in range(index + 1):
        piece = dot_nt(query, keys[j])
        seen = seg_col == seg_row[:, j * block : (j + 1) * block]
        if j == index:
            row_id = lax.broadcasted_iota(jnp.int32, (block, block), 0)
            col_id = lax.broadcasted_iota(jnp.int32, (block, block), 1)
            seen = seen & (col_id <= row_id)
        scores.append(jnp.where(seen, piece, -1e30))
    top = functools.reduce(jnp.maximum, [jnp.max(p, axis=1, keepdims=True) for p in scores])
    expo = [jnp.exp(p - top) for p in scores]
    total = functools.reduce(jnp.add, [jnp.sum(p, axis=1, keepdims=True) for p in expo])
    return expo, total


def attend_forward_kernel(count, block, dim, heads, base, at_ref, *refs):
    q_refs, k_refs, v_refs = refs[:count], refs[count : 2 * count], refs[2 * count : 3 * count]
    col_ref, row_ref = refs[3 * count : 3 * count + 2]
    out_refs = refs[3 * count + 2 :]
    pair = pl.program_id(0) + base
    team = at_ref[0] // 2
    for ref in out_refs:
        ref[...] = jnp.zeros_like(ref)
    for sub in range(LANES // dim):

        @pl.when(pair * (LANES // dim) + sub < heads)
        def _():
            lanes = slice(sub * dim, (sub + 1) * dim)
            keys = [r[:, lanes] for r in k_refs]
            values = [r[:, lanes] for r in v_refs]
            for i in range(count):
                rows = slice(i * block, (i + 1) * block)
                query = q_refs[i][:, lanes]
                expo, total = softmax_pieces(
                    query, keys, col_ref[rows, :], row_ref[...], i, block
                )
                mixed = functools.reduce(
                    jnp.add, [dot_nn(e.astype(LOW), v) for e, v in zip(expo, values)]
                )
                mixed = (mixed / total).astype(LOW)
                for k, ref in enumerate(out_refs):

                    @pl.when((team ^ i) == k)
                    def _():
                        ref[:, lanes] = mixed


def attend_backward_kernel(count, block, dim, heads, share, base, at_ref, *refs):
    q_refs, k_refs, v_refs = refs[:count], refs[count : 2 * count], refs[2 * count : 3 * count]
    g_refs = refs[3 * count : 4 * count]
    col_ref, row_ref, d_ref, acc_k, acc_v, grads = refs[4 * count :]
    pair = pl.program_id(0) + base
    team = at_ref[0] // 2
    scale = dim**-0.5
    d_ref[...] = jnp.zeros_like(d_ref)
    for k, ref in enumerate(g_refs):
        grads[pl.ds(pl.multiple_of((team ^ k) * block, block), block), :] = ref[...]
    for sub in range(LANES // dim):

        @pl.when(pair * (LANES // dim) + sub < heads)
        def _():
            lanes = slice(sub * dim, (sub + 1) * dim)
            column = lax.broadcasted_iota(jnp.int32, (1, dim), 1)
            column = column + at_ref[1 + team] + pair * LANES + sub * dim
            owned = (column >= share * team) & (column < share * (team + 1))
            owned = jnp.where(owned, 1.0, 0.0)
            keys = [r[:, lanes] for r in k_refs]
            values = [r[:, lanes] for r in v_refs]
            acc_k[...] = jnp.zeros_like(acc_k)
            acc_v[...] = jnp.zeros_like(acc_v)
            for i in range(count):
                rows = slice(i * block, (i + 1) * block)
                query = q_refs[i][:, lanes]
                grad = grads[rows, lanes]
                expo, total = softmax_pieces(
                    query, keys, col_ref[rows, :], row_ref[...], i, block
                )
                inverse = 1.0 / total
                probs = [e * inverse for e in expo]
                d_weights = [dot_nt(grad, v) for v in values[: i + 1]]
                delta = functools.reduce(
                    jnp.add,
                    [jnp.sum(p * d, axis=1, keepdims=True) for p, d in zip(probs, d_weights)],
                )
                d_query = jnp.zeros((block, dim), FULL)
                for j in range(i + 1):
                    cols = slice(j * block, (j + 1) * block)
                    d_scores = (probs[j] * (d_weights[j] - delta)).astype(LOW)
                    d_query = d_query + dot_nn(d_scores, keys[j])
                    acc_k[cols, :] += dot_tn(d_scores, query)
                    acc_v[cols, :] += dot_tn(probs[j].astype(LOW), grad)
                d_ref[0, rows, lanes] = (d_query * scale * owned).astype(LOW)
            d_ref[1, :, lanes] = (acc_k[...] * owned).astype(LOW)
            d_ref[2, :, lanes] = (acc_v[...] * owned).astype(LOW)


def merge_norm_kernel(at_ref, *refs, count, rows, span, share, dim, parts):
    att_refs, part_refs = refs[: 2 * count], refs[2 * count : 2 * count + parts]
    x_ref, vec_ref, hid_ref, s_ref, merge_ref, xs, buf, wide = refs[2 * count + parts :]
    core, team = at_ref[0] % 2, at_ref[0] // 2
    place_rows(at_ref[0], part_refs, wide, merge_ref)
    pair_rows([x_ref], core, rows, xs)
    hidden = xs[...].astype(FULL) + vec_ref[4:5, :]
    lane = lax.broadcasted_iota(jnp.int32, (1, span), 1)
    for k in range(count):
        other = team ^ k
        start = at_ref[1 + other]
        low = share * other - start
        owned = (lane >= low) & (lane < low + share)
        piece = jnp.concatenate([att_refs[k][...], att_refs[count + k][...]], axis=1)
        piece = jnp.where(owned, piece, jnp.zeros((), LOW))
        hidden = hidden + dot_nn(piece, merge_ref[pl.ds(pl.multiple_of(start, dim), span), :])
    hid_ref[...] = hidden
    normal, _ = norm_parts(hidden)
    buf[...] = (normal * vec_ref[5:6, :] + vec_ref[6:7, :]).astype(LOW)
    s_ref[:rows, :] = buf[row_slot(0, core, rows), :]
    s_ref[rows:, :] = buf[row_slot(1, core, rows), :]


def feed_kernel(sizes, at_ref, *refs):
    pieces = len(sizes)
    lows = [sum(sizes[:i]) for i in range(pieces)]
    sec_refs, g_refs = refs[:pieces], refs[pieces : 2 * pieces]
    weights, (bias_ref, act_ref, dpre_ref, sum_ref) = (
        refs[2 * pieces : 2 * pieces + 4],
        refs[2 * pieces + 4 : 2 * pieces + 8],
    )
    rest = refs[2 * pieces + 8 :]
    ds_refs, out_refs = rest[:pieces], rest[pieces : 2 * pieces]
    sec, g, acc_s, acc_o, e_held, s_held, sems = rest[2 * pieces :]
    step = pl.program_id(0)
    copies = [
        pltpu.make_async_copy(ref, held.at[i // 2], sems.at[i])
        for i, (ref, held) in enumerate(zip(weights, (e_held, s_held) * 2))
    ]

    @pl.when(step == 0)
    def _():
        for copy in copies:
            copy.start()
        for i in range(pieces):
            sec[lows[i] : lows[i] + sizes[i], :] = sec_refs[i][...]
            g[lows[i] : lows[i] + sizes[i], :] = g_refs[i][...]
        copies[0].wait()
        copies[1].wait()

    @pl.when(step == 1)
    def _():
        copies[2].wait()
        copies[3].wait()

    et, st = e_held[step], s_held[step]
    u = dot_nt(sec[...], et) + bias_ref[...]
    d_act = dot_nn(g[...], st)
    square = u * u
    tanh = jnp.tanh(0.7978845608028654 * u * (1.0 + 0.044715 * square))
    plus = 0.5 * (1.0 + tanh)
    act = (u * plus).astype(LOW)
    slope = plus + u * (0.5 * 0.7978845608028654) * (1.0 - tanh * tanh) * (
        1.0 + 3 * 0.044715 * square
    )
    d_pre = (d_act * slope).astype(LOW)
    act_ref[...] = act
    dpre_ref[...] = d_pre
    sum_ref[...] = jnp.broadcast_to(total_rows(d_pre.astype(FULL)), sum_ref.shape)
    part_s = dot_nn(d_pre, et)
    part_o = dot_nt(act, st)

    @pl.when(step == 0)
    def _():
        acc_s[...] = part_s
        acc_o[...] = part_o

    @pl.when(step == 1)
    def _():
        for i in range(pieces):
            here = slice(lows[i], lows[i] + sizes[i])
            ds_refs[i][...] = (acc_s[here, :] + part_s[here, :]).astype(LOW)
            out_refs[i][...] = (acc_o[here, :] + part_o[here, :]).astype(LOW)


def feed_grad_kernel(pieces, sizes, turned, at_ref, *refs):
    count = len(pieces)
    piece_refs, unit_refs = refs[:count], refs[count : count + len(sizes)]
    mine_ref, give_ref, held, units, sems = refs[count + len(sizes) :]
    step = pl.program_id(0)
    copies = [
        pltpu.make_async_copy(
            ref, held.at[sum(pieces[:i]) : sum(pieces[: i + 1]), :], sems.at[i]
        )
        for i, ref in enumerate(piece_refs)
    ]

    @pl.when(step == 0)
    def _():
        for copy in copies:
            copy.start()
        for copy in copies:
            copy.wait()

    low = 0
    for size, ref in zip(sizes, unit_refs):
        units[low : low + size, :] = ref[...]
        low += size
    if turned:
        grad = dot_tn(held[...], units[...]).astype(LOW)
    else:
        grad = dot_tn(units[...], held[...]).astype(LOW)

    @pl.when(step == 0)
    def _():
        give_ref[...] = grad

    @pl.when(step == 1)
    def _():
        mine_ref[...] = grad


def second_back_kernel(at_ref, *refs, count, rows, span, dim, terms):
    rest = refs[terms:]
    hid_ref, g_ref, merge_ref, vec_ref = rest[:4]
    dh_ref, db_ref, sum_ref = rest[4:7]
    att_refs = rest[7 : 7 + count]
    ds, g = rest[7 + count :]
    core, team = at_ref[0] % 2, at_ref[0] // 2
    pair_rows(refs[:terms], core, rows, ds)
    pair_rows([g_ref], core, rows, g)
    normal, inverse = norm_parts(hid_ref[...])
    d_second = ds[...]
    g_full = g[...].astype(FULL)
    d_hidden = g_full + norm_back(d_second, vec_ref[5:6, :], normal, inverse)
    dh_ref[...] = d_hidden
    d_branch = d_hidden.astype(LOW)
    db_ref[...] = d_branch
    sum_ref[0:1, :] = total_rows(d_second * normal)
    sum_ref[1:2, :] = total_rows(d_second)
    sum_ref[2:3, :] = total_rows(d_branch.astype(FULL))
    sum_ref[3:4, :] = total_rows(g_full)
    sum_ref[4:8, :] = jnp.zeros((4, sum_ref.shape[1]), FULL)
    for k, ref in enumerate(att_refs):
        start = pl.multiple_of(at_ref[1 + (team ^ k)], dim)
        ref[...] = dot_nt(d_branch, merge_ref[pl.ds(start, span), :]).astype(LOW)


def split_cores(core, value, mine_ref, give_ref):
    feats = mine_ref.shape[1]
    for t in range(mine_ref.shape[0]):
        low = value[2 * t * feats : (2 * t + 1) * feats, :]
        high = value[(2 * t + 1) * feats : (2 * t + 2) * feats, :]
        mine_ref[t] = jnp.where(core == 0, low, high).astype(LOW)
        give_ref[t] = jnp.where(core == 0, high, low).astype(LOW)


def merge_grad_kernel(at_ref, *refs, count, span, share, dim, step):
    att_refs = refs[: 2 * count]
    db_ref, mine_ref, give_ref, acc, held = refs[2 * count :]
    team = at_ref[0] // 2
    acc[...] = jnp.zeros_like(acc)
    lane = lax.broadcasted_iota(jnp.int32, (1, span), 1)
    for k in range(count):
        other = team ^ k
        low = share * other - at_ref[1 + other]
        owned = (lane >= low) & (lane < low + share)
        piece = jnp.concatenate([att_refs[k][...], att_refs[count + k][...]], axis=1)
        piece = jnp.where(owned, piece, jnp.zeros((), LOW))
        for c in range(span // step):
            held[k * (span // step) + c] = piece[:, c * step : (c + 1) * step]

    def add(i, carry):
        start = at_ref[1 + (team ^ (i // (span // step)))] + (i % (span // step)) * step
        acc[pl.ds(pl.multiple_of(start, dim), step), :] += dot_tn(held[i], db_ref[...])
        return carry

    lax.fori_loop(0, count * (span // step), add, 0)
    split_cores(at_ref[0] % 2, acc, mine_ref, give_ref)


def first_back_kernel(sizes, rows, span, at_ref, *refs):
    count = len(sizes)
    sides = span // LANES
    d_refs, x_refs, refs = refs[:sides], refs[sides : sides + count], refs[sides + count :]
    mix_ref, sum_ref = refs[:2]
    out_refs = refs[2 : 2 + count]
    buf, low, joined = refs[2 + count :]
    step = pl.program_id(0)
    core = at_ref[0] % 2
    load_pair(step, sizes, x_refs, buf, core, rows)
    normal, _ = norm_parts(buf[...].astype(FULL))
    for m in range(3):
        for i, d_ref in enumerate(d_refs):
            begin = m * span + i * LANES
            joined[:, begin : begin + LANES] = d_ref[m]
    d_first = dot_nt(joined[...], mix_ref[...])

    @pl.when(step == 0)
    def _():
        sum_ref[...] = jnp.zeros_like(sum_ref)

    sum_ref[0:1, :] += total_rows(d_first * normal)
    sum_ref[1:2, :] += total_rows(d_first)
    low[...] = d_first.astype(LOW)
    begin = 0
    for size, ref in zip(sizes, out_refs):
        for i in range(size // rows):
            r = begin // rows + i

            @pl.when(step == r // 2)
            def _():
                ref[i * rows : (i + 1) * rows, :] = low[row_slot(r % 2, core, rows), :]

        begin += size


def mix_grad_kernel(at_ref, *refs):
    first_ref, mine_ref, give_ref, sum_ref, first_t, held, d = refs[-7:]

    @pl.when(pl.program_id(0) == 0)
    def _():
        first_t[...] = first_ref[...].T

    for i, ref in enumerate(refs[:-7]):
        d[:, i * LANES : (i + 1) * LANES] = ref[0]
    sum_ref[...] = jnp.broadcast_to(total_rows(d[...].astype(FULL)), sum_ref.shape)
    held[...] = dot_nn(first_t[...], d[...])
    split_cores(at_ref[0] % 2, held, mine_ref, give_ref)


def block_out_kernel(at_ref, *refs, rows, terms):
    hid_ref, vec_ref, o0_ref, o1_ref = refs[terms:]
    core = at_ref[0] % 2
    for half, ref in enumerate((o0_ref, o1_ref)):
        here = slice(half * rows, (half + 1) * rows)
        value = hid_ref[row_slot(half, core, rows), :] + vec_ref[7:8, :]
        value = functools.reduce(jnp.add, [t[here, :].astype(FULL) for t in refs[:terms]], value)
        ref[...] = value.astype(LOW)


def input_grad_kernel(at_ref, *refs, rows, terms):
    dh_ref, x_ref, vec_ref, o0_ref, o1_ref = refs[terms:]
    core = at_ref[0] % 2
    for half, ref in enumerate((o0_ref, o1_ref)):
        here = slice(half * rows, (half + 1) * rows)
        d_first = functools.reduce(jnp.add, [t[here, :].astype(FULL) for t in refs[:terms]])
        normal, inverse = norm_parts(x_ref[here, :].astype(FULL))
        back = norm_back(d_first, vec_ref[0:1, :], normal, inverse)
        ref[...] = dh_ref[row_slot(half, core, rows), :] + back


def body(
    seq_n,
    dp_n,
    inputs,
    segments,
    cotangent,
    mix_weight,
    merge_weight,
    expand_weight,
    shrink_weight,
    first_gain,
    first_bias,
    query_bias,
    value_bias,
    merge_bias,
    second_gain,
    second_bias,
    expand_bias,
    shrink_bias,
):
    micro, rows, width = inputs.shape
    length = segments.shape[1]
    dim = width // HEADS
    teams = seq_n // 2
    bits = teams.bit_length() - 1
    pieces = seq_n
    own_rows = 2 * rows
    feats = width // seq_n
    share = width // teams
    begins = [share * t // dim for t in range(teams)]
    heads = max(-(-share * (t + 1) // dim) - begins[t] for t in range(teams))
    starts = [dim * min(h, HEADS - heads) for h in begins]
    span = -(-heads * dim // (2 * LANES)) * 2 * LANES
    part = span // 2
    hidden_units = expand_weight.shape[1] * dp_n
    hr = hidden_units // dp_n // teams // 2
    hp = hr
    while hp % 16 or dp_n * hp % LANES:
        hp += 1
    half = dp_n * hp
    units = 2 * half
    whole_rows = feats % 8 == 0

    place = lax.axis_index("seq")
    core = place % 2
    team = place // 2
    at = jnp.concatenate([place[None].astype(jnp.int32), jnp.asarray(starts, jnp.int32)])

    def hop(v, mask):
        shape = v.shape
        if len(shape) == 2 and shape[0] % LANES == 0 and shape[1] % LANES:
            v = v.reshape(2, shape[0] // 2, shape[1])
        return lax.ppermute(v, "seq", [(i, i ^ mask) for i in range(seq_n)]).reshape(shape)

    def pick(v, index):
        return lax.dynamic_index_in_dim(v, index, 0, keepdims=False)

    def along(v):
        return lax.all_gather(v, "dp", axis=0)

    def scatter(v):
        return lax.psum_scatter(v, "dp", scatter_dimension=0)

    def by_core(mine, other):
        return jnp.where(core == 0, jnp.stack([mine, other]), jnp.stack([other, mine]))

    def tie(v, *others):
        return lax.optimization_barrier((v, *others))[0]

    def meet(kept, moved):
        both = lax.optimization_barrier((*kept, *moved))
        return both[: len(kept)], both[len(kept) :]

    def own_pair(v, *others):
        mine = pick(v, core)
        return jnp.concatenate([mine, hop(tie(pick(v, 1 - core), *others), 1)], axis=0)

    def gather_near(own):
        if teams == 4:
            return [own, hop(own, 2), hop(own, 4)]
        return exchange([own] * teams)

    def gather_far(near, *others):
        if teams == 4:
            x, y = tie(near[1][:rows], *others), tie(near[2][rows:], *others)
            return [*near, hop(x, 4), hop(y, 2)]
        return near

    def add_low(a, b):
        return (a.astype(FULL) + b.astype(FULL)).astype(LOW)

    def reduce_far(p):
        return [hop(p[3], 2), hop(p[4], 4)] if teams == 4 else []

    def reduce_near(p, far):
        if teams == 4:
            folded = simple(
                fold_kernel, "fold", (p[1], p[2], *far), [((own_rows, width), LOW)] * 2
            )
            return [hop(folded[0], 2), hop(folded[1], 4)]
        return exchange(p)[1:]

    def exchange(parts):
        return [parts[0]] + [hop(parts[k], 2 * k) for k in range(1, teams)]

    def assemble(parts, extra=0):
        out = jnp.zeros((seq_n + extra,) + parts[0].shape, parts[0].dtype)
        for r in range(pieces):
            out = lax.dynamic_update_index_in_dim(out, parts[r], place ^ r, 0)
        return out.reshape((-1,) + parts[0].shape[1:])

    def swap_out(out0, out1):
        return by_core(out0, hop(out1, 1))

    def gather_small(v):
        cur = v[None]
        for b in range(bits + 1):
            got = hop(cur, 1 << b)
            bit = (place >> b) & 1
            cur = jnp.where(
                bit == 0, jnp.concatenate([cur, got]), jnp.concatenate([got, cur])
            )
        return cur

    def reduce_small(v):
        for b in reversed(range(bits + 1)):
            half_n = v.shape[0] // 2
            bit = (place >> b) & 1
            mine = jnp.where(bit == 0, v[:half_n], v[half_n:])
            give = jnp.where(bit == 0, v[half_n:], v[:half_n])
            v = mine + hop(give, 1 << b)
        v = v[0]
        for b in range(dp_n.bit_length() - 1):
            v = v + lax.ppermute(v, "dp", [(i, i ^ (1 << b)) for i in range(dp_n)])
        return v

    def simple(kernel, name, operands, outs, scratch=(), flops=0, nbytes=None, after=(), **named):
        if nbytes is None:
            nbytes = sum(v.size * v.dtype.itemsize for v in operands)
            nbytes += sum(4 * functools.reduce(lambda a, b: a * b, s) for s, _ in outs)
        return call(
            functools.partial(kernel, **named),
            name,
            (1,),
            at,
            operands,
            [fixed(v.shape) for v in operands],
            outs,
            [fixed(s) for s, _ in outs],
            [pltpu.VMEM(s, d) for s, d in scratch],
            flops,
            nbytes,
            after=after,
        )

    each = mix_weight.shape[1]
    mix_local = jnp.concatenate([mix_weight, merge_weight], axis=1)
    mix_rows = along(mix_local)
    small = (
        first_gain,
        first_bias,
        query_bias,
        value_bias,
        merge_bias,
        second_gain,
        second_bias,
        shrink_bias,
        expand_bias,
    )
    packed = gather_small(jnp.concatenate(small))
    vec = packed[:, : 8 * feats].reshape(seq_n, 8, feats).transpose(1, 0, 2)
    vec = vec.reshape(8, width).astype(FULL)
    e_bias = packed[:, 8 * feats :].reshape(-1).astype(FULL)
    x_own = own_pair(inputs)
    x_near = gather_near(tie(x_own, packed))

    cols = shrink_weight.shape[1]
    e_shape, s_shape = (feats, teams * hr), (hr, teams // 2 * cols)
    ek, eg, sk, sg = simple(
        cut_feed_kernel,
        "cut_feed",
        (expand_weight, shrink_weight),
        [(e_shape, LOW), (e_shape, LOW), (s_shape, LOW), (s_shape, LOW)],
        after=(mix_local,),
        teams=teams,
        hr=hr,
    )
    feed_cut = ((2, hr, cols), LOW)
    feed_cuts = simple(
        join_feed_kernel,
        "join_feed",
        (ek, hop(eg, 1), sk, hop(sg, 1)),
        [feed_cut] * teams,
        after=tuple(x_near[1:]),
        teams=teams,
        hr=hr,
    )
    feed_cuts = exchange(feed_cuts)
    x_pieces = gather_far(x_near)
    e_cut, s_cut = simple(
        lay_feed_kernel,
        "lay_feed",
        feed_cuts,
        [((hp, width), LOW), ((cols, half), LOW)],
        [((teams, 2, hr, cols), LOW)],
        teams=teams,
        hp=hp,
    )

    mix_cut = ((feats, 3 * span), LOW)
    *cuts, merge_rows = simple(
        cut_mix_kernel,
        "cut_mix",
        (mix_rows,),
        [mix_cut] * teams + [((feats, width), LOW)],
        [((feats, 3 * width + LANES), LOW)],
        after=(e_cut, s_cut, vec, *x_pieces[3:]),
        teams=teams,
        dp_n=dp_n,
        each=each,
        span=span,
        starts=starts,
        width=width,
    )
    expand_mine = along(e_cut).reshape(half, width)
    shrink_mine = along(tie(s_cut, expand_mine[0])).reshape(width, half)

    start = at[1 + team]

    def windowed(row):
        return lax.dynamic_slice_in_dim(jnp.pad(vec[row], (0, 2 * LANES)), start, span, 0)

    blank = jnp.zeros((span,), FULL)
    mix_bias = jnp.concatenate([windowed(2), blank, windowed(3)])
    shrinking = jnp.where(jnp.arange(3 * span) < span, dim**-0.5, 1.0).astype(FULL)
    mix_bias = jnp.concatenate([mix_bias[None], shrinking[None], jnp.zeros((6, 3 * span), FULL)])

    act_bytes = length * width * 2
    piece_spec = fixed((rows, width))
    vec_spec = fixed((8, width))
    mix_spec = fixed((width, 3 * span))
    team_rows = lambda n: pl.BlockSpec((own_rows, n), lambda k, a: (k ^ (a[0] // 2), 0))
    x_sizes = [v.shape[0] for v in x_pieces]
    row_specs = lambda sizes: [fixed((n, width)) for n in sizes]
    (first,) = call(
        functools.partial(norm_kernel, x_sizes, rows),
        "norm",
        (teams,),
        at,
        (*x_pieces, vec),
        row_specs(x_sizes) + [vec_spec],
        [((length, width), LOW)],
        [team_rows(width)],
        [pltpu.VMEM((own_rows, width), LOW)],
        length * width * 10,
        2 * act_bytes,
        after=(cuts[0],),
    )
    got = exchange(cuts)
    (first,), got = meet((first,), got)
    merge_rows = tie(merge_rows, *got)
    mix = [v for g in got for v in (g, hop(g, 1))]
    extra = -(-max(0, starts[-1] + span - width) // feats)
    if not whole_rows:
        mix = [assemble(mix)]
    if teams == 4:
        near = [hop(merge_rows, 2), hop(merge_rows, 4)]
    else:
        near = exchange([merge_rows] * teams)[1:]
    merge_shape = (width + extra * feats, width)

    chip_rows = lambda n: pl.BlockSpec((own_rows, n), lambda k, a: (k, 0))
    mixed, mix = call(
        functools.partial(mix_kernel, len(mix)),
        "mix",
        (teams,),
        at,
        (*mix, first, mix_bias),
        [fixed(v.shape) for v in mix] + [chip_rows(width), fixed((8, 3 * span))],
        [((length, 3 * span), LOW), ((width, 3 * span), LOW)],
        [chip_rows(3 * span), mix_spec],
        [pltpu.VMEM((width, 3 * span), FULL)],
        2 * length * width * 3 * span,
        4 * act_bytes,
    )

    (mixed, mix), near = meet((mixed, mix), near)
    merge = [merge_rows, *near]
    if teams == 4:
        merge.append(hop(merge[1], 4))
    g_own = own_pair(cotangent)
    g_near = gather_near(tie(g_own, mixed))

    seg = pick(segments, core)
    per = span // LANES
    runs = [(0, per // 2), (per // 2, per // 2)]
    seg_specs = [fixed((length, 1)), fixed((1, length))]
    segs = (seg.reshape(length, 1), seg.reshape(1, length))
    column = pl.BlockSpec((own_rows, LANES), lambda p, a: (0, p))

    def qkv_specs(base):
        return [
            pl.BlockSpec((own_rows, LANES), lambda p, a, j=j, m=m: (j, m * per + base + p))
            for m in range(3)
            for j in range(teams)
        ]

    attended, wait = [], ()
    for base, count in runs:
        got = call(
            functools.partial(attend_forward_kernel, teams, own_rows, dim, heads, base),
            "attend_forward",
            (count,),
            at,
            (*([mixed] * (3 * teams)), *segs),
            qkv_specs(base) + seg_specs,
            [((own_rows, part), LOW)] * teams,
            [column] * teams,
            [],
            length * length * dim * heads * 2,
            4 * length * part * 2,
            length * length * heads // 4,
            after=wait,
        )
        if base == 0:
            got, moved = meet(got, g_near[1:])
            g_near = [g_own, *moved]
            wait = (got[0],)
            attended = exchange(got)
            expand_mine, shrink_mine = tie(expand_mine, got[0]), tie(shrink_mine, got[0])
        else:
            got, moved = meet(got, (*attended, *merge[3:]))
            attended = [*moved[:teams], *exchange(got)]
            merge = [*merge[:3], *moved[teams:]]
    merge = [v for g in merge for v in (g, hop(g, 1))]
    if not whole_rows:
        merge = [assemble(merge, extra)]

    weights = (expand_mine, shrink_mine, hop(expand_mine, 1), hop(shrink_mine, 1))
    wide = ((own_rows, width), FULL)
    wide_low = ((own_rows, width), LOW)
    piece = ((rows, width), LOW)
    hidden, second, merge = simple(
        merge_norm_kernel,
        "merge_norm",
        (*attended, *merge, x_own, vec),
        [wide, wide_low, (merge_shape, LOW)],
        [wide_low, wide_low, (merge_shape, FULL)],
        2 * own_rows * width * span * teams,
        count=teams,
        rows=rows,
        span=span,
        share=share,
        dim=dim,
        parts=len(merge),
    )
    second = gather_near(second)
    g_pieces = g_near

    e_row = e_bias.reshape(dp_n, teams, 2, hr).transpose(1, 2, 0, 3)
    e_row = pick(e_row, team)
    e_row = jnp.stack([pick(e_row, core), pick(e_row, 1 - core)])
    e_row = jnp.pad(e_row, ((0, 0), (0, 0), (0, hp - hr))).reshape(1, units)

    groups = [[0], [1, 2], [3, 4]] if teams == 4 else [[k] for k in range(teams)]
    acts, d_pres, e_sums, d_second, out = [], [], [], [], []
    for group in groups:
        sizes = [x_sizes[i] for i in group]
        n, m = len(sizes), sum(sizes)
        half_spec = pl.BlockSpec((m, half), lambda f, a: (0, f))
        res = call(
            functools.partial(feed_kernel, sizes),
            "feed",
            (2,),
            at,
            (*[second[i] for i in group], *[g_pieces[i] for i in group], *weights, e_row),
            row_specs(sizes) * 2
            + [pl.BlockSpec(memory_space=pl.ANY)] * 4
            + [pl.BlockSpec((1, half), lambda f, a: (0, f))],
            [((m, units), LOW)] * 2
            + [((8, units), FULL)]
            + [((size, width), LOW) for size in sizes] * 2,
            [half_spec, half_spec, pl.BlockSpec((8, half), lambda f, a: (0, f))]
            + row_specs(sizes) * 2,
            [pltpu.VMEM((m, width), LOW)] * 2
            + [pltpu.VMEM((m, width), FULL)] * 2
            + [
                pltpu.VMEM((2, half, width), LOW),
                pltpu.VMEM((2, width, half), LOW),
                pltpu.SemaphoreType.DMA((4,)),
            ],
            8 * m * width * units,
            4 * width * units + 12 * m * width,
            m * units,
            after=tuple(acts[-1:]),
        )
        if len(acts) == 0:
            res, moved = meet(res, second[1:])
            second = gather_far([second[0], *moved])
            g_pieces = gather_far(g_pieces, *moved)
        elif len(acts) == 1 and teams == 4:
            res, moved = meet(res, (*second[3:], *g_pieces[3:]))
            second, g_pieces = [*second[:3], *moved[:2]], [*g_pieces[:3], *moved[2:]]
        acts.append(res[0])
        d_pres.append(res[1])
        e_sums.append(res[2])
        d_second += res[3 : 3 + n]
        out += res[3 + n :]

    sizes = [v.shape[0] for v in acts]
    def feed_grad(name, parts, units_of, turned, after):
        shape = (width, half) if turned else (half, width)
        return call(
            functools.partial(feed_grad_kernel, x_sizes, sizes, turned),
            name,
            (2,),
            at,
            (*parts, *units_of),
            [pl.BlockSpec(memory_space=pl.ANY)] * len(x_sizes)
            + [pl.BlockSpec((s, half), lambda f, a: (0, 1 - f)) for s in sizes],
            [(shape, LOW)] * 2,
            [fixed(shape)] * 2,
            [
                pltpu.VMEM((length, width), LOW),
                pltpu.VMEM((length, half), LOW),
                pltpu.SemaphoreType.DMA((len(x_sizes),)),
            ],
            2 * length * width * units,
            2 * act_bytes + 2 * width * units,
            after=after,
        )

    far = reduce_far(d_second)
    sm, sg = feed_grad("shrink_grad", g_pieces, acts, True, ())
    (sm, sg), far = meet((sm, sg), far)
    near = reduce_near(d_second, far)
    s_got = hop(sg, 1)
    em, eg = feed_grad("expand_grad", second, d_pres, False, (sm,))
    (em, eg), (s_got, *near) = meet((em, eg), (s_got, *near))
    d_second = [d_second[0], *near]
    s_sum = add_low(sm, s_got)
    e_got = hop(eg, 1)
    g_shrink = scatter(s_sum.reshape(dp_n, cols, half))

    terms = len(d_second)
    window = ((own_rows, span), LOW)
    d_hidden, d_branch, second_sums, *d_attended = simple(
        second_back_kernel,
        "second_back",
        (*d_second, hidden, g_own, merge, vec),
        [wide, wide_low, ((8, width), FULL)] + [window] * teams,
        [wide, wide_low],
        2 * own_rows * width * span * teams,
        after=(s_sum,),
        count=teams,
        rows=rows,
        span=span,
        dim=dim,
        terms=terms,
    )
    d_attended = exchange(d_attended)

    step = min(span, CHUNK)
    feat_block = ((teams, feats, width), LOW)
    mine, give = simple(
        merge_grad_kernel,
        "merge_grad",
        (*attended, d_branch),
        [feat_block, feat_block],
        [(merge_shape, FULL), ((teams * (span // step), own_rows, step), LOW)],
        2 * own_rows * width * span * teams,
        count=teams,
        span=span,
        share=share,
        dim=dim,
        step=step,
    )

    (mine, give), (e_got, *d_attended) = meet((mine, give), (e_got, *d_attended))
    e_sum = add_low(em, e_got)
    g_expand = scatter(e_sum.reshape(dp_n, hp, width))
    out_far = reduce_far([*out[:3], *[tie(v, *d_attended) for v in out[3:]]])

    def core_parts(mine, got):
        return [add_low(pick(mine, team ^ k), pick(got, team ^ k)) for k in range(teams)]

    merge_got = hop(give, 1)
    merge_mine = mine

    d_parts, g_mix, mix_sums = [], [], []
    mix_block = ((teams, feats, 3 * part), LOW)
    wait = (e_sum, mixed)
    merge_near = []
    for base in range(per):
        (d_part,) = call(
            functools.partial(attend_backward_kernel, teams, own_rows, dim, heads, share, base),
            "attend_backward",
            (1,),
            at,
            (*([mixed] * (3 * teams)), *d_attended, *segs),
            qkv_specs(base)
            + [pl.BlockSpec((own_rows, LANES), lambda p, a, base=base: (0, base + p))] * teams
            + seg_specs,
            [((3, length, LANES), LOW)],
            [pl.BlockSpec((3, length, LANES), lambda p, a: (0, 0, p))],
            [
                pltpu.VMEM((length, dim), FULL),
                pltpu.VMEM((length, dim), FULL),
                pltpu.VMEM((length, LANES), LOW),
            ],
            5 * length * length * dim * heads // per * 2,
            8 * length * LANES * 2,
            length * length * heads // per // 2,
            after=wait,
        )
        if base == 0:
            (d_part,), (merge_got, *out_far) = meet((d_part,), (merge_got, *out_far))
            out_near = reduce_near(out, out_far)
            g_merge = core_parts(merge_mine, merge_got)
        if base == per - 1:
            (d_part,), merge_near = meet((d_part,), merge_near)
        d_parts.append(d_part)
        wait = (d_part,)
        if base % (per // 2) == per // 2 - 1:
            sides = d_parts[-(per // 2) :]
            mine, give, sums = call(
                mix_grad_kernel,
                "mix_grad",
                (3,),
                at,
                (*sides, first),
                [pl.BlockSpec((1, length, LANES), lambda c, a: (c, 0, 0))] * len(sides)
                + [fixed((length, width))],
                [mix_block, mix_block, ((8, 3 * part), FULL)],
                [pl.BlockSpec((teams, feats, part), lambda c, a: (0, 0, c))] * 2
                + [pl.BlockSpec((8, part), lambda c, a: (0, c))],
                [
                    pltpu.VMEM((width, length), LOW),
                    pltpu.VMEM((width, part), FULL),
                    pltpu.VMEM((length, part), LOW),
                ],
                2 * length * width * 3 * part,
                3 * act_bytes,
            )
            if base < per - 1:
                (mine, give), out_near = meet((mine, give), out_near)
                merge_near = exchange([tie(v, give) for v in g_merge])[1:]
                mix_got = hop(give, 1)
                wait = (give,)
            else:
                (mine, give), mix_near = meet((mine, give), g_mix[1:])
                g_mix = [g_mix[0], *mix_near]
                mix_got = hop(give, 1)
            mix_sums.append(sums[0].reshape(3, part))
            g_mix += exchange(core_parts(mine, mix_got))
    out = [out[0], *out_near]
    g_merge = [g_merge[0], *merge_near]
    g_merge = functools.reduce(jnp.add, [v.astype(FULL) for v in g_merge]).astype(LOW)
    merge_each = width // dp_n
    g_merge = jnp.stack(
        [g_merge[:, d * merge_each : (d + 1) * merge_each] for d in range(dp_n)]
    )
    grad_merge = scatter(g_merge).astype(FULL)

    block_out = simple(
        block_out_kernel,
        "block_out",
        (*out, hidden, vec),
        [piece, piece],
        after=(d_parts[-1],),
        rows=rows,
        terms=terms,
    )
    block_out = swap_out(*block_out)

    feed_cuts = simple(
        split_feed_kernel,
        "split_feed",
        (g_expand, g_shrink),
        [feed_cut] * teams,
        teams=teams,
        hp=hp,
    )
    groups = [([3, 4], 3), ([1, 2], 1), ([0], 0)] if teams == 4 else [([k], k) for k in range(teams)]
    d_first, first_sums, wait = [None] * len(x_sizes), [], (give,)
    for group, low in groups:
        sizes = [x_sizes[i] for i in group]
        n = sum(sizes) // own_rows
        sums, *got = call(
            functools.partial(first_back_kernel, sizes, rows, span),
            "first_back",
            (n,),
            at,
            (*d_parts, *[x_pieces[i] for i in group], mix),
            [
                pl.BlockSpec(
                    (3, own_rows, LANES), lambda i, a, low=low: (0, (i + low) ^ (a[0] // 2), 0)
                )
            ]
            * per
            + row_specs(sizes)
            + [fixed((width, 3 * span))],
            [((8, width), FULL)] + [((size, width), LOW) for size in sizes],
            [vec_spec] + row_specs(sizes),
            [
                pltpu.VMEM((own_rows, width), LOW),
                pltpu.VMEM((own_rows, width), LOW),
                pltpu.VMEM((own_rows, 3 * span), LOW),
            ],
            2 * n * own_rows * width * 3 * span,
            n * own_rows * width * 8,
            after=wait,
        )
        wait = (sums, feed_cuts[0])
        first_sums.append(sums)
        for i, v in zip(group, got):
            d_first[i] = v
    first_sums = functools.reduce(jnp.add, first_sums)
    far = reduce_far(d_first)
    if teams == 4:
        (d_first[0], d_first[1], d_first[2]), far = meet(d_first[:3], far)
    d_first = [d_first[0], *reduce_near(d_first, far)]

    (g_mix,) = simple(
        join_mix_kernel,
        "join_mix",
        g_mix,
        [((dp_n, feats, each), LOW)],
        [((teams, feats, 3 * span), LOW), ((feats, 3 * width), LOW)],
        teams=teams,
        dp_n=dp_n,
        each=each,
        span=span,
        starts=starts,
        width=width,
    )
    grad_mix = scatter(g_mix).astype(FULL)

    ek, eg, sk, sg = simple(
        part_feed_kernel,
        "part_feed",
        exchange(feed_cuts),
        [(e_shape, LOW), (e_shape, LOW), (s_shape, LOW), (s_shape, LOW)],
        [((teams, 2, hr, cols), LOW)],
        teams=teams,
    )
    grad_expand, grad_shrink = simple(
        end_feed_kernel,
        "end_feed",
        (ek, hop(eg, 1), sk, hop(sg, 1)),
        [(expand_weight.shape, FULL), (shrink_weight.shape, FULL)],
        teams=teams,
        hr=hr,
    )

    def spread(v):
        return lax.dynamic_update_slice_in_dim(
            jnp.zeros((width + 2 * LANES,), FULL), v, start, 0
        )[:width]

    mix_sums = jnp.concatenate(mix_sums, axis=1)
    d_e = functools.reduce(jnp.add, [s[0] for s in e_sums]).reshape(2, dp_n, hp)[:, :, :hr]
    d_e = jnp.where(core == 0, d_e, d_e[::-1]).transpose(1, 0, 2)
    d_e = lax.dynamic_update_slice_in_dim(
        jnp.zeros((dp_n, teams, 2, hr), FULL), d_e[:, None], team, 1
    )
    partial = (
        first_sums[0],
        first_sums[1],
        spread(mix_sums[0]),
        spread(mix_sums[2]),
        second_sums[2],
        second_sums[0],
        second_sums[1],
        second_sums[3],
        d_e.reshape(-1),
    )
    total = reduce_small(
        jnp.concatenate([v.reshape(seq_n, -1) for v in partial], axis=1)
    )
    piece_full = ((rows, width), FULL)
    input_grad = simple(
        input_grad_kernel,
        "input_grad",
        (*d_first, d_hidden, x_own, vec),
        [piece_full, piece_full],
        after=(total, grad_expand),
        rows=rows,
        terms=terms,
    )
    input_grad = swap_out(*input_grad)

    ends = [total[i * feats : (i + 1) * feats] for i in range(8)]
    vectors = (*ends[:7], total[8 * feats :], ends[7])
    return (block_out, input_grad, grad_mix, grad_merge, grad_expand, grad_shrink, *vectors)


def solution(mesh):
    rows = P("dp", "seq", None)
    matrix = P("seq", "dp")
    vector = P("seq")
    return jax.shard_map(
        functools.partial(body, mesh.shape["seq"], mesh.shape["dp"]),
        mesh=mesh,
        in_specs=(rows, P("dp", None), rows) + (matrix,) * 4 + (vector,) * 9,
        out_specs=(rows, rows) + (matrix,) * 4 + (vector,) * 9,
        check_vma=False,
    )
```

```python
import functools

import jax
import jax.numpy as jnp
from jax import lax
from jax.experimental import pallas as pl
from jax.experimental.pallas import tpu as pltpu
from jax.sharding import PartitionSpec as P

HEADS = 25
COST = 0.25
LANES = 128
CHUNK = 256
QUERY_ROWS = 384
KEY_ROWS = 384
LOW = jnp.bfloat16
FULL = jnp.float32
VMEM_BYTES = 60 * 1024 * 1024


def dot_nn(left, right):
    return lax.dot_general(left, right, (((1,), (0,)), ((), ())), preferred_element_type=FULL)


def dot_tn(left, right):
    return lax.dot_general(left, right, (((0,), (0,)), ((), ())), preferred_element_type=FULL)


def dot_nt(left, right):
    return lax.dot_general(left, right, (((1,), (1,)), ((), ())), preferred_element_type=FULL)


def norm_parts(v):
    center = v - jnp.mean(v, axis=-1, keepdims=True)
    spread = jnp.mean(center * center, axis=-1, keepdims=True)
    inverse = lax.rsqrt(spread + 1e-05)
    return center * inverse, inverse


def norm_back(grad, gain, normal, inverse):
    e = grad * gain
    mean_e = jnp.mean(e, axis=-1, keepdims=True)
    mean_en = jnp.mean(e * normal, axis=-1, keepdims=True)
    return inverse * (e - mean_e - normal * mean_en)


def total_rows(v):
    return jnp.sum(v, axis=0, keepdims=True)


def fixed(shape):
    return pl.BlockSpec(shape, lambda *_: (0,) * len(shape), pipeline_mode=pl.Buffered(1))


def call(
    kernel, name, grid, at, operands, in_specs, outs, out_specs, scratch, flops, nbytes, exps=0, after=()
):
    if after:
        count, inner = len(operands), kernel
        kernel = lambda at_ref, *refs: inner(at_ref, *refs[:count], *refs[count + len(after) :])
        operands = (*operands, *after)
        in_specs = list(in_specs) + [pl.BlockSpec(memory_space=pl.ANY)] * len(after)
    spec = pltpu.PrefetchScalarGridSpec(
        num_scalar_prefetch=1,
        grid=grid,
        in_specs=in_specs,
        out_specs=out_specs,
        scratch_shapes=scratch,
    )
    return pl.pallas_call(
        kernel,
        grid_spec=spec,
        out_shape=[jax.ShapeDtypeStruct(s, d) for s, d in outs],
        compiler_params=pltpu.CompilerParams(vmem_limit_bytes=VMEM_BYTES),
        cost_estimate=pl.CostEstimate(
            flops=int(COST * flops),
            bytes_accessed=int(COST * nbytes),
            transcendentals=int(COST * exps),
        ),
        name=name,
    )(at, *operands)


def row_slot(half, core, rows):
    slot = core if half == 0 else 1 - core
    return pl.ds(pl.multiple_of(slot * rows, rows), rows)


def load_pair(step, sizes, refs, buf, core, rows):
    low = 0
    for size, ref in zip(sizes, refs):
        for i in range(size // rows):
            r = low // rows + i

            @pl.when(step == r // 2)
            def _():
                buf[row_slot(r % 2, core, rows), :] = ref[i * rows : (i + 1) * rows, :]

        low += size


def half_sum(refs, half, rows):
    parts = []
    for i, ref in enumerate(refs):
        if ref.shape[0] > rows:
            parts.append(ref[half * rows : (half + 1) * rows, :])
        elif (i + 1) % 2 == half:
            parts.append(ref[...])
    return functools.reduce(jnp.add, [v.astype(FULL) for v in parts])


def pair_rows(refs, core, rows, buf):
    for half in range(2):
        buf[row_slot(half, core, rows), :] = half_sum(refs, half, rows).astype(buf.dtype)


def fold_kernel(at_ref, x_ref, y_ref, far0_ref, far1_ref, xo_ref, yo_ref):
    xo_ref[...] = (x_ref[...].astype(FULL) + far1_ref[...].astype(FULL)).astype(LOW)
    yo_ref[...] = (y_ref[...].astype(FULL) + far0_ref[...].astype(FULL)).astype(LOW)


def place_rows(place, refs, wide, out):
    each = refs[0].shape[0]
    if len(refs) == 1:
        out[...] = refs[0][...]
        return
    for r, ref in enumerate(refs):
        begin = pl.multiple_of((place ^ r) * each, each)
        wide[pl.ds(begin, each), :] = ref[...].astype(FULL)
    filled = each * len(refs)
    if filled < wide.shape[0]:
        wide[filled:, :] = jnp.zeros((wide.shape[0] - filled, wide.shape[1]), FULL)
    block = 16
    for size in range(16, 129, 16):
        block = size if out.shape[0] % size == 0 else block

    def narrow(i, carry):
        span = pl.ds(pl.multiple_of(i * block, block), block)
        out[span, :] = wide[span, :].astype(LOW)
        return carry

    lax.fori_loop(0, out.shape[0] // block, narrow, 0)


def flip(v):
    rows, cols = v.shape
    v = jnp.pad(v.astype(FULL), ((0, -rows % LANES), (0, -cols % LANES)))
    return v.T[:cols, :rows]


def cut_feed_kernel(at_ref, e_ref, s_ref, ek_ref, eg_ref, sk_ref, sg_ref, *, teams, hr):
    first = at_ref[0] % 2 == 0
    cols = s_ref.shape[1]
    e, s = e_ref[...].astype(FULL), s_ref[...].astype(FULL)
    for t in range(teams):
        a, b = e[:, 2 * t * hr : (2 * t + 1) * hr], e[:, (2 * t + 1) * hr : (2 * t + 2) * hr]
        ek_ref[:, t * hr : (t + 1) * hr] = jnp.where(first, a, b).astype(LOW)
        eg_ref[:, t * hr : (t + 1) * hr] = jnp.where(first, b, a).astype(LOW)
    for t in range(teams // 2):
        a, b = s[2 * t * hr : (2 * t + 1) * hr], s[(2 * t + 1) * hr : (2 * t + 2) * hr]
        sk_ref[:, t * cols : (t + 1) * cols] = jnp.where(first, a, b).astype(LOW)
        sg_ref[:, t * cols : (t + 1) * cols] = jnp.where(first, b, a).astype(LOW)


def join_feed_kernel(at_ref, ek_ref, eo_ref, sk_ref, so_ref, *out_refs, teams, hr):
    first, team = at_ref[0] % 2 == 0, at_ref[0] // 2
    feats = ek_ref.shape[0]
    cols = 2 * feats
    mine, other = flip(ek_ref[...]), flip(eo_ref[...])
    low = jnp.where(first, mine, other).astype(LOW)
    high = jnp.where(first, other, mine).astype(LOW)
    for t in range(teams):
        part = slice((t % (teams // 2)) * cols, (t % (teams // 2) + 1) * cols)
        here = first if t < teams // 2 else jnp.logical_not(first)
        piece = jnp.where(here, sk_ref[:, part], so_ref[:, part])
        for k, ref in enumerate(out_refs):

            @pl.when((team ^ t) == k)
            def _():
                ref[0, :, :feats] = low[t * hr : (t + 1) * hr, :]
                ref[0, :, feats:] = high[t * hr : (t + 1) * hr, :]
                ref[1] = piece


def lay_feed_kernel(at_ref, *refs, teams, hp):
    part_refs, e_ref, s_ref, whole = refs[:teams], *refs[teams:]
    team = at_ref[0] // 2
    for k, ref in enumerate(part_refs):
        whole[team ^ k] = ref[...]
    hr, cols = whole.shape[2:]
    e_ref[hr:, :] = jnp.zeros((hp - hr, e_ref.shape[1]), LOW)
    s_ref[...] = jnp.zeros_like(s_ref)
    for t in range(teams):
        e_ref[:hr, t * cols : (t + 1) * cols] = whole[t, 0]
        s_ref[:, t * hp : t * hp + hr] = flip(whole[t, 1]).astype(LOW)


def split_feed_kernel(at_ref, e_ref, s_ref, *out_refs, teams, hp):
    team = at_ref[0] // 2
    hr, cols = out_refs[0].shape[1:]
    for t in range(teams):
        piece = flip(s_ref[:, t * hp : t * hp + hr]).astype(LOW)
        for k, ref in enumerate(out_refs):

            @pl.when((team ^ t) == k)
            def _():
                ref[0] = e_ref[:hr, t * cols : (t + 1) * cols]
                ref[1] = piece


def part_feed_kernel(at_ref, *refs, teams):
    part_refs, ek_ref, eg_ref, sk_ref, sg_ref, whole = refs[:teams], *refs[teams:]
    first, team = at_ref[0] % 2 == 0, at_ref[0] // 2
    for k, ref in enumerate(part_refs):
        whole[team ^ k] = ref[...]
    hr, cols = whole.shape[2:]
    feats = cols // 2
    for t in range(teams):
        e = flip(whole[t, 0])
        a, b = e[:feats, :], e[feats:, :]
        ek_ref[:, t * hr : (t + 1) * hr] = jnp.where(first, a, b).astype(LOW)
        eg_ref[:, t * hr : (t + 1) * hr] = jnp.where(first, b, a).astype(LOW)
    for t in range(teams // 2):
        a, b = whole[t, 1], whole[teams // 2 + t, 1]
        sk_ref[:, t * cols : (t + 1) * cols] = jnp.where(first, a, b)
        sg_ref[:, t * cols : (t + 1) * cols] = jnp.where(first, b, a)


def end_feed_kernel(at_ref, ek_ref, eo_ref, sk_ref, so_ref, e_ref, s_ref, *, teams, hr):
    first = at_ref[0] % 2 == 0
    cols = s_ref.shape[1]
    mine, other = ek_ref[...].astype(FULL), eo_ref[...].astype(FULL)
    low, high = jnp.where(first, mine, other), jnp.where(first, other, mine)
    for t in range(teams):
        e_ref[:, 2 * t * hr : (2 * t + 1) * hr] = low[:, t * hr : (t + 1) * hr]
        e_ref[:, (2 * t + 1) * hr : (2 * t + 2) * hr] = high[:, t * hr : (t + 1) * hr]
    mine, other = sk_ref[...].astype(FULL), so_ref[...].astype(FULL)
    low, high = jnp.where(first, mine, other), jnp.where(first, other, mine)
    for t in range(teams // 2):
        s_ref[2 * t * hr : (2 * t + 1) * hr, :] = low[:, t * cols : (t + 1) * cols]
        s_ref[(2 * t + 1) * hr : (2 * t + 2) * hr, :] = high[:, t * cols : (t + 1) * cols]


def cut_mix_kernel(at_ref, rows_ref, *refs, teams, dp_n, each, span, starts, width):
    out_refs, merge_ref, full = refs[:teams], refs[teams], refs[teams + 1]
    team = at_ref[0] // 2
    part = width // dp_n
    for d in range(dp_n):
        full[:, d * each : (d + 1) * each] = rows_ref[d, :, :each]
        merge_ref[:, d * part : (d + 1) * part] = rows_ref[d, :, each:]
    full[:, dp_n * each :] = jnp.zeros((full.shape[0], full.shape[1] - dp_n * each), LOW)
    for t in range(teams):
        for k, ref in enumerate(out_refs):

            @pl.when((team ^ t) == k)
            def _():
                for m in range(3):
                    begin = m * width + starts[t]
                    ref[:, m * span : (m + 1) * span] = full[:, begin : begin + span]


def join_mix_kernel(at_ref, *refs, teams, dp_n, each, span, starts, width):
    part_refs, out_ref, whole, flat = refs[:teams], *refs[teams:]
    team = at_ref[0] // 2
    share = width // teams
    for k, ref in enumerate(part_refs):
        whole[team ^ k] = ref[...]
    for m in range(3):
        for t in range(teams):
            low = m * span + share * t - starts[t]
            begin = m * width + share * t
            flat[:, begin : begin + share] = whole[t, :, low : low + share]
    for d in range(dp_n):
        out_ref[d] = flat[:, d * each : (d + 1) * each]


def add_parts_kernel(at_ref, mine_ref, got_ref, *out_refs):
    team = at_ref[0] // 2
    for k, ref in enumerate(out_refs):
        total = mine_ref[team ^ k].astype(FULL) + got_ref[team ^ k].astype(FULL)
        ref[...] = total.astype(LOW)


def norm_kernel(sizes, rows, at_ref, *refs):
    count = len(sizes)
    vec_ref, first_ref, turned_ref, buf = refs[count:]
    load_pair(pl.program_id(0), sizes, refs[:count], buf, at_ref[0] % 2, rows)
    normal, _ = norm_parts(buf[...].astype(FULL))
    first = (normal * vec_ref[0:1, :] + vec_ref[1:2, :]).astype(LOW)
    first_ref[...] = first
    turned_ref[...] = first.T


def mix_kernel(parts, at_ref, *refs):
    first_ref, bias_ref, mixed_ref, mix_ref, wide = refs[parts:]

    @pl.when(pl.program_id(0) == 0)
    def _():
        place_rows(at_ref[0], refs[:parts], wide, mix_ref)

    mixed = dot_nn(first_ref[...], mix_ref[...]) + bias_ref[0:1, :]
    mixed_ref[...] = (mixed * bias_ref[1:2, :]).astype(LOW)


def causal_chunks(length, begin):
    stop = begin + QUERY_ROWS
    return [(low, min(low + KEY_ROWS, stop)) for low in range(0, stop, KEY_ROWS)]


def visible_scores(query, key, begin, low, col_ref, row_ref):
    scores = dot_nt(query, key)
    rows, cols = scores.shape
    seen = col_ref[begin : begin + rows, :] == row_ref[:, low : low + cols]
    if low + cols > begin:
        row_id = lax.broadcasted_iota(jnp.int32, (rows, cols), 0) + begin
        col_id = lax.broadcasted_iota(jnp.int32, (rows, cols), 1) + low
        seen = seen & (col_id <= row_id)
    return jnp.where(seen, scores, -1e30)


def attend_forward_kernel(count, block, dim, heads, base, at_ref, *refs):
    q_ref, k_ref, v_ref, col_ref, row_ref = refs[:5]
    out_refs, log_ref = refs[5:-1], refs[-1]
    pair = pl.program_id(0) + base
    team = at_ref[0] // 2
    for ref in out_refs:
        ref[...] = jnp.zeros_like(ref)
    for sub in range(LANES // dim):

        @pl.when(pair * (LANES // dim) + sub < heads)
        def _():
            lanes = slice(sub * dim, (sub + 1) * dim)
            for begin in range(0, count * block, QUERY_ROWS):
                rows = slice(begin, begin + QUERY_ROWS)
                query = q_ref[rows, lanes]
                chunks = causal_chunks(count * block, begin)
                scores = [
                    visible_scores(
                        query, k_ref[low:high, lanes], begin, low, col_ref, row_ref
                    )
                    for low, high in chunks
                ]
                top = functools.reduce(
                    jnp.maximum, [jnp.max(p, axis=1, keepdims=True) for p in scores]
                )
                expo = [jnp.exp(p - top) for p in scores]
                total = functools.reduce(
                    jnp.add, [jnp.sum(p, axis=1, keepdims=True) for p in expo]
                )
                mixed = functools.reduce(
                    jnp.add,
                    [
                        dot_nn(e.astype(LOW), v_ref[low:high, lanes])
                        for e, (low, high) in zip(expo, chunks)
                    ],
                )
                mixed = (mixed / total).astype(LOW)
                log_ref[rows, lanes] = jnp.broadcast_to(top + jnp.log(total), (QUERY_ROWS, dim))
                place = slice(begin % block, begin % block + QUERY_ROWS)
                for k, ref in enumerate(out_refs):

                    @pl.when((team ^ (begin // block)) == k)
                    def _():
                        ref[place, lanes] = mixed


def attend_backward_kernel(count, block, dim, heads, share, base, at_ref, *refs):
    q_ref, k_ref, v_ref, *g_refs = refs[: 3 + count]
    col_ref, row_ref, log_ref, d_ref, acc_k, acc_v, grads, logs = refs[3 + count :]
    pair = pl.program_id(0) + base
    team = at_ref[0] // 2
    scale = dim**-0.5
    d_ref[...] = jnp.zeros_like(d_ref)
    logs[...] = log_ref[...].T
    for k, ref in enumerate(g_refs):
        grads[pl.ds(pl.multiple_of((team ^ k) * block, block), block), :] = ref[...]
    for sub in range(LANES // dim):

        @pl.when(pair * (LANES // dim) + sub < heads)
        def _():
            lanes = slice(sub * dim, (sub + 1) * dim)
            column = lax.broadcasted_iota(jnp.int32, (1, dim), 1)
            column = column + at_ref[1 + team] + pair * LANES + sub * dim
            owned = (column >= share * team) & (column < share * (team + 1))
            owned = jnp.where(owned, 1.0, 0.0)
            acc_k[...] = jnp.zeros_like(acc_k)
            acc_v[...] = jnp.zeros_like(acc_v)
            for begin in range(0, count * block, QUERY_ROWS):
                rows = slice(begin, begin + QUERY_ROWS)
                query = q_ref[rows, lanes]
                grad = grads[rows, lanes]
                log_total = logs[sub * dim : sub * dim + 1, rows]
                chunks = causal_chunks(count * block, begin)
                probs, d_weights = [], []
                for low, high in chunks:
                    scores = dot_nt(k_ref[low:high, lanes], query)
                    seen = col_ref[low:high, :] == row_ref[:, rows]
                    if high > begin:
                        key_id = lax.broadcasted_iota(jnp.int32, scores.shape, 0) + low
                        query_id = lax.broadcasted_iota(jnp.int32, scores.shape, 1) + begin
                        seen = seen & (key_id <= query_id)
                    probs.append(jnp.exp(jnp.where(seen, scores, -1e30) - log_total))
                    d_weights.append(dot_nt(v_ref[low:high, lanes], grad))
                delta = functools.reduce(
                    jnp.add, [total_rows(p * d) for p, d in zip(probs, d_weights)]
                )
                d_query = jnp.zeros((QUERY_ROWS, dim), FULL)
                for prob, d_weight, (low, high) in zip(probs, d_weights, chunks):
                    d_scores = (prob * (d_weight - delta)).astype(LOW)
                    d_query = d_query + dot_tn(d_scores, k_ref[low:high, lanes])
                    acc_k[low:high, :] += dot_nn(d_scores, query)
                    acc_v[low:high, :] += dot_nn(prob.astype(LOW), grad)
                d_ref[0, rows, lanes] = (d_query * scale * owned).astype(LOW)
            d_ref[1, :, lanes] = (acc_k[...] * owned).astype(LOW)
            d_ref[2, :, lanes] = (acc_v[...] * owned).astype(LOW)


def merge_norm_kernel(at_ref, *refs, count, rows, span, share, dim, parts):
    att_refs, part_refs = refs[: 2 * count], refs[2 * count : 2 * count + parts]
    x_ref, vec_ref, hid_ref, s_ref, merge_ref, xs, buf, wide = refs[2 * count + parts :]
    core, team = at_ref[0] % 2, at_ref[0] // 2
    place_rows(at_ref[0], part_refs, wide, merge_ref)
    pair_rows([x_ref], core, rows, xs)
    hidden = xs[...].astype(FULL) + vec_ref[4:5, :]
    lane = lax.broadcasted_iota(jnp.int32, (1, span), 1)
    for k in range(count):
        other = team ^ k
        start = at_ref[1 + other]
        low = share * other - start
        owned = (lane >= low) & (lane < low + share)
        piece = jnp.concatenate([att_refs[k][...], att_refs[count + k][...]], axis=1)
        piece = jnp.where(owned, piece, jnp.zeros((), LOW))
        hidden = hidden + dot_nn(piece, merge_ref[pl.ds(pl.multiple_of(start, dim), span), :])
    hid_ref[...] = hidden
    normal, _ = norm_parts(hidden)
    buf[...] = (normal * vec_ref[5:6, :] + vec_ref[6:7, :]).astype(LOW)
    s_ref[:rows, :] = buf[row_slot(0, core, rows), :]
    s_ref[rows:, :] = buf[row_slot(1, core, rows), :]


def feed_kernel(sizes, out_sizes, at_ref, *refs):
    pieces, count = len(sizes), len(out_sizes)
    lows = [sum(sizes[:i]) for i in range(pieces)]
    sec_refs, g_refs = refs[:pieces], refs[pieces : 2 * pieces]
    weights, (bias_ref, act_ref, dpre_ref, sum_ref) = (
        refs[2 * pieces : 2 * pieces + 4],
        refs[2 * pieces + 4 : 2 * pieces + 8],
    )
    rest = refs[2 * pieces + 8 :]
    ds_refs, out_refs = rest[:count], rest[count : 2 * count]
    sec, g, acc_s, acc_o, e_held, s_held, sems = rest[2 * count :]
    step = pl.program_id(0)
    copies = [
        pltpu.make_async_copy(ref, held.at[i // 2], sems.at[i])
        for i, (ref, held) in enumerate(zip(weights, (e_held, s_held) * 2))
    ]

    @pl.when(step == 0)
    def _():
        for copy in copies:
            copy.start()
        for i in range(pieces):
            sec[lows[i] : lows[i] + sizes[i], :] = sec_refs[i][...]
            g[lows[i] : lows[i] + sizes[i], :] = g_refs[i][...]
        copies[0].wait()
        copies[1].wait()

    @pl.when(step == 1)
    def _():
        copies[2].wait()
        copies[3].wait()

    et, st = e_held[step], s_held[step]
    u = dot_nt(sec[...], et) + bias_ref[...]
    d_act = dot_nn(g[...], st)
    square = u * u
    tanh = jnp.tanh(0.7978845608028654 * u * (1.0 + 0.044715 * square))
    plus = 0.5 * (1.0 + tanh)
    act = (u * plus).astype(LOW)
    slope = plus + u * (0.5 * 0.7978845608028654) * (1.0 - tanh * tanh) * (
        1.0 + 3 * 0.044715 * square
    )
    d_pre = (d_act * slope).astype(LOW)
    act_ref[...] = act
    dpre_ref[...] = d_pre
    sum_ref[...] = jnp.broadcast_to(total_rows(d_pre.astype(FULL)), sum_ref.shape)
    part_s = dot_nn(d_pre, et)
    part_o = dot_nt(act, st)

    @pl.when(step == 0)
    def _():
        acc_s[...] = part_s
        acc_o[...] = part_o

    @pl.when(step == 1)
    def _():
        for i in range(count):
            here = slice(sum(out_sizes[:i]), sum(out_sizes[: i + 1]))
            ds_refs[i][...] = (acc_s[here, :] + part_s[here, :]).astype(LOW)
            out_refs[i][...] = (acc_o[here, :] + part_o[here, :]).astype(LOW)


def feed_grad_kernel(pieces, sizes, turned, at_ref, *refs):
    count = len(pieces)
    piece_refs, unit_refs = refs[:count], refs[count : count + len(sizes)]
    mine_ref, give_ref, held, units, sems = refs[count + len(sizes) :]
    step = pl.program_id(0)
    copies = [
        pltpu.make_async_copy(
            ref, held.at[sum(pieces[:i]) : sum(pieces[: i + 1]), :], sems.at[i]
        )
        for i, ref in enumerate(piece_refs)
    ]

    @pl.when(step == 0)
    def _():
        for copy in copies:
            copy.start()
        for copy in copies:
            copy.wait()

    low = 0
    for size, ref in zip(sizes, unit_refs):
        units[low : low + size, :] = ref[...]
        low += size
    if turned:
        grad = dot_tn(held[...], units[...]).astype(LOW)
    else:
        grad = dot_tn(units[...], held[...]).astype(LOW)

    @pl.when(step == 0)
    def _():
        give_ref[...] = grad

    @pl.when(step == 1)
    def _():
        mine_ref[...] = grad


def second_back_kernel(at_ref, *refs, count, rows, span, dim, terms):
    rest = refs[terms:]
    hid_ref, g_ref, merge_ref, vec_ref = rest[:4]
    dh_ref, db_ref, sum_ref = rest[4:7]
    att_refs = rest[7 : 7 + count]
    ds, g = rest[7 + count :]
    core, team = at_ref[0] % 2, at_ref[0] // 2
    pair_rows(refs[:terms], core, rows, ds)
    pair_rows([g_ref], core, rows, g)
    normal, inverse = norm_parts(hid_ref[...])
    d_second = ds[...]
    g_full = g[...].astype(FULL)
    d_hidden = g_full + norm_back(d_second, vec_ref[5:6, :], normal, inverse)
    dh_ref[...] = d_hidden
    d_branch = d_hidden.astype(LOW)
    db_ref[...] = d_branch
    sum_ref[0:1, :] = total_rows(d_second * normal)
    sum_ref[1:2, :] = total_rows(d_second)
    sum_ref[2:3, :] = total_rows(d_branch.astype(FULL))
    sum_ref[3:4, :] = total_rows(g_full)
    sum_ref[4:8, :] = jnp.zeros((4, sum_ref.shape[1]), FULL)
    for k, ref in enumerate(att_refs):
        start = pl.multiple_of(at_ref[1 + (team ^ k)], dim)
        ref[...] = dot_nt(d_branch, merge_ref[pl.ds(start, span), :]).astype(LOW)


def split_cores(core, value, mine_ref, give_ref):
    feats = mine_ref.shape[1]
    for t in range(mine_ref.shape[0]):
        low = value[2 * t * feats : (2 * t + 1) * feats, :]
        high = value[(2 * t + 1) * feats : (2 * t + 2) * feats, :]
        mine_ref[t] = jnp.where(core == 0, low, high).astype(LOW)
        give_ref[t] = jnp.where(core == 0, high, low).astype(LOW)


def merge_grad_kernel(at_ref, *refs, count, span, share, dim, step):
    att_refs = refs[: 2 * count]
    db_ref, mine_ref, give_ref, acc, held = refs[2 * count :]
    team = at_ref[0] // 2
    acc[...] = jnp.zeros_like(acc)
    lane = lax.broadcasted_iota(jnp.int32, (1, span), 1)
    for k in range(count):
        other = team ^ k
        low = share * other - at_ref[1 + other]
        owned = (lane >= low) & (lane < low + share)
        piece = jnp.concatenate([att_refs[k][...], att_refs[count + k][...]], axis=1)
        piece = jnp.where(owned, piece, jnp.zeros((), LOW))
        for c in range(span // step):
            held[k * (span // step) + c] = piece[:, c * step : (c + 1) * step]

    def add(i, carry):
        start = at_ref[1 + (team ^ (i // (span // step)))] + (i % (span // step)) * step
        acc[pl.ds(pl.multiple_of(start, dim), step), :] += dot_tn(held[i], db_ref[...])
        return carry

    lax.fori_loop(0, count * (span // step), add, 0)
    split_cores(at_ref[0] % 2, acc, mine_ref, give_ref)


def first_back_kernel(sizes, out_sizes, rows, span, at_ref, *refs):
    count, out_count = len(sizes), len(out_sizes)
    sides = 2
    d_refs, x_refs, refs = refs[:sides], refs[sides : sides + count], refs[sides + count :]
    mix_ref, sum_ref = refs[:2]
    out_refs = refs[2 : 2 + out_count]
    buf, low, joined = refs[2 + out_count :]
    step = pl.program_id(0)
    core = at_ref[0] % 2
    load_pair(step, sizes, x_refs, buf, core, rows)
    normal, _ = norm_parts(buf[...].astype(FULL))
    for m in range(3):
        for i, d_ref in enumerate(d_refs):
            n = span // sides
            begin = m * span + i * n
            joined[:, begin : begin + n] = d_ref[m]
    d_first = dot_nt(joined[...], mix_ref[...])

    @pl.when(step == 0)
    def _():
        sum_ref[...] = jnp.zeros_like(sum_ref)

    sum_ref[0:1, :] += total_rows(d_first * normal)
    sum_ref[1:2, :] += total_rows(d_first)
    low[...] = d_first.astype(LOW)
    begin = 0
    for size, ref in zip(out_sizes, out_refs):
        for i in range(size // rows):
            r = begin // rows + i

            @pl.when(step == r // 2)
            def _():
                ref[i * rows : (i + 1) * rows, :] = low[row_slot(r % 2, core, rows), :]

        begin += size


def mix_grad_kernel(at_ref, *refs):
    turned_ref, mine_ref, give_ref, sum_ref, held, d = refs[-6:]
    for i, ref in enumerate(refs[:-6]):
        n = ref.shape[2]
        d[:, i * n : (i + 1) * n] = ref[0]
    sum_ref[...] = jnp.broadcast_to(total_rows(d[...].astype(FULL)), sum_ref.shape)
    held[...] = dot_nn(turned_ref[...], d[...])
    split_cores(at_ref[0] % 2, held, mine_ref, give_ref)


def block_out_kernel(at_ref, *refs, rows, terms):
    hid_ref, vec_ref, o0_ref, o1_ref = refs[terms:]
    core = at_ref[0] % 2
    for half, ref in enumerate((o0_ref, o1_ref)):
        value = hid_ref[row_slot(half, core, rows), :] + vec_ref[7:8, :]
        ref[...] = (value + half_sum(refs[:terms], half, rows)).astype(LOW)


def input_grad_kernel(at_ref, *refs, rows, terms):
    dh_ref, x_ref, vec_ref, o0_ref, o1_ref = refs[terms:]
    core = at_ref[0] % 2
    for half, ref in enumerate((o0_ref, o1_ref)):
        d_first = half_sum(refs[:terms], half, rows)
        normal, inverse = norm_parts(x_ref[half * rows : (half + 1) * rows, :].astype(FULL))
        back = norm_back(d_first, vec_ref[0:1, :], normal, inverse)
        ref[...] = dh_ref[row_slot(half, core, rows), :] + back


def body(
    seq_n,
    dp_n,
    inputs,
    segments,
    cotangent,
    mix_weight,
    merge_weight,
    expand_weight,
    shrink_weight,
    first_gain,
    first_bias,
    query_bias,
    value_bias,
    merge_bias,
    second_gain,
    second_bias,
    expand_bias,
    shrink_bias,
):
    micro, rows, width = inputs.shape
    length = segments.shape[1]
    dim = width // HEADS
    teams = seq_n // 2
    bits = teams.bit_length() - 1
    pieces = seq_n
    own_rows = 2 * rows
    feats = width // seq_n
    share = width // teams
    begins = [share * t // dim for t in range(teams)]
    heads = max(-(-share * (t + 1) // dim) - begins[t] for t in range(teams))
    starts = [dim * min(h, HEADS - heads) for h in begins]
    span = -(-heads * dim // (2 * LANES)) * 2 * LANES
    part = span // 2
    hidden_units = expand_weight.shape[1] * dp_n
    hr = hidden_units // dp_n // teams // 2
    hp = hr
    while hp % 16 or dp_n * hp % LANES:
        hp += 1
    half = dp_n * hp
    units = 2 * half
    whole_rows = feats % 8 == 0

    place = lax.axis_index("seq")
    core = place % 2
    team = place // 2
    at = jnp.concatenate([place[None].astype(jnp.int32), jnp.asarray(starts, jnp.int32)])

    def hop(v, mask):
        shape = v.shape
        if len(shape) == 2 and shape[0] % LANES == 0 and shape[1] % LANES:
            v = v.reshape(2, shape[0] // 2, shape[1])
        return lax.ppermute(v, "seq", [(i, i ^ mask) for i in range(seq_n)]).reshape(shape)

    def pick(v, index):
        return lax.dynamic_index_in_dim(v, index, 0, keepdims=False)

    def along(v):
        return lax.all_gather(v, "dp", axis=0)

    def scatter(v):
        return lax.psum_scatter(v, "dp", scatter_dimension=0)

    def by_core(mine, other):
        return jnp.where(core == 0, jnp.stack([mine, other]), jnp.stack([other, mine]))

    def tie(v, *others):
        return lax.optimization_barrier((v, *others))[0]

    def meet(kept, moved):
        both = lax.optimization_barrier((*kept, *moved))
        return both[: len(kept)], both[len(kept) :]

    def own_pair(v, *others):
        mine = pick(v, core)
        return jnp.concatenate([mine, hop(tie(pick(v, 1 - core), *others), 1)], axis=0)

    def gather_near(own):
        if teams == 4:
            return [own, hop(own, 2), hop(own, 4)]
        return exchange([own] * teams)

    def gather_far(near, *others):
        if teams == 4:
            x, y = tie(near[1][:rows], *others), tie(near[2][rows:], *others)
            return [*near, hop(x, 4), hop(y, 2)]
        return near

    def add_low(a, b):
        return (a.astype(FULL) + b.astype(FULL)).astype(LOW)

    def reduce_early(p):
        return [hop(p[1], 2), hop(p[4], 4)] if teams == 4 else exchange(p)[1:]

    def reduce_far(p):
        return [hop(p[5], 2), hop(p[6], 4)] if teams == 4 else []

    def reduce_late(p, far, after=()):
        if teams != 4:
            return [], ()
        folded = simple(
            fold_kernel, "fold", (p[2], p[3], *far), [((rows, width), LOW)] * 2, after=after
        )
        return [hop(folded[0], 2), hop(folded[1], 4)], folded

    def reduce_terms(p, early, late):
        if teams == 4:
            return [p[0], early[0], late[0], late[1], early[1]]
        return [p[0], *early]

    def exchange(parts):
        return [parts[0]] + [hop(parts[k], 2 * k) for k in range(1, teams)]

    def assemble(parts, extra=0):
        out = jnp.zeros((seq_n + extra,) + parts[0].shape, parts[0].dtype)
        for r in range(pieces):
            out = lax.dynamic_update_index_in_dim(out, parts[r], place ^ r, 0)
        return out.reshape((-1,) + parts[0].shape[1:])

    def swap_out(out0, out1):
        return by_core(out0, hop(out1, 1))

    def gather_small(v):
        cur = v[None]
        for b in range(bits + 1):
            got = hop(cur, 1 << b)
            bit = (place >> b) & 1
            cur = jnp.where(
                bit == 0, jnp.concatenate([cur, got]), jnp.concatenate([got, cur])
            )
        return cur

    def reduce_small(v, *others):
        for b in reversed(range(bits + 1)):
            half_n = v.shape[0] // 2
            bit = (place >> b) & 1
            mine = jnp.where(bit == 0, v[:half_n], v[half_n:])
            give = jnp.where(bit == 0, v[half_n:], v[:half_n])
            v = mine + hop(give, 1 << b)
        v = tie(v[0], *others)
        for b in range(dp_n.bit_length() - 1):
            v = v + lax.ppermute(v, "dp", [(i, i ^ (1 << b)) for i in range(dp_n)])
        return v

    def simple(kernel, name, operands, outs, scratch=(), flops=0, nbytes=None, after=(), **named):
        if nbytes is None:
            nbytes = sum(v.size * v.dtype.itemsize for v in operands)
            nbytes += sum(4 * functools.reduce(lambda a, b: a * b, s) for s, _ in outs)
        return call(
            functools.partial(kernel, **named),
            name,
            (1,),
            at,
            operands,
            [fixed(v.shape) for v in operands],
            outs,
            [fixed(s) for s, _ in outs],
            [pltpu.VMEM(s, d) for s, d in scratch],
            flops,
            nbytes,
            after=after,
        )

    each = mix_weight.shape[1]
    mix_local = jnp.concatenate([mix_weight, merge_weight], axis=1)
    mix_rows = along(mix_local)
    small = (
        first_gain,
        first_bias,
        query_bias,
        value_bias,
        merge_bias,
        second_gain,
        second_bias,
        shrink_bias,
        expand_bias,
    )
    packed = gather_small(jnp.concatenate([v.reshape(-1, feats) for v in small], axis=0))
    x_own = own_pair(inputs)
    x_near = gather_near(tie(x_own, packed))

    cols = shrink_weight.shape[1]
    e_shape, s_shape = (feats, teams * hr), (hr, teams // 2 * cols)
    ek, eg, sk, sg = simple(
        cut_feed_kernel,
        "cut_feed",
        (expand_weight, shrink_weight),
        [(e_shape, LOW), (e_shape, LOW), (s_shape, LOW), (s_shape, LOW)],
        after=(mix_local,),
        teams=teams,
        hr=hr,
    )
    feed_cut = ((2, hr, cols), LOW)
    feed_cuts = simple(
        join_feed_kernel,
        "join_feed",
        (ek, hop(eg, 1), sk, hop(sg, 1)),
        [feed_cut] * teams,
        teams=teams,
        hr=hr,
    )
    feed_cuts, x_near = meet(exchange(feed_cuts), x_near)
    x_pieces = gather_far(x_near)
    vec = packed[:, :8].transpose(1, 0, 2)
    vec = vec.reshape(8, width).astype(FULL)
    e_bias = packed[:, 8:].reshape(-1).astype(FULL)
    mix_cut = ((feats, 3 * span), LOW)
    *cuts, merge_rows = simple(
        cut_mix_kernel,
        "cut_mix",
        (mix_rows,),
        [mix_cut] * teams + [((feats, width), LOW)],
        [((feats, 3 * width + LANES), LOW)],
        after=(*feed_cuts, vec),
        teams=teams,
        dp_n=dp_n,
        each=each,
        span=span,
        starts=starts,
        width=width,
    )
    e_cut, s_cut = simple(
        lay_feed_kernel,
        "lay_feed",
        feed_cuts,
        [((hp, width), LOW), ((cols, half), LOW)],
        [((teams, 2, hr, cols), LOW)],
        after=(cuts[0],),
        teams=teams,
        hp=hp,
    )

    expand_mine = along(e_cut).reshape(half, width)
    shrink_mine = along(tie(s_cut, expand_mine[0])).reshape(width, half)

    start = at[1 + team]

    def windowed(row):
        return lax.dynamic_slice_in_dim(jnp.pad(vec[row], (0, 2 * LANES)), start, span, 0)

    blank = jnp.zeros((span,), FULL)
    mix_bias = jnp.concatenate([windowed(2), blank, windowed(3)])
    shrinking = jnp.where(jnp.arange(3 * span) < span, dim**-0.5, 1.0).astype(FULL)
    mix_bias = jnp.concatenate([mix_bias[None], shrinking[None], jnp.zeros((6, 3 * span), FULL)])

    act_bytes = length * width * 2
    piece_spec = fixed((rows, width))
    vec_spec = fixed((8, width))
    mix_spec = fixed((width, 3 * span))
    team_rows = lambda n: pl.BlockSpec((own_rows, n), lambda k, a: (k ^ (a[0] // 2), 0))
    x_sizes = [v.shape[0] for v in x_pieces]
    row_specs = lambda sizes: [fixed((n, width)) for n in sizes]
    first, first_t = call(
        functools.partial(norm_kernel, x_sizes, rows),
        "norm",
        (teams,),
        at,
        (*x_pieces, vec),
        row_specs(x_sizes) + [vec_spec],
        [((length, width), LOW), ((width, length), LOW)],
        [
            team_rows(width),
            pl.BlockSpec((width, own_rows), lambda k, a: (0, k ^ (a[0] // 2))),
        ],
        [pltpu.VMEM((own_rows, width), LOW)],
        length * width * 10,
        2 * act_bytes,
        after=(cuts[0],),
    )
    got = exchange(cuts)
    (first, first_t), moved = meet((first, first_t), got[1:])
    got = [got[0], *moved]
    merge_rows = tie(merge_rows, *got)
    mix = [v for g in got for v in (g, hop(g, 1))]
    extra = -(-max(0, starts[-1] + span - width) // feats)
    if not whole_rows:
        mix = [assemble(mix)]
    if teams == 4:
        near = [hop(merge_rows, 2), hop(merge_rows, 4)]
    else:
        near = exchange([merge_rows] * teams)[1:]
    merge_shape = (width + extra * feats, width)

    chip_rows = lambda n: pl.BlockSpec((own_rows, n), lambda k, a: (k, 0))
    mixed, mix = call(
        functools.partial(mix_kernel, len(mix)),
        "mix",
        (teams,),
        at,
        (*mix, first, mix_bias),
        [fixed(v.shape) for v in mix] + [chip_rows(width), fixed((8, 3 * span))],
        [((length, 3 * span), LOW), ((width, 3 * span), LOW)],
        [chip_rows(3 * span), mix_spec],
        [pltpu.VMEM((width, 3 * span), FULL)],
        2 * length * width * 3 * span,
        4 * act_bytes,
    )

    (mixed, mix), near = meet((mixed, mix), near)
    merge = [merge_rows, *near]
    g_own = own_pair(cotangent)
    g_near = gather_near(tie(g_own, mixed))

    seg = pick(segments, core)
    per = span // LANES
    runs = [(0, per // 2), (per // 2, per // 2)]
    seg_specs = [fixed((length, 1)), fixed((1, length))]
    segs = (seg.reshape(length, 1), seg.reshape(1, length))
    column = pl.BlockSpec((own_rows, LANES), lambda p, a: (0, p))

    def qkv_specs(base):
        return [
            pl.BlockSpec((length, LANES), lambda p, a, m=m: (0, m * per + base + p))
            for m in range(3)
        ]

    attended, wait = [], ()
    logs = []
    for base, count in runs:
        *got, log = call(
            functools.partial(attend_forward_kernel, teams, own_rows, dim, heads, base),
            "attend_forward",
            (count,),
            at,
            (mixed, mixed, mixed, *segs),
            qkv_specs(base) + seg_specs,
            [((own_rows, part), LOW)] * teams + [((length, part), FULL)],
            [column] * teams + [pl.BlockSpec((length, LANES), lambda p, a: (0, p))],
            [],
            length * length * dim * heads * 2,
            4 * length * part * 2,
            length * length * heads // 4,
            after=wait,
        )
        logs.append(log)
        if base == 0:
            other = [hop(v, 1) for v in merge]
            got, (*other, g_x, g_y) = meet(got, (*other, *g_near[1:3]))
            g_near = [g_own, g_x, g_y, *g_near[3:]]
            wait = (got[0],)
            attended = exchange(got)
            expand_other = hop(tie(expand_mine, got[0]), 1)
            if teams == 4:
                merge.append(hop(tie(merge[1], got[0]), 4))
        else:
            got, (expand_other, *moved) = meet(got, (expand_other, *attended, *merge[3:]))
            attended = [*moved[:teams], *exchange(got)]
            shrink_other = hop(tie(shrink_mine, got[0]), 1)
            merge = [*merge[:3], *moved[teams:]]
            other += [hop(v, 1) for v in merge[len(other) :]]
    merge = [v for both in zip(merge, other) for v in both]
    if not whole_rows:
        merge = [assemble(merge, extra)]

    weights = (expand_mine, shrink_mine, expand_other, shrink_other)
    wide = ((own_rows, width), FULL)
    wide_low = ((own_rows, width), LOW)
    piece = ((rows, width), LOW)
    hidden, second, merge = simple(
        merge_norm_kernel,
        "merge_norm",
        (*attended, *merge, x_own, vec),
        [wide, wide_low, (merge_shape, LOW)],
        [wide_low, wide_low, (merge_shape, FULL)],
        2 * own_rows * width * span * teams,
        count=teams,
        rows=rows,
        span=span,
        share=share,
        dim=dim,
        parts=len(merge),
    )
    second = gather_near(second)
    g_pieces = g_near

    e_row = e_bias.reshape(dp_n, teams, 2, hr).transpose(1, 2, 0, 3)
    e_row = pick(e_row, team)
    e_row = jnp.stack([pick(e_row, core), pick(e_row, 1 - core)])
    e_row = jnp.pad(e_row, ((0, 0), (0, 0), (0, hp - hr))).reshape(1, units)

    groups = [[0], [1, 2], [3, 4]] if teams == 4 else [[k] for k in range(teams)]
    acts, d_pres, e_sums, d_second, out = [], [], [], [], []
    for group in groups:
        sizes = [x_sizes[i] for i in group]
        out_sizes = sizes if len(sizes) == 1 else [rows] * (sum(sizes) // rows)
        n, m = len(out_sizes), sum(sizes)
        half_spec = pl.BlockSpec((m, half), lambda f, a: (0, f))
        res = call(
            functools.partial(feed_kernel, sizes, out_sizes),
            "feed",
            (2,),
            at,
            (*[second[i] for i in group], *[g_pieces[i] for i in group], *weights, e_row),
            row_specs(sizes) * 2
            + [pl.BlockSpec(memory_space=pl.ANY)] * 4
            + [pl.BlockSpec((1, half), lambda f, a: (0, f))],
            [((m, units), LOW)] * 2
            + [((8, units), FULL)]
            + [((size, width), LOW) for size in out_sizes] * 2,
            [half_spec, half_spec, pl.BlockSpec((8, half), lambda f, a: (0, f))]
            + row_specs(out_sizes) * 2,
            [pltpu.VMEM((m, width), LOW)] * 2
            + [pltpu.VMEM((m, width), FULL)] * 2
            + [
                pltpu.VMEM((2, half, width), LOW),
                pltpu.VMEM((2, width, half), LOW),
                pltpu.SemaphoreType.DMA((4,)),
            ],
            8 * m * width * units,
            4 * width * units + 12 * m * width,
            m * units,
            after=tuple(acts[-1:]),
        )
        if len(acts) == 0:
            res, moved = meet(res, second[1:])
            second = gather_far([second[0], *moved])
            g_pieces = gather_far(g_pieces, *moved)
        elif len(acts) == 1 and teams == 4:
            res, moved = meet(res, (*second[3:], *g_pieces[3:]))
            second, g_pieces = [*second[:3], *moved[:2]], [*g_pieces[:3], *moved[2:]]
            early = reduce_early([None, *res[3 : 3 + n]])
        elif teams == 4:
            res, early = meet(res, early)
        acts.append(res[0])
        d_pres.append(res[1])
        e_sums.append(res[2])
        d_second += res[3 : 3 + n]
        out += res[3 + n :]

    sizes = [v.shape[0] for v in acts]
    def feed_grad(name, parts, units_of, turned, after):
        shape = (width, half) if turned else (half, width)
        return call(
            functools.partial(feed_grad_kernel, x_sizes, sizes, turned),
            name,
            (2,),
            at,
            (*parts, *units_of),
            [pl.BlockSpec(memory_space=pl.ANY)] * len(x_sizes)
            + [pl.BlockSpec((s, half), lambda f, a: (0, 1 - f)) for s in sizes],
            [(shape, LOW)] * 2,
            [fixed(shape)] * 2,
            [
                pltpu.VMEM((length, width), LOW),
                pltpu.VMEM((length, half), LOW),
                pltpu.SemaphoreType.DMA((len(x_sizes),)),
            ],
            2 * length * width * units,
            2 * act_bytes + 2 * width * units,
            after=after,
        )

    if teams != 4:
        early = reduce_early(d_second)
    far = reduce_far(d_second)
    sm, sg = feed_grad("shrink_grad", g_pieces, acts, True, ())
    (sm, sg), far = meet((sm, sg), far)
    late, folded = reduce_late(d_second, far)
    s_got = hop(sg, 1)
    out_early = reduce_early([tie(v, *folded[:1]) for v in out])
    em, eg = feed_grad("expand_grad", second, d_pres, False, (sm, *folded))
    (em, eg), (s_got, *late) = meet((em, eg), (s_got, *late))
    d_second = reduce_terms(d_second, early, late)
    s_sum = add_low(sm, s_got)
    e_got = hop(eg, 1)
    g_shrink = scatter(s_sum.reshape(dp_n, cols, half))

    terms = len(d_second)
    window = ((own_rows, span), LOW)
    d_hidden, d_branch, second_sums, *d_attended = simple(
        second_back_kernel,
        "second_back",
        (*d_second, hidden, g_own, merge, vec),
        [wide, wide_low, ((8, width), FULL)] + [window] * teams,
        [wide, wide_low],
        2 * own_rows * width * span * teams,
        after=(s_sum,),
        count=teams,
        rows=rows,
        span=span,
        dim=dim,
        terms=terms,
    )
    d_attended = exchange(d_attended)

    step = min(span, CHUNK)
    feat_block = ((teams, feats, width), LOW)
    mine, give = simple(
        merge_grad_kernel,
        "merge_grad",
        (*attended, d_branch),
        [feat_block, feat_block],
        [(merge_shape, FULL), ((teams * (span // step), own_rows, step), LOW)],
        2 * own_rows * width * span * teams,
        count=teams,
        span=span,
        share=share,
        dim=dim,
        step=step,
    )

    (mine, give), (e_got, *moved) = meet((mine, give), (e_got, *d_attended, *out_early))
    d_attended, out_early = moved[:teams], moved[teams:]
    e_sum = add_low(em, e_got)
    g_expand = scatter(e_sum.reshape(dp_n, hp, width))

    def core_parts(mine, got):
        return simple(
            add_parts_kernel,
            "add_parts",
            (mine, got),
            [(mine.shape[1:], LOW)] * teams,
        )

    g_merge = core_parts(mine, hop(give, 1))
    merge_near = exchange([tie(v, *d_attended) for v in g_merge])[1:]

    d_parts, wait = [], (e_sum, mixed, g_merge[0])
    for base, count in runs:
        (d_part,) = call(
            functools.partial(attend_backward_kernel, teams, own_rows, dim, heads, share, base),
            "attend_backward",
            (count,),
            at,
            (mixed, mixed, mixed, *d_attended, *segs, logs[len(d_parts)]),
            qkv_specs(base)
            + [pl.BlockSpec((own_rows, LANES), lambda p, a, base=base: (0, base + p))] * teams
            + seg_specs
            + [pl.BlockSpec((length, LANES), lambda p, a: (0, p))],
            [((3, length, part), LOW)],
            [pl.BlockSpec((3, length, LANES), lambda p, a: (0, 0, p))],
            [
                pltpu.VMEM((length, dim), FULL),
                pltpu.VMEM((length, dim), FULL),
                pltpu.VMEM((length, LANES), LOW),
                pltpu.VMEM((LANES, length), FULL),
            ],
            5 * length * length * dim * heads,
            8 * length * part * 2,
            length * length * heads // 4,
            after=wait,
        )
        if base == 0:
            (d_part,), merge_near = meet((d_part,), merge_near)
            out_far = reduce_far([*out[:5], *[tie(v, d_part) for v in out[5:]]])
            wait = (d_part,)
        else:
            (d_part,), out_far = meet((d_part,), out_far)
            out_late, folded = reduce_late(out, out_far)
        d_parts.append(d_part)

    mix_block = ((teams, feats, 3 * span), LOW)
    mine, give, mix_sums = call(
        mix_grad_kernel,
        "mix_grad",
        (3,),
        at,
        (*d_parts, first_t),
        [pl.BlockSpec((1, length, part), lambda c, a: (c, 0, 0))] * 2 + [fixed((width, length))],
        [mix_block, mix_block, ((8, 3 * span), FULL)],
        [pl.BlockSpec((teams, feats, span), lambda c, a: (0, 0, c))] * 2
        + [pl.BlockSpec((8, span), lambda c, a: (0, c))],
        [pltpu.VMEM((width, span), FULL), pltpu.VMEM((length, span), LOW)],
        2 * length * width * 3 * span,
        3 * act_bytes,
        after=tuple(folded[:1]),
    )
    mix_sums = mix_sums[0].reshape(3, span)
    (mine, give), out_late = meet((mine, give), out_late)
    mix_got = hop(give, 1)
    feed_cuts = simple(
        split_feed_kernel,
        "split_feed",
        (g_expand, g_shrink),
        [feed_cut] * teams,
        teams=teams,
        after=(give,),
        hp=hp,
    )
    out = reduce_terms(out, out_early, out_late)
    block_out = simple(
        block_out_kernel,
        "block_out",
        (*out, hidden, vec),
        [piece, piece],
        after=(give,),
        rows=rows,
        terms=terms,
    )
    g_merge = [g_merge[0], *merge_near]
    g_merge = functools.reduce(jnp.add, [v.astype(FULL) for v in g_merge]).astype(LOW)
    merge_each = width // dp_n
    g_merge = jnp.stack(
        [g_merge[:, d * merge_each : (d + 1) * merge_each] for d in range(dp_n)]
    )
    grad_merge = scatter(g_merge).astype(FULL)

    groups = [([3, 4], 3), ([1, 2], 1), ([0], 0)] if teams == 4 else [([k], k) for k in range(teams)]
    kept, (mix_got,) = meet((*block_out, *feed_cuts), (mix_got,))
    block_out, feed_cuts = kept[:2], kept[2:]
    g_mix = core_parts(mine, mix_got)
    d_first, first_sums, wait = [], [], (g_mix[0], g_merge)
    feed_cuts, g_mix = exchange(feed_cuts), exchange(g_mix)
    block_out = swap_out(*block_out)
    far = early = ()
    for group, low in groups:
        sizes = [x_sizes[i] for i in group]
        out_sizes = sizes if len(sizes) == 1 else [rows] * (sum(sizes) // rows)
        n = sum(sizes) // own_rows
        sums, *got = call(
            functools.partial(first_back_kernel, sizes, out_sizes, rows, span),
            "first_back",
            (n,),
            at,
            (*d_parts, *[x_pieces[i] for i in group], mix),
            [
                pl.BlockSpec(
                    (3, own_rows, part), lambda i, a, low=low: (0, (i + low) ^ (a[0] // 2), 0)
                )
            ]
            * 2
            + row_specs(sizes)
            + [fixed((width, 3 * span))],
            [((8, width), FULL)] + [((size, width), LOW) for size in out_sizes],
            [vec_spec] + row_specs(out_sizes),
            [
                pltpu.VMEM((own_rows, width), LOW),
                pltpu.VMEM((own_rows, width), LOW),
                pltpu.VMEM((own_rows, 3 * span), LOW),
            ],
            2 * n * own_rows * width * 3 * span,
            n * own_rows * width * 8,
            after=wait,
        )
        first_sums.append(sums)
        if not d_first:
            got, moved = meet(got, feed_cuts[1:])
            feed_cuts = [feed_cuts[0], *moved]
            wait = (sums,)
            far = reduce_far([None] * 5 + list(got))
        elif len(first_sums) == 2:
            got, moved = meet(got, g_mix[1:])
            g_mix = [g_mix[0], *moved]
            wait = (sums,)
            if teams == 4:
                early = reduce_early([None, *got])
        else:
            got, far = meet(got, far)
        d_first.append(got)
    (g_mix,) = simple(
        join_mix_kernel,
        "join_mix",
        g_mix,
        [((dp_n, feats, each), LOW)],
        [((teams, feats, 3 * span), LOW), ((feats, 3 * width), LOW)],
        teams=teams,
        dp_n=dp_n,
        each=each,
        span=span,
        starts=starts,
        width=width,
    )
    grad_mix = scatter(g_mix).astype(FULL)
    first_sums = functools.reduce(jnp.add, first_sums)
    if teams == 4:
        d_first = [*d_first[2], *d_first[1], *d_first[0]]
    else:
        d_first = [v for got in d_first for v in got]
        early = reduce_early(d_first)
    ek, eg, sk, sg = simple(
        part_feed_kernel,
        "part_feed",
        feed_cuts,
        [(e_shape, LOW), (e_shape, LOW), (s_shape, LOW), (s_shape, LOW)],
        [((teams, 2, hr, cols), LOW)],
        teams=teams,
    )
    late, folded = reduce_late(d_first, far, (g_mix, ek))
    def spread(v):
        return lax.dynamic_update_slice_in_dim(
            jnp.zeros((width + 2 * LANES,), FULL), v, start, 0
        )[:width]

    d_e = functools.reduce(jnp.add, [s[0] for s in e_sums]).reshape(2, dp_n, hp)[:, :, :hr]
    d_e = jnp.where(core == 0, d_e, d_e[::-1]).transpose(1, 0, 2)
    d_e = lax.dynamic_update_slice_in_dim(
        jnp.zeros((dp_n, teams, 2, hr), FULL), d_e[:, None], team, 1
    )
    partial = (
        first_sums[0],
        first_sums[1],
        spread(mix_sums[0]),
        spread(mix_sums[2]),
        second_sums[2],
        second_sums[0],
        second_sums[1],
        second_sums[3],
        d_e.reshape(-1),
    )
    partial = jnp.concatenate([v.reshape(seq_n, -1) for v in partial], axis=1)
    total = reduce_small(tie(partial, *folded[:1]))
    (ek, sk), (total, *early) = meet((ek, sk), (total, *early))
    d_first = reduce_terms(d_first, early, late)
    grad_expand, grad_shrink = simple(
        end_feed_kernel,
        "end_feed",
        (ek, hop(eg, 1), sk, hop(sg, 1)),
        [(expand_weight.shape, FULL), (shrink_weight.shape, FULL)],
        teams=teams,
        hr=hr,
    )

    piece_full = ((rows, width), FULL)
    input_grad = simple(
        input_grad_kernel,
        "input_grad",
        (*d_first, d_hidden, x_own, vec),
        [piece_full, piece_full],
        after=(grad_expand,),
        rows=rows,
        terms=terms,
    )
    input_grad = swap_out(*input_grad)

    ends = [total[i * feats : (i + 1) * feats] for i in range(8)]
    vectors = (*ends[:7], total[8 * feats :], ends[7])
    return (block_out, input_grad, grad_mix, grad_merge, grad_expand, grad_shrink, *vectors)


def solution(mesh):
    rows = P("dp", "seq", None)
    matrix = P("seq", "dp")
    vector = P("seq")
    return jax.shard_map(
        functools.partial(body, mesh.shape["seq"], mesh.shape["dp"]),
        mesh=mesh,
        in_specs=(rows, P("dp", None), rows) + (matrix,) * 4 + (vector,) * 9,
        out_specs=(rows, rows) + (matrix,) * 4 + (vector,) * 9,
        check_vma=False,
    )
```

```python
import functools

import jax
import jax.numpy as jnp
from jax import lax
from jax.experimental import pallas as pl
from jax.experimental.pallas import tpu as pltpu
from jax.sharding import PartitionSpec as P

HEADS = 25
COST = 0.12
LANES = 128
CHUNK = 256
QUERY_ROWS = 384
KEY_ROWS = 384
LOW = jnp.bfloat16
FULL = jnp.float32
VMEM_BYTES = 60 * 1024 * 1024


def dot_nn(left, right):
    return lax.dot_general(left, right, (((1,), (0,)), ((), ())), preferred_element_type=FULL)


def dot_tn(left, right):
    return lax.dot_general(left, right, (((0,), (0,)), ((), ())), preferred_element_type=FULL)


def dot_nt(left, right):
    return lax.dot_general(left, right, (((1,), (1,)), ((), ())), preferred_element_type=FULL)


def norm_parts(v):
    center = v - jnp.mean(v, axis=-1, keepdims=True)
    spread = jnp.mean(center * center, axis=-1, keepdims=True)
    inverse = lax.rsqrt(spread + 1e-05)
    return center * inverse, inverse


def norm_back(grad, gain, normal, inverse):
    e = grad * gain
    mean_e = jnp.mean(e, axis=-1, keepdims=True)
    mean_en = jnp.mean(e * normal, axis=-1, keepdims=True)
    return inverse * (e - mean_e - normal * mean_en)


def total_rows(v):
    return jnp.sum(v, axis=0, keepdims=True)


def fixed(shape):
    return pl.BlockSpec(shape, lambda *_: (0,) * len(shape), pipeline_mode=pl.Buffered(1))


def call(
    kernel, name, grid, at, operands, in_specs, outs, out_specs, scratch, flops, nbytes, exps=0, after=()
):
    if after:
        count, inner = len(operands), kernel
        kernel = lambda at_ref, *refs: inner(at_ref, *refs[:count], *refs[count + len(after) :])
        operands = (*operands, *after)
        in_specs = list(in_specs) + [pl.BlockSpec(memory_space=pl.ANY)] * len(after)
    spec = pltpu.PrefetchScalarGridSpec(
        num_scalar_prefetch=1,
        grid=grid,
        in_specs=in_specs,
        out_specs=out_specs,
        scratch_shapes=scratch,
    )
    return pl.pallas_call(
        kernel,
        grid_spec=spec,
        out_shape=[jax.ShapeDtypeStruct(s, d) for s, d in outs],
        compiler_params=pltpu.CompilerParams(vmem_limit_bytes=VMEM_BYTES),
        cost_estimate=pl.CostEstimate(
            flops=int(COST * flops),
            bytes_accessed=int(COST * nbytes),
            transcendentals=int(COST * exps),
        ),
        name=name,
    )(at, *operands)


def row_slot(half, core, rows):
    slot = core if half == 0 else 1 - core
    return pl.ds(pl.multiple_of(slot * rows, rows), rows)


def load_pair(step, sizes, refs, buf, core, rows):
    low = 0
    for size, ref in zip(sizes, refs):
        for i in range(size // rows):
            r = low // rows + i

            @pl.when(step == r // 2)
            def _():
                buf[row_slot(r % 2, core, rows), :] = ref[i * rows : (i + 1) * rows, :]

        low += size


def half_sum(refs, half, rows):
    parts = []
    for i, ref in enumerate(refs):
        if ref.shape[0] > rows:
            parts.append(ref[half * rows : (half + 1) * rows, :])
        elif (i + 1) % 2 == half:
            parts.append(ref[...])
    return functools.reduce(jnp.add, [v.astype(FULL) for v in parts])


def pair_rows(refs, core, rows, buf):
    for half in range(2):
        buf[row_slot(half, core, rows), :] = half_sum(refs, half, rows).astype(buf.dtype)


def fold_kernel(at_ref, x_ref, y_ref, far0_ref, far1_ref, xo_ref, yo_ref):
    xo_ref[...] = (x_ref[...].astype(FULL) + far1_ref[...].astype(FULL)).astype(LOW)
    yo_ref[...] = (y_ref[...].astype(FULL) + far0_ref[...].astype(FULL)).astype(LOW)


def place_rows(place, refs, wide, out):
    each = refs[0].shape[0]
    if len(refs) == 1:
        out[...] = refs[0][...]
        return
    for r, ref in enumerate(refs):
        begin = pl.multiple_of((place ^ r) * each, each)
        wide[pl.ds(begin, each), :] = ref[...].astype(FULL)
    filled = each * len(refs)
    if filled < wide.shape[0]:
        wide[filled:, :] = jnp.zeros((wide.shape[0] - filled, wide.shape[1]), FULL)
    block = 16
    for size in range(16, 129, 16):
        block = size if out.shape[0] % size == 0 else block

    def narrow(i, carry):
        span = pl.ds(pl.multiple_of(i * block, block), block)
        out[span, :] = wide[span, :].astype(LOW)
        return carry

    lax.fori_loop(0, out.shape[0] // block, narrow, 0)


def flip(v):
    rows, cols = v.shape
    v = jnp.pad(v.astype(FULL), ((0, -rows % LANES), (0, -cols % LANES)))
    return v.T[:cols, :rows]


def cut_feed_kernel(at_ref, e_ref, s_ref, ek_ref, eg_ref, sk_ref, sg_ref, *, teams, hr):
    first = at_ref[0] % 2 == 0
    cols = s_ref.shape[1]
    e, s = e_ref[...].astype(FULL), s_ref[...].astype(FULL)
    for t in range(teams):
        a, b = e[:, 2 * t * hr : (2 * t + 1) * hr], e[:, (2 * t + 1) * hr : (2 * t + 2) * hr]
        ek_ref[:, t * hr : (t + 1) * hr] = jnp.where(first, a, b).astype(LOW)
        eg_ref[:, t * hr : (t + 1) * hr] = jnp.where(first, b, a).astype(LOW)
    for t in range(teams // 2):
        a, b = s[2 * t * hr : (2 * t + 1) * hr], s[(2 * t + 1) * hr : (2 * t + 2) * hr]
        sk_ref[:, t * cols : (t + 1) * cols] = jnp.where(first, a, b).astype(LOW)
        sg_ref[:, t * cols : (t + 1) * cols] = jnp.where(first, b, a).astype(LOW)


def join_feed_kernel(at_ref, ek_ref, eo_ref, sk_ref, so_ref, *out_refs, teams, hr):
    first, team = at_ref[0] % 2 == 0, at_ref[0] // 2
    feats = ek_ref.shape[0]
    cols = 2 * feats
    mine, other = flip(ek_ref[...]), flip(eo_ref[...])
    low = jnp.where(first, mine, other).astype(LOW)
    high = jnp.where(first, other, mine).astype(LOW)
    for t in range(teams):
        part = slice((t % (teams // 2)) * cols, (t % (teams // 2) + 1) * cols)
        here = first if t < teams // 2 else jnp.logical_not(first)
        piece = jnp.where(here, sk_ref[:, part], so_ref[:, part])
        for k, ref in enumerate(out_refs):

            @pl.when((team ^ t) == k)
            def _():
                ref[0, :, :feats] = low[t * hr : (t + 1) * hr, :]
                ref[0, :, feats:] = high[t * hr : (t + 1) * hr, :]
                ref[1] = piece


def lay_feed_kernel(at_ref, *refs, teams, hp):
    part_refs, e_ref, s_ref, whole = refs[:teams], *refs[teams:]
    team = at_ref[0] // 2
    for k, ref in enumerate(part_refs):
        whole[team ^ k] = ref[...]
    hr, cols = whole.shape[2:]
    e_ref[hr:, :] = jnp.zeros((hp - hr, e_ref.shape[1]), LOW)
    s_ref[...] = jnp.zeros_like(s_ref)
    for t in range(teams):
        e_ref[:hr, t * cols : (t + 1) * cols] = whole[t, 0]
        s_ref[:, t * hp : t * hp + hr] = flip(whole[t, 1]).astype(LOW)


def split_feed_kernel(at_ref, e_ref, s_ref, *out_refs, teams, hp):
    team = at_ref[0] // 2
    hr, cols = out_refs[0].shape[1:]
    for t in range(teams):
        piece = flip(s_ref[:, t * hp : t * hp + hr]).astype(LOW)
        for k, ref in enumerate(out_refs):

            @pl.when((team ^ t) == k)
            def _():
                ref[0] = e_ref[:hr, t * cols : (t + 1) * cols]
                ref[1] = piece


def part_feed_kernel(at_ref, *refs, teams):
    part_refs, ek_ref, eg_ref, sk_ref, sg_ref, whole = refs[:teams], *refs[teams:]
    first, team = at_ref[0] % 2 == 0, at_ref[0] // 2
    for k, ref in enumerate(part_refs):
        whole[team ^ k] = ref[...]
    hr, cols = whole.shape[2:]
    feats = cols // 2
    for t in range(teams):
        e = flip(whole[t, 0])
        a, b = e[:feats, :], e[feats:, :]
        ek_ref[:, t * hr : (t + 1) * hr] = jnp.where(first, a, b).astype(LOW)
        eg_ref[:, t * hr : (t + 1) * hr] = jnp.where(first, b, a).astype(LOW)
    for t in range(teams // 2):
        a, b = whole[t, 1], whole[teams // 2 + t, 1]
        sk_ref[:, t * cols : (t + 1) * cols] = jnp.where(first, a, b)
        sg_ref[:, t * cols : (t + 1) * cols] = jnp.where(first, b, a)


def end_feed_kernel(at_ref, ek_ref, eo_ref, sk_ref, so_ref, e_ref, s_ref, *, teams, hr):
    first = at_ref[0] % 2 == 0
    cols = s_ref.shape[1]
    mine, other = ek_ref[...].astype(FULL), eo_ref[...].astype(FULL)
    low, high = jnp.where(first, mine, other), jnp.where(first, other, mine)
    for t in range(teams):
        e_ref[:, 2 * t * hr : (2 * t + 1) * hr] = low[:, t * hr : (t + 1) * hr]
        e_ref[:, (2 * t + 1) * hr : (2 * t + 2) * hr] = high[:, t * hr : (t + 1) * hr]
    mine, other = sk_ref[...].astype(FULL), so_ref[...].astype(FULL)
    low, high = jnp.where(first, mine, other), jnp.where(first, other, mine)
    for t in range(teams // 2):
        s_ref[2 * t * hr : (2 * t + 1) * hr, :] = low[:, t * cols : (t + 1) * cols]
        s_ref[(2 * t + 1) * hr : (2 * t + 2) * hr, :] = high[:, t * cols : (t + 1) * cols]


def cut_mix_kernel(at_ref, rows_ref, *refs, teams, dp_n, each, span, starts, width):
    out_refs, merge_ref, full = refs[:teams], refs[teams], refs[teams + 1]
    team = at_ref[0] // 2
    part = width // dp_n
    for d in range(dp_n):
        full[:, d * each : (d + 1) * each] = rows_ref[d, :, :each]
        merge_ref[:, d * part : (d + 1) * part] = rows_ref[d, :, each:]
    full[:, dp_n * each :] = jnp.zeros((full.shape[0], full.shape[1] - dp_n * each), LOW)
    for t in range(teams):
        for k, ref in enumerate(out_refs):

            @pl.when((team ^ t) == k)
            def _():
                for m in range(3):
                    begin = m * width + starts[t]
                    ref[:, m * span : (m + 1) * span] = full[:, begin : begin + span]


def join_mix_kernel(at_ref, *refs, teams, dp_n, each, span, starts, width):
    part_refs, out_ref, whole, flat = refs[:teams], *refs[teams:]
    team = at_ref[0] // 2
    share = width // teams
    for k, ref in enumerate(part_refs):
        whole[team ^ k] = ref[...]
    for m in range(3):
        for t in range(teams):
            low = m * span + share * t - starts[t]
            begin = m * width + share * t
            flat[:, begin : begin + share] = whole[t, :, low : low + share]
    for d in range(dp_n):
        out_ref[d] = flat[:, d * each : (d + 1) * each]


def add_parts_kernel(at_ref, mine_ref, got_ref, *out_refs):
    team = at_ref[0] // 2
    for k, ref in enumerate(out_refs):
        total = mine_ref[team ^ k].astype(FULL) + got_ref[team ^ k].astype(FULL)
        ref[...] = total.astype(LOW)


def norm_kernel(sizes, rows, at_ref, *refs):
    count = len(sizes)
    vec_ref, first_ref, turned_ref, buf = refs[count:]
    load_pair(pl.program_id(0), sizes, refs[:count], buf, at_ref[0] % 2, rows)
    normal, _ = norm_parts(buf[...].astype(FULL))
    first = (normal * vec_ref[0:1, :] + vec_ref[1:2, :]).astype(LOW)
    first_ref[...] = first
    turned_ref[...] = first.T


def mix_kernel(parts, at_ref, *refs):
    first_ref, bias_ref, mixed_ref, mix_ref, wide = refs[parts:]

    @pl.when(pl.program_id(0) == 0)
    def _():
        place_rows(at_ref[0], refs[:parts], wide, mix_ref)

    mixed = dot_nn(first_ref[...], mix_ref[...]) + bias_ref[0:1, :]
    mixed_ref[...] = (mixed * bias_ref[1:2, :]).astype(LOW)


def causal_chunks(length, begin):
    stop = begin + QUERY_ROWS
    return [(low, min(low + KEY_ROWS, stop)) for low in range(0, stop, KEY_ROWS)]


def visible_scores(query, key, begin, low, col_ref, row_ref):
    scores = dot_nt(query, key)
    rows, cols = scores.shape
    seen = col_ref[begin : begin + rows, :] == row_ref[:, low : low + cols]
    if low + cols > begin:
        row_id = lax.broadcasted_iota(jnp.int32, (rows, cols), 0) + begin
        col_id = lax.broadcasted_iota(jnp.int32, (rows, cols), 1) + low
        seen = seen & (col_id <= row_id)
    return jnp.where(seen, scores, -1e30)


def attend_forward_kernel(count, block, dim, heads, base, at_ref, *refs):
    q_ref, k_ref, v_ref, col_ref, row_ref = refs[:5]
    out_refs, log_ref = refs[5:-1], refs[-1]
    pair = pl.program_id(0) + base
    team = at_ref[0] // 2
    for ref in out_refs:
        ref[...] = jnp.zeros_like(ref)
    for sub in range(LANES // dim):

        @pl.when(pair * (LANES // dim) + sub < heads)
        def _():
            lanes = slice(sub * dim, (sub + 1) * dim)
            for begin in range(0, count * block, QUERY_ROWS):
                rows = slice(begin, begin + QUERY_ROWS)
                query = q_ref[rows, lanes]
                chunks = causal_chunks(count * block, begin)
                scores = [
                    visible_scores(
                        query, k_ref[low:high, lanes], begin, low, col_ref, row_ref
                    )
                    for low, high in chunks
                ]
                top = functools.reduce(
                    jnp.maximum, [jnp.max(p, axis=1, keepdims=True) for p in scores]
                )
                expo = [jnp.exp(p - top) for p in scores]
                total = functools.reduce(
                    jnp.add, [jnp.sum(p, axis=1, keepdims=True) for p in expo]
                )
                mixed = functools.reduce(
                    jnp.add,
                    [
                        dot_nn(e.astype(LOW), v_ref[low:high, lanes])
                        for e, (low, high) in zip(expo, chunks)
                    ],
                )
                mixed = (mixed / total).astype(LOW)
                log_ref[rows, lanes] = jnp.broadcast_to(top + jnp.log(total), (QUERY_ROWS, dim))
                place = slice(begin % block, begin % block + QUERY_ROWS)
                for k, ref in enumerate(out_refs):

                    @pl.when((team ^ (begin // block)) == k)
                    def _():
                        ref[place, lanes] = mixed


def attend_backward_kernel(count, block, dim, heads, share, base, at_ref, *refs):
    q_ref, k_ref, v_ref, *g_refs = refs[: 3 + count]
    col_ref, row_ref, log_ref, d_ref, acc_k, acc_v, grads, logs = refs[3 + count :]
    pair = pl.program_id(0) + base
    team = at_ref[0] // 2
    scale = dim**-0.5
    d_ref[...] = jnp.zeros_like(d_ref)
    logs[...] = log_ref[...].T
    for k, ref in enumerate(g_refs):
        grads[pl.ds(pl.multiple_of((team ^ k) * block, block), block), :] = ref[...]
    for sub in range(LANES // dim):

        @pl.when(pair * (LANES // dim) + sub < heads)
        def _():
            lanes = slice(sub * dim, (sub + 1) * dim)
            column = lax.broadcasted_iota(jnp.int32, (1, dim), 1)
            column = column + at_ref[1 + team] + pair * LANES + sub * dim
            owned = (column >= share * team) & (column < share * (team + 1))
            owned = jnp.where(owned, 1.0, 0.0)
            acc_k[...] = jnp.zeros_like(acc_k)
            acc_v[...] = jnp.zeros_like(acc_v)
            for begin in range(0, count * block, QUERY_ROWS):
                rows = slice(begin, begin + QUERY_ROWS)
                query = q_ref[rows, lanes]
                grad = grads[rows, lanes]
                log_total = logs[sub * dim : sub * dim + 1, rows]
                chunks = causal_chunks(count * block, begin)
                probs, d_weights = [], []
                for low, high in chunks:
                    scores = dot_nt(k_ref[low:high, lanes], query)
                    seen = col_ref[low:high, :] == row_ref[:, rows]
                    if high > begin:
                        key_id = lax.broadcasted_iota(jnp.int32, scores.shape, 0) + low
                        query_id = lax.broadcasted_iota(jnp.int32, scores.shape, 1) + begin
                        seen = seen & (key_id <= query_id)
                    probs.append(jnp.exp(jnp.where(seen, scores, -1e30) - log_total))
                    d_weights.append(dot_nt(v_ref[low:high, lanes], grad))
                delta = functools.reduce(
                    jnp.add, [total_rows(p * d) for p, d in zip(probs, d_weights)]
                )
                d_query = jnp.zeros((QUERY_ROWS, dim), FULL)
                for prob, d_weight, (low, high) in zip(probs, d_weights, chunks):
                    d_scores = (prob * (d_weight - delta)).astype(LOW)
                    d_query = d_query + dot_tn(d_scores, k_ref[low:high, lanes])
                    acc_k[low:high, :] += dot_nn(d_scores, query)
                    acc_v[low:high, :] += dot_nn(prob.astype(LOW), grad)
                d_ref[0, rows, lanes] = (d_query * scale * owned).astype(LOW)
            d_ref[1, :, lanes] = (acc_k[...] * owned).astype(LOW)
            d_ref[2, :, lanes] = (acc_v[...] * owned).astype(LOW)


def merge_norm_kernel(at_ref, *refs, count, rows, span, share, dim, parts):
    att_refs, part_refs = refs[: 2 * count], refs[2 * count : 2 * count + parts]
    x_ref, vec_ref, hid_ref, s0_ref, s1_ref, merge_ref, xs, buf, wide = refs[2 * count + parts :]
    core, team = at_ref[0] % 2, at_ref[0] // 2
    place_rows(at_ref[0], part_refs, wide, merge_ref)
    pair_rows([x_ref], core, rows, xs)
    hidden = xs[...].astype(FULL) + vec_ref[4:5, :]
    lane = lax.broadcasted_iota(jnp.int32, (1, span), 1)
    for k in range(count):
        other = team ^ k
        start = at_ref[1 + other]
        low = share * other - start
        owned = (lane >= low) & (lane < low + share)
        piece = jnp.concatenate([att_refs[k][...], att_refs[count + k][...]], axis=1)
        piece = jnp.where(owned, piece, jnp.zeros((), LOW))
        hidden = hidden + dot_nn(piece, merge_ref[pl.ds(pl.multiple_of(start, dim), span), :])
    hid_ref[...] = hidden
    normal, _ = norm_parts(hidden)
    buf[...] = (normal * vec_ref[5:6, :] + vec_ref[6:7, :]).astype(LOW)
    s0_ref[...] = buf[row_slot(0, core, rows), :]
    s1_ref[...] = buf[row_slot(1, core, rows), :]


def feed_kernel(rows, sizes, out_sizes, at_ref, *refs):
    pieces, count = len(sizes), len(out_sizes)
    lows = [sum(sizes[:i]) for i in range(pieces)]
    halves = sum(sizes) // rows
    sec_refs, g_refs, refs = refs[:halves], refs[halves : halves + pieces], refs[halves + pieces :]
    weights, (bias_ref, act_ref, dpre_ref, sum_ref), rest = refs[:4], refs[4:8], refs[8:]
    ds_refs, out_refs = rest[:count], rest[count : 2 * count]
    sec, g, acc_s, acc_o, e_held, s_held, sems = rest[2 * count :]
    step = pl.program_id(0)
    copies = [
        pltpu.make_async_copy(ref, held.at[i // 2], sems.at[i])
        for i, (ref, held) in enumerate(zip(weights, (e_held, s_held) * 2))
    ]

    @pl.when(step == 0)
    def _():
        for copy in copies:
            copy.start()
        for i in range(halves):
            sec[i * rows : (i + 1) * rows, :] = sec_refs[i][...]
        for i in range(pieces):
            g[lows[i] : lows[i] + sizes[i], :] = g_refs[i][...]
        copies[0].wait()
        copies[1].wait()

    @pl.when(step == 1)
    def _():
        copies[2].wait()
        copies[3].wait()

    et, st = e_held[step], s_held[step]
    u = dot_nt(sec[...], et) + bias_ref[...]
    d_act = dot_nn(g[...], st)
    square = u * u
    tanh = jnp.tanh(0.7978845608028654 * u * (1.0 + 0.044715 * square))
    plus = 0.5 * (1.0 + tanh)
    act = (u * plus).astype(LOW)
    slope = plus + u * (0.5 * 0.7978845608028654) * (1.0 - tanh * tanh) * (
        1.0 + 3 * 0.044715 * square
    )
    d_pre = (d_act * slope).astype(LOW)
    act_ref[...] = act
    dpre_ref[...] = d_pre
    sum_ref[...] = jnp.broadcast_to(total_rows(d_pre.astype(FULL)), sum_ref.shape)
    part_s = dot_nn(d_pre, et)
    part_o = dot_nt(act, st)

    @pl.when(step == 0)
    def _():
        acc_s[...] = part_s
        acc_o[...] = part_o

    @pl.when(step == 1)
    def _():
        for i in range(count):
            here = slice(sum(out_sizes[:i]), sum(out_sizes[: i + 1]))
            ds_refs[i][...] = (acc_s[here, :] + part_s[here, :]).astype(LOW)
            out_refs[i][...] = (acc_o[here, :] + part_o[here, :]).astype(LOW)


def feed_grad_kernel(pieces, sizes, turned, at_ref, *refs):
    count = len(pieces)
    piece_refs, unit_refs = refs[:count], refs[count : count + len(sizes)]
    mine_ref, give_ref, held, units, sems = refs[count + len(sizes) :]
    step = pl.program_id(0)
    copies = [
        pltpu.make_async_copy(
            ref, held.at[sum(pieces[:i]) : sum(pieces[: i + 1]), :], sems.at[i]
        )
        for i, ref in enumerate(piece_refs)
    ]

    @pl.when(step == 0)
    def _():
        for copy in copies:
            copy.start()
        for copy in copies:
            copy.wait()

    low = 0
    for size, ref in zip(sizes, unit_refs):
        units[low : low + size, :] = ref[...]
        low += size
    if turned:
        grad = dot_tn(held[...], units[...]).astype(LOW)
    else:
        grad = dot_tn(units[...], held[...]).astype(LOW)

    @pl.when(step == 0)
    def _():
        give_ref[...] = grad

    @pl.when(step == 1)
    def _():
        mine_ref[...] = grad


def second_back_kernel(at_ref, *refs, count, rows, span, dim, terms):
    rest = refs[terms:]
    hid_ref, g_ref, merge_ref, vec_ref = rest[:4]
    dh_ref, db_ref, sum_ref = rest[4:7]
    att_refs = rest[7 : 7 + count]
    ds, g = rest[7 + count :]
    core, team = at_ref[0] % 2, at_ref[0] // 2
    pair_rows(refs[:terms], core, rows, ds)
    pair_rows([g_ref], core, rows, g)
    normal, inverse = norm_parts(hid_ref[...])
    d_second = ds[...]
    g_full = g[...].astype(FULL)
    d_hidden = g_full + norm_back(d_second, vec_ref[5:6, :], normal, inverse)
    dh_ref[...] = d_hidden
    d_branch = d_hidden.astype(LOW)
    db_ref[...] = d_branch
    sum_ref[0:1, :] = total_rows(d_second * normal)
    sum_ref[1:2, :] = total_rows(d_second)
    sum_ref[2:3, :] = total_rows(d_branch.astype(FULL))
    sum_ref[3:4, :] = total_rows(g_full)
    sum_ref[4:8, :] = jnp.zeros((4, sum_ref.shape[1]), FULL)
    for k, ref in enumerate(att_refs):
        start = pl.multiple_of(at_ref[1 + (team ^ k)], dim)
        ref[...] = dot_nt(d_branch, merge_ref[pl.ds(start, span), :]).astype(LOW)


def split_cores(core, value, mine_ref, give_ref):
    feats = mine_ref.shape[1]
    for t in range(mine_ref.shape[0]):
        low = value[2 * t * feats : (2 * t + 1) * feats, :]
        high = value[(2 * t + 1) * feats : (2 * t + 2) * feats, :]
        mine_ref[t] = jnp.where(core == 0, low, high).astype(LOW)
        give_ref[t] = jnp.where(core == 0, high, low).astype(LOW)


def merge_grad_kernel(at_ref, *refs, count, span, share, dim, step):
    att_refs = refs[: 2 * count]
    db_ref, mine_ref, give_ref, acc, held = refs[2 * count :]
    team = at_ref[0] // 2
    acc[...] = jnp.zeros_like(acc)
    lane = lax.broadcasted_iota(jnp.int32, (1, span), 1)
    for k in range(count):
        other = team ^ k
        low = share * other - at_ref[1 + other]
        owned = (lane >= low) & (lane < low + share)
        piece = jnp.concatenate([att_refs[k][...], att_refs[count + k][...]], axis=1)
        piece = jnp.where(owned, piece, jnp.zeros((), LOW))
        for c in range(span // step):
            held[k * (span // step) + c] = piece[:, c * step : (c + 1) * step]

    def add(i, carry):
        start = at_ref[1 + (team ^ (i // (span // step)))] + (i % (span // step)) * step
        acc[pl.ds(pl.multiple_of(start, dim), step), :] += dot_tn(held[i], db_ref[...])
        return carry

    lax.fori_loop(0, count * (span // step), add, 0)
    split_cores(at_ref[0] % 2, acc, mine_ref, give_ref)


def first_back_kernel(sizes, out_sizes, rows, span, at_ref, *refs):
    count, out_count = len(sizes), len(out_sizes)
    sides = 2
    d_refs, x_refs, refs = refs[:sides], refs[sides : sides + count], refs[sides + count :]
    mix_ref, sum_ref = refs[:2]
    out_refs = refs[2 : 2 + out_count]
    buf, low, joined = refs[2 + out_count :]
    step = pl.program_id(0)
    core = at_ref[0] % 2
    load_pair(step, sizes, x_refs, buf, core, rows)
    normal, _ = norm_parts(buf[...].astype(FULL))
    for m in range(3):
        for i, d_ref in enumerate(d_refs):
            n = span // sides
            begin = m * span + i * n
            joined[:, begin : begin + n] = d_ref[m]
    d_first = dot_nt(joined[...], mix_ref[...])

    @pl.when(step == 0)
    def _():
        sum_ref[...] = jnp.zeros_like(sum_ref)

    sum_ref[0:1, :] += total_rows(d_first * normal)
    sum_ref[1:2, :] += total_rows(d_first)
    low[...] = d_first.astype(LOW)
    begin = 0
    for size, ref in zip(out_sizes, out_refs):
        for i in range(size // rows):
            r = begin // rows + i

            @pl.when(step == r // 2)
            def _():
                ref[i * rows : (i + 1) * rows, :] = low[row_slot(r % 2, core, rows), :]

        begin += size


def mix_grad_kernel(at_ref, *refs):
    turned_ref, mine_ref, give_ref, sum_ref, held, d = refs[-6:]
    for i, ref in enumerate(refs[:-6]):
        n = ref.shape[2]
        d[:, i * n : (i + 1) * n] = ref[0]
    sum_ref[...] = jnp.broadcast_to(total_rows(d[...].astype(FULL)), sum_ref.shape)
    held[...] = dot_nn(turned_ref[...], d[...])
    split_cores(at_ref[0] % 2, held, mine_ref, give_ref)


def block_out_kernel(at_ref, *refs, rows, terms):
    hid_ref, vec_ref, o0_ref, o1_ref = refs[terms:]
    core = at_ref[0] % 2
    for half, ref in enumerate((o0_ref, o1_ref)):
        value = hid_ref[row_slot(half, core, rows), :] + vec_ref[7:8, :]
        ref[...] = (value + half_sum(refs[:terms], half, rows)).astype(LOW)


def input_grad_kernel(at_ref, *refs, rows, terms):
    dh_ref, x_ref, vec_ref, o0_ref, o1_ref = refs[terms:]
    core = at_ref[0] % 2
    for half, ref in enumerate((o0_ref, o1_ref)):
        d_first = half_sum(refs[:terms], half, rows)
        normal, inverse = norm_parts(x_ref[half * rows : (half + 1) * rows, :].astype(FULL))
        back = norm_back(d_first, vec_ref[0:1, :], normal, inverse)
        ref[...] = dh_ref[row_slot(half, core, rows), :] + back


def body(
    seq_n,
    dp_n,
    inputs,
    segments,
    cotangent,
    mix_weight,
    merge_weight,
    expand_weight,
    shrink_weight,
    first_gain,
    first_bias,
    query_bias,
    value_bias,
    merge_bias,
    second_gain,
    second_bias,
    expand_bias,
    shrink_bias,
):
    micro, rows, width = inputs.shape
    length = segments.shape[1]
    dim = width // HEADS
    teams = seq_n // 2
    bits = teams.bit_length() - 1
    pieces = seq_n
    own_rows = 2 * rows
    feats = width // seq_n
    share = width // teams
    begins = [share * t // dim for t in range(teams)]
    heads = max(-(-share * (t + 1) // dim) - begins[t] for t in range(teams))
    starts = [dim * min(h, HEADS - heads) for h in begins]
    span = -(-heads * dim // (2 * LANES)) * 2 * LANES
    part = span // 2
    hidden_units = expand_weight.shape[1] * dp_n
    hr = hidden_units // dp_n // teams // 2
    hp = hr
    while hp % 16 or dp_n * hp % LANES:
        hp += 1
    half = dp_n * hp
    units = 2 * half
    whole_rows = feats % 8 == 0

    place = lax.axis_index("seq")
    core = place % 2
    team = place // 2
    at = jnp.concatenate([place[None].astype(jnp.int32), jnp.asarray(starts, jnp.int32)])

    def hop(v, mask):
        shape = v.shape
        if len(shape) == 2 and shape[0] % LANES == 0 and shape[1] % LANES:
            v = v.reshape(2, shape[0] // 2, shape[1])
        return lax.ppermute(v, "seq", [(i, i ^ mask) for i in range(seq_n)]).reshape(shape)

    def pick(v, index):
        return lax.dynamic_index_in_dim(v, index, 0, keepdims=False)

    def along(v):
        return lax.all_gather(v, "dp", axis=0)

    def scatter(v):
        return lax.psum_scatter(v, "dp", scatter_dimension=0)

    def by_core(mine, other):
        return jnp.where(core == 0, jnp.stack([mine, other]), jnp.stack([other, mine]))

    def tie(v, *others):
        return lax.optimization_barrier((v, *others))[0]

    def meet(kept, moved):
        both = lax.optimization_barrier((*kept, *moved))
        return both[: len(kept)], both[len(kept) :]

    def own_pair(v, *others):
        mine = pick(v, core)
        return jnp.concatenate([mine, hop(tie(pick(v, 1 - core), *others), 1)], axis=0)

    def gather_near(own):
        if teams == 4:
            return [own, hop(own, 2), hop(own, 4)]
        return exchange([own] * teams)

    def gather_far(near, *others):
        if teams == 4:
            x, y = tie(near[1][:rows], *others), tie(near[2][rows:], *others)
            return [*near, hop(x, 4), hop(y, 2)]
        return near

    def add_low(a, b):
        return (a.astype(FULL) + b.astype(FULL)).astype(LOW)

    def reduce_early(p):
        return [hop(p[1], 2), hop(p[4], 4)] if teams == 4 else exchange(p)[1:]

    def reduce_far(p):
        return [hop(p[5], 2), hop(p[6], 4)] if teams == 4 else []

    def reduce_late(p, far, after=()):
        if teams != 4:
            return [], ()
        folded = simple(
            fold_kernel, "fold", (p[2], p[3], *far), [((rows, width), LOW)] * 2, after=after
        )
        return [hop(folded[0], 2), hop(folded[1], 4)], folded

    def reduce_terms(p, early, late):
        if teams == 4:
            return [p[0], early[0], late[0], late[1], early[1]]
        return [p[0], *early]

    def exchange(parts):
        return [parts[0]] + [hop(parts[k], 2 * k) for k in range(1, teams)]

    def assemble(parts, extra=0):
        out = jnp.zeros((seq_n + extra,) + parts[0].shape, parts[0].dtype)
        for r in range(pieces):
            out = lax.dynamic_update_index_in_dim(out, parts[r], place ^ r, 0)
        return out.reshape((-1,) + parts[0].shape[1:])

    def swap_out(out0, out1):
        return by_core(out0, hop(out1, 1))

    def gather_small(v):
        cur = v[None]
        for b in range(bits + 1):
            got = hop(cur, 1 << b)
            bit = (place >> b) & 1
            cur = jnp.where(
                bit == 0, jnp.concatenate([cur, got]), jnp.concatenate([got, cur])
            )
        return cur

    def reduce_small(v, *others):
        for b in reversed(range(bits + 1)):
            half_n = v.shape[0] // 2
            bit = (place >> b) & 1
            mine = jnp.where(bit == 0, v[:half_n], v[half_n:])
            give = jnp.where(bit == 0, v[half_n:], v[:half_n])
            v = mine + hop(give, 1 << b)
        v = tie(v[0], *others)
        for b in range(dp_n.bit_length() - 1):
            v = v + lax.ppermute(v, "dp", [(i, i ^ (1 << b)) for i in range(dp_n)])
        return v

    def simple(kernel, name, operands, outs, scratch=(), flops=0, nbytes=None, after=(), **named):
        if nbytes is None:
            nbytes = sum(v.size * v.dtype.itemsize for v in operands)
            nbytes += sum(4 * functools.reduce(lambda a, b: a * b, s) for s, _ in outs)
        return call(
            functools.partial(kernel, **named),
            name,
            (1,),
            at,
            operands,
            [fixed(v.shape) for v in operands],
            outs,
            [fixed(s) for s, _ in outs],
            [pltpu.VMEM(s, d) for s, d in scratch],
            flops,
            nbytes,
            after=after,
        )

    each = mix_weight.shape[1]
    mix_local = jnp.concatenate([mix_weight, merge_weight], axis=1)
    mix_rows = along(mix_local)
    small = (
        first_gain,
        first_bias,
        query_bias,
        value_bias,
        merge_bias,
        second_gain,
        second_bias,
        shrink_bias,
        expand_bias,
    )
    packed = gather_small(jnp.concatenate([v.reshape(-1, feats) for v in small], axis=0))
    x_own = own_pair(inputs)
    x_near = gather_near(tie(x_own, packed))

    cols = shrink_weight.shape[1]
    e_shape, s_shape = (feats, teams * hr), (hr, teams // 2 * cols)
    ek, eg, sk, sg = simple(
        cut_feed_kernel,
        "cut_feed",
        (expand_weight, shrink_weight),
        [(e_shape, LOW), (e_shape, LOW), (s_shape, LOW), (s_shape, LOW)],
        after=(mix_local,),
        teams=teams,
        hr=hr,
    )
    feed_cut = ((2, hr, cols), LOW)
    feed_cuts = simple(
        join_feed_kernel,
        "join_feed",
        (ek, hop(eg, 1), sk, hop(sg, 1)),
        [feed_cut] * teams,
        teams=teams,
        hr=hr,
    )
    feed_cuts, x_near = meet(exchange(feed_cuts), x_near)
    x_pieces = gather_far(x_near)
    vec = packed[:, :8].transpose(1, 0, 2)
    vec = vec.reshape(8, width).astype(FULL)
    e_bias = packed[:, 8:].reshape(-1).astype(FULL)
    mix_cut = ((feats, 3 * span), LOW)
    *cuts, merge_rows = simple(
        cut_mix_kernel,
        "cut_mix",
        (mix_rows,),
        [mix_cut] * teams + [((feats, width), LOW)],
        [((feats, 3 * width + LANES), LOW)],
        after=(*feed_cuts, vec),
        teams=teams,
        dp_n=dp_n,
        each=each,
        span=span,
        starts=starts,
        width=width,
    )
    e_cut, s_cut = simple(
        lay_feed_kernel,
        "lay_feed",
        feed_cuts,
        [((hp, width), LOW), ((cols, half), LOW)],
        [((teams, 2, hr, cols), LOW)],
        after=(cuts[0],),
        teams=teams,
        hp=hp,
    )

    expand_mine = along(e_cut).reshape(half, width)
    shrink_mine = along(tie(s_cut, expand_mine[0])).reshape(width, half)

    start = at[1 + team]

    def windowed(row):
        return lax.dynamic_slice_in_dim(jnp.pad(vec[row], (0, 2 * LANES)), start, span, 0)

    blank = jnp.zeros((span,), FULL)
    mix_bias = jnp.concatenate([windowed(2), blank, windowed(3)])
    shrinking = jnp.where(jnp.arange(3 * span) < span, dim**-0.5, 1.0).astype(FULL)
    mix_bias = jnp.concatenate([mix_bias[None], shrinking[None], jnp.zeros((6, 3 * span), FULL)])

    act_bytes = length * width * 2
    piece_spec = fixed((rows, width))
    vec_spec = fixed((8, width))
    mix_spec = fixed((width, 3 * span))
    team_rows = lambda n: pl.BlockSpec((own_rows, n), lambda k, a: (k ^ (a[0] // 2), 0))
    kept, moved = meet((*cuts, merge_rows), x_pieces[3:])
    cuts, merge_rows, x_pieces = kept[:-1], kept[-1], [*x_near, *moved]
    x_sizes = [v.shape[0] for v in x_pieces]
    row_specs = lambda sizes: [fixed((n, width)) for n in sizes]
    first, first_t = call(
        functools.partial(norm_kernel, x_sizes, rows),
        "norm",
        (teams,),
        at,
        (*x_pieces, vec),
        row_specs(x_sizes) + [vec_spec],
        [((length, width), LOW), ((width, length), LOW)],
        [
            team_rows(width),
            pl.BlockSpec((width, own_rows), lambda k, a: (0, k ^ (a[0] // 2))),
        ],
        [pltpu.VMEM((own_rows, width), LOW)],
        length * width * 10,
        2 * act_bytes,
        after=(cuts[0],),
    )
    got = exchange(cuts)
    (first, first_t), moved = meet((first, first_t), got[1:])
    got = [got[0], *moved]
    merge_rows = tie(merge_rows, *got)
    mix = [v for g in got for v in (g, hop(g, 1))]
    extra = -(-max(0, starts[-1] + span - width) // feats)
    if not whole_rows:
        mix = [assemble(mix)]
    if teams == 4:
        near = [hop(merge_rows, 2), hop(merge_rows, 4)]
    else:
        near = exchange([merge_rows] * teams)[1:]
    merge_shape = (width + extra * feats, width)

    chip_rows = lambda n: pl.BlockSpec((own_rows, n), lambda k, a: (k, 0))
    mixed, mix = call(
        functools.partial(mix_kernel, len(mix)),
        "mix",
        (teams,),
        at,
        (*mix, first, mix_bias),
        [fixed(v.shape) for v in mix] + [chip_rows(width), fixed((8, 3 * span))],
        [((length, 3 * span), LOW), ((width, 3 * span), LOW)],
        [chip_rows(3 * span), mix_spec],
        [pltpu.VMEM((width, 3 * span), FULL)],
        2 * length * width * 3 * span,
        4 * act_bytes,
    )

    (mixed, mix), near = meet((mixed, mix), near)
    merge = [merge_rows, *near]
    g_own = own_pair(cotangent)
    g_near = gather_near(tie(g_own, mixed))

    seg = pick(segments, core)
    per = span // LANES
    runs = [(0, per // 2), (per // 2, per // 2)]
    seg_specs = [fixed((length, 1)), fixed((1, length))]
    segs = (seg.reshape(length, 1), seg.reshape(1, length))
    column = pl.BlockSpec((own_rows, LANES), lambda p, a: (0, p))

    def qkv_specs(base):
        return [
            pl.BlockSpec((length, LANES), lambda p, a, m=m: (0, m * per + base + p))
            for m in range(3)
        ]

    attended, wait = [], ()
    logs = []
    for base, count in runs:
        *got, log = call(
            functools.partial(attend_forward_kernel, teams, own_rows, dim, heads, base),
            "attend_forward",
            (count,),
            at,
            (mixed, mixed, mixed, *segs),
            qkv_specs(base) + seg_specs,
            [((own_rows, part), LOW)] * teams + [((length, part), FULL)],
            [column] * teams + [pl.BlockSpec((length, LANES), lambda p, a: (0, p))],
            [],
            length * length * dim * heads * 2,
            4 * length * part * 2,
            length * length * heads // 4,
            after=wait,
        )
        logs.append(log)
        if base == 0:
            other = [hop(v, 1) for v in merge]
            got, (*other, g_x, g_y) = meet(got, (*other, *g_near[1:3]))
            g_near = [g_own, g_x, g_y, *g_near[3:]]
            wait = (got[0],)
            attended = exchange(got)
            expand_other = hop(tie(expand_mine, got[0]), 1)
            if teams == 4:
                merge.append(hop(tie(merge[1], got[0]), 4))
        else:
            got, (expand_other, *moved) = meet(got, (expand_other, *attended, *merge[3:]))
            attended = [*moved[:teams], *exchange(got)]
            shrink_other = hop(tie(shrink_mine, got[0]), 1)
            merge = [*merge[:3], *moved[teams:]]
            other += [hop(v, 1) for v in merge[len(other) :]]
    merge = [v for both in zip(merge, other) for v in both]
    if not whole_rows:
        merge = [assemble(merge, extra)]

    weights = (expand_mine, shrink_mine, expand_other, shrink_other)
    wide = ((own_rows, width), FULL)
    wide_low = ((own_rows, width), LOW)
    piece = ((rows, width), LOW)
    hidden, *second, merge = simple(
        merge_norm_kernel,
        "merge_norm",
        (*attended, *merge, x_own, vec),
        [wide, piece, piece, (merge_shape, LOW)],
        [wide_low, wide_low, (merge_shape, FULL)],
        2 * own_rows * width * span * teams,
        count=teams,
        rows=rows,
        span=span,
        share=share,
        dim=dim,
        parts=len(merge),
    )
    near = [hop(v, 2 * k) for k in range(1, teams) if teams != 4 or k < 3 for v in second]
    second = [*second, *near]
    g_pieces = g_near

    e_row = e_bias.reshape(dp_n, teams, 2, hr).transpose(1, 2, 0, 3)
    e_row = pick(e_row, team)
    e_row = jnp.stack([pick(e_row, core), pick(e_row, 1 - core)])
    e_row = jnp.pad(e_row, ((0, 0), (0, 0), (0, hp - hr))).reshape(1, units)

    groups = [[0], [1, 2], [3, 4]] if teams == 4 else [[k] for k in range(teams)]
    halves = [[0, 1], [2, 3, 4, 5], [6, 7]] if teams == 4 else [[2 * k, 2 * k + 1] for k in range(teams)]
    acts, d_pres, e_sums, d_second, out = [], [], [], [], []
    for group, halved in zip(groups, halves):
        sizes = [x_sizes[i] for i in group]
        out_sizes = sizes if len(sizes) == 1 else [rows] * (sum(sizes) // rows)
        n, m = len(out_sizes), sum(sizes)
        half_spec = pl.BlockSpec((m, half), lambda f, a: (0, f))
        res = call(
            functools.partial(feed_kernel, rows, sizes, out_sizes),
            "feed",
            (2,),
            at,
            (*[second[i] for i in halved], *[g_pieces[i] for i in group], *weights, e_row),
            [piece_spec] * len(halved)
            + row_specs(sizes)
            + [pl.BlockSpec(memory_space=pl.ANY)] * 4
            + [pl.BlockSpec((1, half), lambda f, a: (0, f))],
            [((m, units), LOW)] * 2
            + [((8, units), FULL)]
            + [((size, width), LOW) for size in out_sizes] * 2,
            [half_spec, half_spec, pl.BlockSpec((8, half), lambda f, a: (0, f))]
            + row_specs(out_sizes) * 2,
            [pltpu.VMEM((m, width), LOW)] * 2
            + [pltpu.VMEM((m, width), FULL)] * 2
            + [
                pltpu.VMEM((2, half, width), LOW),
                pltpu.VMEM((2, width, half), LOW),
                pltpu.SemaphoreType.DMA((4,)),
            ],
            8 * m * width * units,
            4 * width * units + 12 * m * width,
            m * units,
            after=tuple(acts[-1:]),
        )
        if len(acts) == 0:
            res, moved = meet(res, second[2:])
            second = [*second[:2], *moved]
            if teams == 4:
                second += [hop(moved[0], 4), hop(moved[3], 2)]
            g_pieces = gather_far(g_pieces, *moved)
        elif len(acts) == 1 and teams == 4:
            res, moved = meet(res, (*second[6:], *g_pieces[3:]))
            second, g_pieces = [*second[:6], *moved[:2]], [*g_pieces[:3], *moved[2:]]
            early = reduce_early([None, *res[3 : 3 + n]])
        elif teams == 4:
            res, early = meet(res, early)
        acts.append(res[0])
        d_pres.append(res[1])
        e_sums.append(res[2])
        d_second += res[3 : 3 + n]
        out += res[3 + n :]

    sizes = [v.shape[0] for v in acts]
    def feed_grad(name, parts, units_of, turned, after):
        shape = (width, half) if turned else (half, width)
        return call(
            functools.partial(feed_grad_kernel, [v.shape[0] for v in parts], sizes, turned),
            name,
            (2,),
            at,
            (*parts, *units_of),
            [pl.BlockSpec(memory_space=pl.ANY)] * len(parts)
            + [pl.BlockSpec((s, half), lambda f, a: (0, 1 - f)) for s in sizes],
            [(shape, LOW)] * 2,
            [fixed(shape)] * 2,
            [
                pltpu.VMEM((length, width), LOW),
                pltpu.VMEM((length, half), LOW),
                pltpu.SemaphoreType.DMA((len(parts),)),
            ],
            2 * length * width * units,
            2 * act_bytes + 2 * width * units,
            after=after,
        )

    if teams != 4:
        early = reduce_early(d_second)
    far = reduce_far(d_second)
    sm, sg = feed_grad("shrink_grad", g_pieces, acts, True, ())
    (sm, sg), far = meet((sm, sg), far)
    late, folded = reduce_late(d_second, far)
    s_got = hop(sg, 1)
    out_early = reduce_early([tie(v, *folded[:1]) for v in out])
    em, eg = feed_grad("expand_grad", second, d_pres, False, (sm, *folded))
    (em, eg), (s_got, *late) = meet((em, eg), (s_got, *late))
    d_second = reduce_terms(d_second, early, late)
    s_sum = add_low(sm, s_got)
    e_got = hop(eg, 1)
    g_shrink = scatter(s_sum.reshape(dp_n, cols, half))

    terms = len(d_second)
    window = ((own_rows, span), LOW)
    d_hidden, d_branch, second_sums, *d_attended = simple(
        second_back_kernel,
        "second_back",
        (*d_second, hidden, g_own, merge, vec),
        [wide, wide_low, ((8, width), FULL)] + [window] * teams,
        [wide, wide_low],
        2 * own_rows * width * span * teams,
        after=(s_sum,),
        count=teams,
        rows=rows,
        span=span,
        dim=dim,
        terms=terms,
    )
    d_attended = exchange(d_attended)

    step = min(span, CHUNK)
    feat_block = ((teams, feats, width), LOW)
    mine, give = simple(
        merge_grad_kernel,
        "merge_grad",
        (*attended, d_branch),
        [feat_block, feat_block],
        [(merge_shape, FULL), ((teams * (span // step), own_rows, step), LOW)],
        2 * own_rows * width * span * teams,
        count=teams,
        span=span,
        share=share,
        dim=dim,
        step=step,
    )

    (mine, give), (e_got, *moved) = meet((mine, give), (e_got, *d_attended, *out_early))
    d_attended, out_early = moved[:teams], moved[teams:]
    e_sum = add_low(em, e_got)
    g_expand = scatter(e_sum.reshape(dp_n, hp, width))

    def core_parts(mine, got):
        return simple(
            add_parts_kernel,
            "add_parts",
            (mine, got),
            [(mine.shape[1:], LOW)] * teams,
        )

    g_merge = core_parts(mine, hop(give, 1))
    merge_near = exchange([tie(v, *d_attended) for v in g_merge])[1:]

    d_parts, wait = [], (e_sum, mixed, g_merge[0])
    for base, count in runs:
        (d_part,) = call(
            functools.partial(attend_backward_kernel, teams, own_rows, dim, heads, share, base),
            "attend_backward",
            (count,),
            at,
            (mixed, mixed, mixed, *d_attended, *segs, logs[len(d_parts)]),
            qkv_specs(base)
            + [pl.BlockSpec((own_rows, LANES), lambda p, a, base=base: (0, base + p))] * teams
            + seg_specs
            + [pl.BlockSpec((length, LANES), lambda p, a: (0, p))],
            [((3, length, part), LOW)],
            [pl.BlockSpec((3, length, LANES), lambda p, a: (0, 0, p))],
            [
                pltpu.VMEM((length, dim), FULL),
                pltpu.VMEM((length, dim), FULL),
                pltpu.VMEM((length, LANES), LOW),
                pltpu.VMEM((LANES, length), FULL),
            ],
            5 * length * length * dim * heads,
            8 * length * part * 2,
            length * length * heads // 4,
            after=wait,
        )
        if base == 0:
            (d_part,), merge_near = meet((d_part,), merge_near)
            out_far = reduce_far([*out[:5], *[tie(v, d_part) for v in out[5:]]])
            wait = (d_part,)
        else:
            (d_part,), out_far = meet((d_part,), out_far)
            out_late, folded = reduce_late(out, out_far)
        d_parts.append(d_part)

    mix_block = ((teams, feats, 3 * span), LOW)
    mine, give, mix_sums = call(
        mix_grad_kernel,
        "mix_grad",
        (3,),
        at,
        (*d_parts, first_t),
        [pl.BlockSpec((1, length, part), lambda c, a: (c, 0, 0))] * 2 + [fixed((width, length))],
        [mix_block, mix_block, ((8, 3 * span), FULL)],
        [pl.BlockSpec((teams, feats, span), lambda c, a: (0, 0, c))] * 2
        + [pl.BlockSpec((8, span), lambda c, a: (0, c))],
        [pltpu.VMEM((width, span), FULL), pltpu.VMEM((length, span), LOW)],
        2 * length * width * 3 * span,
        3 * act_bytes,
        after=tuple(folded[:1]),
    )
    mix_sums = mix_sums[0].reshape(3, span)
    (mine, give), out_late = meet((mine, give), out_late)
    mix_got = hop(give, 1)
    feed_cuts = simple(
        split_feed_kernel,
        "split_feed",
        (g_expand, g_shrink),
        [feed_cut] * teams,
        teams=teams,
        after=(give,),
        hp=hp,
    )
    out = reduce_terms(out, out_early, out_late)
    block_out = simple(
        block_out_kernel,
        "block_out",
        (*out, hidden, vec),
        [piece, piece],
        after=(give,),
        rows=rows,
        terms=terms,
    )
    g_merge = [g_merge[0], *merge_near]
    g_merge = functools.reduce(jnp.add, [v.astype(FULL) for v in g_merge]).astype(LOW)
    merge_each = width // dp_n
    g_merge = jnp.stack(
        [g_merge[:, d * merge_each : (d + 1) * merge_each] for d in range(dp_n)]
    )
    grad_merge = scatter(g_merge).astype(FULL)

    groups = [([3, 4], 3), ([1, 2], 1), ([0], 0)] if teams == 4 else [([k], k) for k in range(teams)]
    kept, (mix_got,) = meet((*block_out, *feed_cuts), (mix_got,))
    block_out, feed_cuts = kept[:2], kept[2:]
    g_mix = core_parts(mine, mix_got)
    d_first, first_sums, wait = [], [], (g_mix[0], g_merge)
    feed_cuts, g_mix = exchange(feed_cuts), exchange(g_mix)
    block_out = swap_out(*block_out)
    far = early = ()
    for group, low in groups:
        sizes = [x_sizes[i] for i in group]
        out_sizes = sizes if len(sizes) == 1 else [rows] * (sum(sizes) // rows)
        n = sum(sizes) // own_rows
        sums, *got = call(
            functools.partial(first_back_kernel, sizes, out_sizes, rows, span),
            "first_back",
            (n,),
            at,
            (*d_parts, *[x_pieces[i] for i in group], mix),
            [
                pl.BlockSpec(
                    (3, own_rows, part), lambda i, a, low=low: (0, (i + low) ^ (a[0] // 2), 0)
                )
            ]
            * 2
            + row_specs(sizes)
            + [fixed((width, 3 * span))],
            [((8, width), FULL)] + [((size, width), LOW) for size in out_sizes],
            [vec_spec] + row_specs(out_sizes),
            [
                pltpu.VMEM((own_rows, width), LOW),
                pltpu.VMEM((own_rows, width), LOW),
                pltpu.VMEM((own_rows, 3 * span), LOW),
            ],
            2 * n * own_rows * width * 3 * span,
            n * own_rows * width * 8,
            after=wait,
        )
        first_sums.append(sums)
        if not d_first:
            got, moved = meet(got, feed_cuts[1:])
            feed_cuts = [feed_cuts[0], *moved]
            wait = (sums,)
            far = reduce_far([None] * 5 + list(got))
        elif len(first_sums) == 2:
            got, moved = meet(got, g_mix[1:])
            g_mix = [g_mix[0], *moved]
            wait = (sums,)
            if teams == 4:
                early = reduce_early([None, *got])
        else:
            got, far = meet(got, far)
        d_first.append(got)
    (g_mix,) = simple(
        join_mix_kernel,
        "join_mix",
        g_mix,
        [((dp_n, feats, each), LOW)],
        [((teams, feats, 3 * span), LOW), ((feats, 3 * width), LOW)],
        teams=teams,
        dp_n=dp_n,
        each=each,
        span=span,
        starts=starts,
        width=width,
    )
    grad_mix = scatter(g_mix).astype(FULL)
    first_sums = functools.reduce(jnp.add, first_sums)
    if teams == 4:
        d_first = [*d_first[2], *d_first[1], *d_first[0]]
    else:
        d_first = [v for got in d_first for v in got]
        early = reduce_early(d_first)
    ek, eg, sk, sg = simple(
        part_feed_kernel,
        "part_feed",
        feed_cuts,
        [(e_shape, LOW), (e_shape, LOW), (s_shape, LOW), (s_shape, LOW)],
        [((teams, 2, hr, cols), LOW)],
        teams=teams,
    )
    late, folded = reduce_late(d_first, far, (g_mix, ek))
    def spread(v):
        return lax.dynamic_update_slice_in_dim(
            jnp.zeros((width + 2 * LANES,), FULL), v, start, 0
        )[:width]

    d_e = functools.reduce(jnp.add, [s[0] for s in e_sums]).reshape(2, dp_n, hp)[:, :, :hr]
    d_e = jnp.where(core == 0, d_e, d_e[::-1]).transpose(1, 0, 2)
    d_e = lax.dynamic_update_slice_in_dim(
        jnp.zeros((dp_n, teams, 2, hr), FULL), d_e[:, None], team, 1
    )
    partial = (
        first_sums[0],
        first_sums[1],
        spread(mix_sums[0]),
        spread(mix_sums[2]),
        second_sums[2],
        second_sums[0],
        second_sums[1],
        second_sums[3],
        d_e.reshape(-1),
    )
    partial = jnp.concatenate([v.reshape(seq_n, -1) for v in partial], axis=1)
    total = reduce_small(tie(partial, *folded[:1]))
    (ek, sk), (total, *early) = meet((ek, sk), (total, *early))
    d_first = reduce_terms(d_first, early, late)
    grad_expand, grad_shrink = simple(
        end_feed_kernel,
        "end_feed",
        (ek, hop(eg, 1), sk, hop(sg, 1)),
        [(expand_weight.shape, FULL), (shrink_weight.shape, FULL)],
        teams=teams,
        hr=hr,
    )

    piece_full = ((rows, width), FULL)
    input_grad = simple(
        input_grad_kernel,
        "input_grad",
        (*d_first, d_hidden, x_own, vec),
        [piece_full, piece_full],
        after=(grad_expand,),
        rows=rows,
        terms=terms,
    )
    input_grad = swap_out(*input_grad)

    ends = [total[i * feats : (i + 1) * feats] for i in range(8)]
    vectors = (*ends[:7], total[8 * feats :], ends[7])
    return (block_out, input_grad, grad_mix, grad_merge, grad_expand, grad_shrink, *vectors)


def solution(mesh):
    rows = P("dp", "seq", None)
    matrix = P("seq", "dp")
    vector = P("seq")
    return jax.shard_map(
        functools.partial(body, mesh.shape["seq"], mesh.shape["dp"]),
        mesh=mesh,
        in_specs=(rows, P("dp", None), rows) + (matrix,) * 4 + (vector,) * 9,
        out_specs=(rows, rows) + (matrix,) * 4 + (vector,) * 9,
        check_vma=False,
    )
```

```python
import functools

import jax
import jax.numpy as jnp
from jax import lax
from jax.experimental import pallas as pl
from jax.experimental.pallas import tpu as pltpu
from jax.sharding import PartitionSpec as P

HEADS = 25
COST = 0.12
LANES = 128
CHUNK = 256
QUERY_ROWS = 384
KEY_ROWS = 384
LOW = jnp.bfloat16
FULL = jnp.float32
VMEM_BYTES = 60 * 1024 * 1024


def dot_nn(left, right):
    return lax.dot_general(left, right, (((1,), (0,)), ((), ())), preferred_element_type=FULL)


def dot_tn(left, right):
    return lax.dot_general(left, right, (((0,), (0,)), ((), ())), preferred_element_type=FULL)


def dot_nt(left, right):
    return lax.dot_general(left, right, (((1,), (1,)), ((), ())), preferred_element_type=FULL)


def norm_parts(v):
    center = v - jnp.mean(v, axis=-1, keepdims=True)
    spread = jnp.mean(center * center, axis=-1, keepdims=True)
    inverse = lax.rsqrt(spread + 1e-05)
    return center * inverse, inverse


def norm_back(grad, gain, normal, inverse):
    e = grad * gain
    mean_e = jnp.mean(e, axis=-1, keepdims=True)
    mean_en = jnp.mean(e * normal, axis=-1, keepdims=True)
    return inverse * (e - mean_e - normal * mean_en)


def total_rows(v):
    return jnp.sum(v, axis=0, keepdims=True)


def fixed(shape):
    return pl.BlockSpec(shape, lambda *_: (0,) * len(shape), pipeline_mode=pl.Buffered(1))


def call(
    kernel, name, grid, at, operands, in_specs, outs, out_specs, scratch, flops, nbytes, exps=0, after=()
):
    if after:
        count, inner = len(operands), kernel
        kernel = lambda at_ref, *refs: inner(at_ref, *refs[:count], *refs[count + len(after) :])
        operands = (*operands, *after)
        in_specs = list(in_specs) + [pl.BlockSpec(memory_space=pl.ANY)] * len(after)
    spec = pltpu.PrefetchScalarGridSpec(
        num_scalar_prefetch=1,
        grid=grid,
        in_specs=in_specs,
        out_specs=out_specs,
        scratch_shapes=scratch,
    )
    return pl.pallas_call(
        kernel,
        grid_spec=spec,
        out_shape=[jax.ShapeDtypeStruct(s, d) for s, d in outs],
        compiler_params=pltpu.CompilerParams(vmem_limit_bytes=VMEM_BYTES),
        cost_estimate=pl.CostEstimate(
            flops=int(COST * flops),
            bytes_accessed=int(COST * nbytes),
            transcendentals=int(COST * exps),
        ),
        name=name,
    )(at, *operands)


def row_slot(half, core, rows):
    slot = core if half == 0 else 1 - core
    return pl.ds(pl.multiple_of(slot * rows, rows), rows)


def load_pair(step, sizes, refs, buf, core, rows):
    low = 0
    for size, ref in zip(sizes, refs):
        for i in range(size // rows):
            r = low // rows + i

            @pl.when(step == r // 2)
            def _():
                buf[row_slot(r % 2, core, rows), :] = ref[i * rows : (i + 1) * rows, :]

        low += size


def half_sum(refs, half, rows):
    parts = []
    for i, ref in enumerate(refs):
        if ref.shape[0] > rows:
            parts.append(ref[half * rows : (half + 1) * rows, :])
        elif (i + 1) % 2 == half:
            parts.append(ref[...])
    return functools.reduce(jnp.add, [v.astype(FULL) for v in parts])


def pair_rows(refs, core, rows, buf):
    for half in range(2):
        buf[row_slot(half, core, rows), :] = half_sum(refs, half, rows).astype(buf.dtype)


def fold_kernel(at_ref, x_ref, y_ref, far0_ref, far1_ref, xo_ref, yo_ref):
    xo_ref[...] = (x_ref[...].astype(FULL) + far1_ref[...].astype(FULL)).astype(LOW)
    yo_ref[...] = (y_ref[...].astype(FULL) + far0_ref[...].astype(FULL)).astype(LOW)


def place_rows(place, refs, wide, out):
    each = refs[0].shape[0]
    if len(refs) == 1:
        out[...] = refs[0][...]
        return
    for r, ref in enumerate(refs):
        begin = pl.multiple_of((place ^ r) * each, each)
        wide[pl.ds(begin, each), :] = ref[...].astype(FULL)
    filled = each * len(refs)
    if filled < wide.shape[0]:
        wide[filled:, :] = jnp.zeros((wide.shape[0] - filled, wide.shape[1]), FULL)
    block = 16
    for size in range(16, 129, 16):
        block = size if out.shape[0] % size == 0 else block

    def narrow(i, carry):
        span = pl.ds(pl.multiple_of(i * block, block), block)
        out[span, :] = wide[span, :].astype(LOW)
        return carry

    lax.fori_loop(0, out.shape[0] // block, narrow, 0)


def flip(v):
    rows, cols = v.shape
    v = jnp.pad(v.astype(FULL), ((0, -rows % LANES), (0, -cols % LANES)))
    return v.T[:cols, :rows]


def cut_feed_kernel(at_ref, e_ref, s_ref, ek_ref, eg_ref, sk_ref, sg_ref, *, teams, hr):
    first = at_ref[0] % 2 == 0
    cols = s_ref.shape[1]
    e, s = e_ref[...].astype(FULL), s_ref[...].astype(FULL)
    for t in range(teams):
        a, b = e[:, 2 * t * hr : (2 * t + 1) * hr], e[:, (2 * t + 1) * hr : (2 * t + 2) * hr]
        ek_ref[:, t * hr : (t + 1) * hr] = jnp.where(first, a, b).astype(LOW)
        eg_ref[:, t * hr : (t + 1) * hr] = jnp.where(first, b, a).astype(LOW)
    for t in range(teams // 2):
        a, b = s[2 * t * hr : (2 * t + 1) * hr], s[(2 * t + 1) * hr : (2 * t + 2) * hr]
        sk_ref[:, t * cols : (t + 1) * cols] = jnp.where(first, a, b).astype(LOW)
        sg_ref[:, t * cols : (t + 1) * cols] = jnp.where(first, b, a).astype(LOW)


def join_feed_kernel(at_ref, ek_ref, eo_ref, sk_ref, so_ref, *out_refs, teams, hr):
    first, team = at_ref[0] % 2 == 0, at_ref[0] // 2
    feats = ek_ref.shape[0]
    cols = 2 * feats
    mine, other = flip(ek_ref[...]), flip(eo_ref[...])
    low = jnp.where(first, mine, other).astype(LOW)
    high = jnp.where(first, other, mine).astype(LOW)
    for t in range(teams):
        part = slice((t % (teams // 2)) * cols, (t % (teams // 2) + 1) * cols)
        here = first if t < teams // 2 else jnp.logical_not(first)
        piece = jnp.where(here, sk_ref[:, part], so_ref[:, part])
        for k, ref in enumerate(out_refs):

            @pl.when((team ^ t) == k)
            def _():
                ref[0, :, :feats] = low[t * hr : (t + 1) * hr, :]
                ref[0, :, feats:] = high[t * hr : (t + 1) * hr, :]
                ref[1] = piece


def lay_feed_kernel(at_ref, *refs, teams, hp):
    part_refs, e_ref, s_ref, whole = refs[:teams], *refs[teams:]
    team = at_ref[0] // 2
    for k, ref in enumerate(part_refs):
        whole[team ^ k] = ref[...]
    hr, cols = whole.shape[2:]
    e_ref[hr:, :] = jnp.zeros((hp - hr, e_ref.shape[1]), LOW)
    s_ref[...] = jnp.zeros_like(s_ref)
    for t in range(teams):
        e_ref[:hr, t * cols : (t + 1) * cols] = whole[t, 0]
        s_ref[:, t * hp : t * hp + hr] = flip(whole[t, 1]).astype(LOW)


def split_feed_kernel(at_ref, e_ref, s_ref, *out_refs, teams, hp):
    team = at_ref[0] // 2
    hr, cols = out_refs[0].shape[1:]
    for t in range(teams):
        piece = flip(s_ref[:, t * hp : t * hp + hr]).astype(LOW)
        for k, ref in enumerate(out_refs):

            @pl.when((team ^ t) == k)
            def _():
                ref[0] = e_ref[:hr, t * cols : (t + 1) * cols]
                ref[1] = piece


def part_feed_kernel(at_ref, *refs, teams):
    part_refs, ek_ref, eg_ref, sk_ref, sg_ref, whole = refs[:teams], *refs[teams:]
    first, team = at_ref[0] % 2 == 0, at_ref[0] // 2
    for k, ref in enumerate(part_refs):
        whole[team ^ k] = ref[...]
    hr, cols = whole.shape[2:]
    feats = cols // 2
    for t in range(teams):
        e = flip(whole[t, 0])
        a, b = e[:feats, :], e[feats:, :]
        ek_ref[:, t * hr : (t + 1) * hr] = jnp.where(first, a, b).astype(LOW)
        eg_ref[:, t * hr : (t + 1) * hr] = jnp.where(first, b, a).astype(LOW)
    for t in range(teams // 2):
        a, b = whole[t, 1], whole[teams // 2 + t, 1]
        sk_ref[:, t * cols : (t + 1) * cols] = jnp.where(first, a, b)
        sg_ref[:, t * cols : (t + 1) * cols] = jnp.where(first, b, a)


def end_feed_kernel(at_ref, ek_ref, eo_ref, sk_ref, so_ref, e_ref, s_ref, *, teams, hr):
    first = at_ref[0] % 2 == 0
    cols = s_ref.shape[1]
    mine, other = ek_ref[...].astype(FULL), eo_ref[...].astype(FULL)
    low, high = jnp.where(first, mine, other), jnp.where(first, other, mine)
    for t in range(teams):
        e_ref[:, 2 * t * hr : (2 * t + 1) * hr] = low[:, t * hr : (t + 1) * hr]
        e_ref[:, (2 * t + 1) * hr : (2 * t + 2) * hr] = high[:, t * hr : (t + 1) * hr]
    mine, other = sk_ref[...].astype(FULL), so_ref[...].astype(FULL)
    low, high = jnp.where(first, mine, other), jnp.where(first, other, mine)
    for t in range(teams // 2):
        s_ref[2 * t * hr : (2 * t + 1) * hr, :] = low[:, t * cols : (t + 1) * cols]
        s_ref[(2 * t + 1) * hr : (2 * t + 2) * hr, :] = high[:, t * cols : (t + 1) * cols]


def cut_mix_kernel(at_ref, rows_ref, *refs, teams, dp_n, each, span, starts, width):
    out_refs, merge_ref, full = refs[:teams], refs[teams], refs[teams + 1]
    team = at_ref[0] // 2
    part = width // dp_n
    for d in range(dp_n):
        full[:, d * each : (d + 1) * each] = rows_ref[d, :, :each]
        merge_ref[:, d * part : (d + 1) * part] = rows_ref[d, :, each:]
    full[:, dp_n * each :] = jnp.zeros((full.shape[0], full.shape[1] - dp_n * each), LOW)
    for t in range(teams):
        for k, ref in enumerate(out_refs):

            @pl.when((team ^ t) == k)
            def _():
                for m in range(3):
                    begin = m * width + starts[t]
                    ref[:, m * span : (m + 1) * span] = full[:, begin : begin + span]


def join_mix_kernel(at_ref, *refs, teams, dp_n, each, span, starts, width):
    part_refs, out_ref, whole, flat = refs[:teams], *refs[teams:]
    team = at_ref[0] // 2
    share = width // teams
    for k, ref in enumerate(part_refs):
        whole[team ^ k] = ref[...]
    for m in range(3):
        for t in range(teams):
            low = m * span + share * t - starts[t]
            begin = m * width + share * t
            flat[:, begin : begin + share] = whole[t, :, low : low + share]
    for d in range(dp_n):
        out_ref[d] = flat[:, d * each : (d + 1) * each]


def add_parts_kernel(at_ref, mine_ref, got_ref, *out_refs):
    team = at_ref[0] // 2
    for k, ref in enumerate(out_refs):
        total = mine_ref[team ^ k].astype(FULL) + got_ref[team ^ k].astype(FULL)
        ref[...] = total.astype(LOW)


def norm_kernel(sizes, rows, at_ref, *refs):
    count = len(sizes)
    vec_ref, first_ref, turned_ref, buf = refs[count:]
    load_pair(pl.program_id(0), sizes, refs[:count], buf, at_ref[0] % 2, rows)
    normal, _ = norm_parts(buf[...].astype(FULL))
    first = (normal * vec_ref[0:1, :] + vec_ref[1:2, :]).astype(LOW)
    first_ref[...] = first
    turned_ref[...] = first.T


def mix_kernel(parts, at_ref, *refs):
    first_ref, bias_ref, mixed_ref, mix_ref, wide = refs[parts:]

    @pl.when(pl.program_id(0) == 0)
    def _():
        place_rows(at_ref[0], refs[:parts], wide, mix_ref)

    mixed = dot_nn(first_ref[...], mix_ref[...]) + bias_ref[0:1, :]
    mixed_ref[...] = (mixed * bias_ref[1:2, :]).astype(LOW)


def causal_chunks(length, begin):
    stop = begin + QUERY_ROWS
    return [(low, min(low + KEY_ROWS, stop)) for low in range(0, stop, KEY_ROWS)]


def visible_scores(query, key, begin, low, col_ref, row_ref):
    scores = dot_nt(query, key)
    rows, cols = scores.shape
    seen = col_ref[begin : begin + rows, :] == row_ref[:, low : low + cols]
    if low + cols > begin:
        row_id = lax.broadcasted_iota(jnp.int32, (rows, cols), 0) + begin
        col_id = lax.broadcasted_iota(jnp.int32, (rows, cols), 1) + low
        seen = seen & (col_id <= row_id)
    return jnp.where(seen, scores, -1e30)


def attend_forward_kernel(count, block, dim, heads, base, at_ref, *refs):
    q_ref, k_ref, v_ref, col_ref, row_ref = refs[:5]
    out_refs, log_ref = refs[5:-1], refs[-1]
    pair = pl.program_id(0) + base
    team = at_ref[0] // 2
    for ref in out_refs:
        ref[...] = jnp.zeros_like(ref)
    for sub in range(LANES // dim):

        @pl.when(pair * (LANES // dim) + sub < heads)
        def _():
            lanes = slice(sub * dim, (sub + 1) * dim)
            for begin in range(0, count * block, QUERY_ROWS):
                rows = slice(begin, begin + QUERY_ROWS)
                query = q_ref[rows, lanes]
                chunks = causal_chunks(count * block, begin)
                scores = [
                    visible_scores(
                        query, k_ref[low:high, lanes], begin, low, col_ref, row_ref
                    )
                    for low, high in chunks
                ]
                top = functools.reduce(
                    jnp.maximum, [jnp.max(p, axis=1, keepdims=True) for p in scores]
                )
                expo = [jnp.exp(p - top) for p in scores]
                total = functools.reduce(
                    jnp.add, [jnp.sum(p, axis=1, keepdims=True) for p in expo]
                )
                mixed = functools.reduce(
                    jnp.add,
                    [
                        dot_nn(e.astype(LOW), v_ref[low:high, lanes])
                        for e, (low, high) in zip(expo, chunks)
                    ],
                )
                mixed = (mixed / total).astype(LOW)
                log_ref[rows, lanes] = jnp.broadcast_to(top + jnp.log(total), (QUERY_ROWS, dim))
                place = slice(begin % block, begin % block + QUERY_ROWS)
                for k, ref in enumerate(out_refs):

                    @pl.when((team ^ (begin // block)) == k)
                    def _():
                        ref[place, lanes] = mixed


def attend_backward_kernel(count, block, dim, heads, share, base, at_ref, *refs):
    q_ref, k_ref, v_ref, *g_refs = refs[: 3 + count]
    col_ref, row_ref, log_ref, d_ref, acc_k, acc_v, grads, logs = refs[3 + count :]
    pair = pl.program_id(0) + base
    team = at_ref[0] // 2
    scale = dim**-0.5
    d_ref[...] = jnp.zeros_like(d_ref)
    logs[...] = log_ref[...].T
    for k, ref in enumerate(g_refs):
        grads[pl.ds(pl.multiple_of((team ^ k) * block, block), block), :] = ref[...]
    for sub in range(LANES // dim):

        @pl.when(pair * (LANES // dim) + sub < heads)
        def _():
            lanes = slice(sub * dim, (sub + 1) * dim)
            column = lax.broadcasted_iota(jnp.int32, (1, dim), 1)
            column = column + at_ref[1 + team] + pair * LANES + sub * dim
            owned = (column >= share * team) & (column < share * (team + 1))
            owned = jnp.where(owned, 1.0, 0.0)
            acc_k[...] = jnp.zeros_like(acc_k)
            acc_v[...] = jnp.zeros_like(acc_v)
            for begin in range(0, count * block, QUERY_ROWS):
                rows = slice(begin, begin + QUERY_ROWS)
                query = q_ref[rows, lanes]
                grad = grads[rows, lanes]
                log_total = logs[sub * dim : sub * dim + 1, rows]
                chunks = causal_chunks(count * block, begin)
                probs, d_weights = [], []
                for low, high in chunks:
                    scores = dot_nt(k_ref[low:high, lanes], query)
                    seen = col_ref[low:high, :] == row_ref[:, rows]
                    if high > begin:
                        key_id = lax.broadcasted_iota(jnp.int32, scores.shape, 0) + low
                        query_id = lax.broadcasted_iota(jnp.int32, scores.shape, 1) + begin
                        seen = seen & (key_id <= query_id)
                    probs.append(jnp.exp(jnp.where(seen, scores, -1e30) - log_total))
                    d_weights.append(dot_nt(v_ref[low:high, lanes], grad))
                delta = functools.reduce(
                    jnp.add, [total_rows(p * d) for p, d in zip(probs, d_weights)]
                )
                d_query = jnp.zeros((QUERY_ROWS, dim), FULL)
                for prob, d_weight, (low, high) in zip(probs, d_weights, chunks):
                    d_scores = (prob * (d_weight - delta)).astype(LOW)
                    d_query = d_query + dot_tn(d_scores, k_ref[low:high, lanes])
                    acc_k[low:high, :] += dot_nn(d_scores, query)
                    acc_v[low:high, :] += dot_nn(prob.astype(LOW), grad)
                d_ref[0, rows, lanes] = (d_query * scale * owned).astype(LOW)
            d_ref[1, :, lanes] = (acc_k[...] * owned).astype(LOW)
            d_ref[2, :, lanes] = (acc_v[...] * owned).astype(LOW)


def merge_norm_kernel(at_ref, *refs, count, rows, span, share, dim, parts):
    att_refs, part_refs = refs[: 2 * count], refs[2 * count : 2 * count + parts]
    x_ref, vec_ref, hid_ref, s0_ref, s1_ref, merge_ref, xs, buf, wide = refs[2 * count + parts :]
    core, team = at_ref[0] % 2, at_ref[0] // 2
    place_rows(at_ref[0], part_refs, wide, merge_ref)
    pair_rows([x_ref], core, rows, xs)
    hidden = xs[...].astype(FULL) + vec_ref[4:5, :]
    lane = lax.broadcasted_iota(jnp.int32, (1, span), 1)
    for k in range(count):
        other = team ^ k
        start = at_ref[1 + other]
        low = share * other - start
        owned = (lane >= low) & (lane < low + share)
        piece = jnp.concatenate([att_refs[k][...], att_refs[count + k][...]], axis=1)
        piece = jnp.where(owned, piece, jnp.zeros((), LOW))
        hidden = hidden + dot_nn(piece, merge_ref[pl.ds(pl.multiple_of(start, dim), span), :])
    hid_ref[...] = hidden
    normal, _ = norm_parts(hidden)
    buf[...] = (normal * vec_ref[5:6, :] + vec_ref[6:7, :]).astype(LOW)
    s0_ref[...] = buf[row_slot(0, core, rows), :]
    s1_ref[...] = buf[row_slot(1, core, rows), :]


def feed_kernel(rows, sizes, out_sizes, at_ref, *refs):
    pieces, count = len(sizes), len(out_sizes)
    lows = [sum(sizes[:i]) for i in range(pieces)]
    halves = sum(sizes) // rows
    sec_refs, g_refs, refs = refs[:halves], refs[halves : halves + pieces], refs[halves + pieces :]
    weights, (bias_ref, act_ref, dpre_ref, sum_ref), rest = refs[:4], refs[4:8], refs[8:]
    ds_refs, out_refs = rest[:count], rest[count : 2 * count]
    sec, g, acc_s, acc_o, e_held, s_held, sems = rest[2 * count :]
    step = pl.program_id(0)
    copies = [
        pltpu.make_async_copy(ref, held.at[i // 2], sems.at[i])
        for i, (ref, held) in enumerate(zip(weights, (e_held, s_held) * 2))
    ]

    @pl.when(step == 0)
    def _():
        for copy in copies:
            copy.start()
        for i in range(halves):
            sec[i * rows : (i + 1) * rows, :] = sec_refs[i][...]
        for i in range(pieces):
            g[lows[i] : lows[i] + sizes[i], :] = g_refs[i][...]
        copies[0].wait()
        copies[1].wait()

    @pl.when(step == 1)
    def _():
        copies[2].wait()
        copies[3].wait()

    et, st = e_held[step], s_held[step]
    u = dot_nt(sec[...], et) + bias_ref[...]
    d_act = dot_nn(g[...], st)
    square = u * u
    tanh = jnp.tanh(0.7978845608028654 * u * (1.0 + 0.044715 * square))
    plus = 0.5 * (1.0 + tanh)
    act = (u * plus).astype(LOW)
    slope = plus + u * (0.5 * 0.7978845608028654) * (1.0 - tanh * tanh) * (
        1.0 + 3 * 0.044715 * square
    )
    d_pre = (d_act * slope).astype(LOW)
    act_ref[...] = act
    dpre_ref[...] = d_pre
    sum_ref[...] = jnp.broadcast_to(total_rows(d_pre.astype(FULL)), sum_ref.shape)
    part_s = dot_nn(d_pre, et)
    part_o = dot_nt(act, st)

    @pl.when(step == 0)
    def _():
        acc_s[...] = part_s
        acc_o[...] = part_o

    @pl.when(step == 1)
    def _():
        for i in range(count):
            here = slice(sum(out_sizes[:i]), sum(out_sizes[: i + 1]))
            ds_refs[i][...] = (acc_s[here, :] + part_s[here, :]).astype(LOW)
            out_refs[i][...] = (acc_o[here, :] + part_o[here, :]).astype(LOW)


def feed_grad_kernel(pieces, sizes, turned, at_ref, *refs):
    count = len(pieces)
    piece_refs, unit_refs = refs[:count], refs[count : count + len(sizes)]
    mine_ref, give_ref, held, units, sems = refs[count + len(sizes) :]
    step = pl.program_id(0)
    copies = [
        pltpu.make_async_copy(
            ref, held.at[sum(pieces[:i]) : sum(pieces[: i + 1]), :], sems.at[i]
        )
        for i, ref in enumerate(piece_refs)
    ]

    @pl.when(step == 0)
    def _():
        for copy in copies:
            copy.start()
        for copy in copies:
            copy.wait()

    low = 0
    for size, ref in zip(sizes, unit_refs):
        units[low : low + size, :] = ref[...]
        low += size
    if turned:
        grad = dot_tn(held[...], units[...]).astype(LOW)
    else:
        grad = dot_tn(units[...], held[...]).astype(LOW)

    @pl.when(step == 0)
    def _():
        give_ref[...] = grad

    @pl.when(step == 1)
    def _():
        mine_ref[...] = grad


def second_back_kernel(at_ref, *refs, count, rows, span, dim, terms):
    rest = refs[terms:]
    hid_ref, g_ref, merge_ref, vec_ref = rest[:4]
    dh_ref, db_ref, sum_ref = rest[4:7]
    att_refs = rest[7 : 7 + count]
    ds, g = rest[7 + count :]
    core, team = at_ref[0] % 2, at_ref[0] // 2
    pair_rows(refs[:terms], core, rows, ds)
    pair_rows([g_ref], core, rows, g)
    normal, inverse = norm_parts(hid_ref[...])
    d_second = ds[...]
    g_full = g[...].astype(FULL)
    d_hidden = g_full + norm_back(d_second, vec_ref[5:6, :], normal, inverse)
    dh_ref[...] = d_hidden
    d_branch = d_hidden.astype(LOW)
    db_ref[...] = d_branch
    sum_ref[0:1, :] = total_rows(d_second * normal)
    sum_ref[1:2, :] = total_rows(d_second)
    sum_ref[2:3, :] = total_rows(d_branch.astype(FULL))
    sum_ref[3:4, :] = total_rows(g_full)
    sum_ref[4:8, :] = jnp.zeros((4, sum_ref.shape[1]), FULL)
    for k, ref in enumerate(att_refs):
        start = pl.multiple_of(at_ref[1 + (team ^ k)], dim)
        ref[...] = dot_nt(d_branch, merge_ref[pl.ds(start, span), :]).astype(LOW)


def split_cores(core, value, mine_ref, give_ref):
    feats = mine_ref.shape[1]
    for t in range(mine_ref.shape[0]):
        low = value[2 * t * feats : (2 * t + 1) * feats, :]
        high = value[(2 * t + 1) * feats : (2 * t + 2) * feats, :]
        mine_ref[t] = jnp.where(core == 0, low, high).astype(LOW)
        give_ref[t] = jnp.where(core == 0, high, low).astype(LOW)


def merge_grad_kernel(at_ref, *refs, count, span, share, dim, step):
    att_refs = refs[: 2 * count]
    db_ref, mine_ref, give_ref, acc, held = refs[2 * count :]
    team = at_ref[0] // 2
    acc[...] = jnp.zeros_like(acc)
    lane = lax.broadcasted_iota(jnp.int32, (1, span), 1)
    for k in range(count):
        other = team ^ k
        low = share * other - at_ref[1 + other]
        owned = (lane >= low) & (lane < low + share)
        piece = jnp.concatenate([att_refs[k][...], att_refs[count + k][...]], axis=1)
        piece = jnp.where(owned, piece, jnp.zeros((), LOW))
        for c in range(span // step):
            held[k * (span // step) + c] = piece[:, c * step : (c + 1) * step]

    def add(i, carry):
        start = at_ref[1 + (team ^ (i // (span // step)))] + (i % (span // step)) * step
        acc[pl.ds(pl.multiple_of(start, dim), step), :] += dot_tn(held[i], db_ref[...])
        return carry

    lax.fori_loop(0, count * (span // step), add, 0)
    split_cores(at_ref[0] % 2, acc, mine_ref, give_ref)


def first_back_kernel(sizes, out_sizes, rows, span, at_ref, *refs):
    count, out_count = len(sizes), len(out_sizes)
    sides = 2
    d_refs, x_refs, refs = refs[:sides], refs[sides : sides + count], refs[sides + count :]
    mix_ref, sum_ref = refs[:2]
    out_refs = refs[2 : 2 + out_count]
    buf, low, joined = refs[2 + out_count :]
    step = pl.program_id(0)
    core = at_ref[0] % 2
    load_pair(step, sizes, x_refs, buf, core, rows)
    normal, _ = norm_parts(buf[...].astype(FULL))
    for m in range(3):
        for i, d_ref in enumerate(d_refs):
            n = span // sides
            begin = m * span + i * n
            joined[:, begin : begin + n] = d_ref[m]
    d_first = dot_nt(joined[...], mix_ref[...])

    @pl.when(step == 0)
    def _():
        sum_ref[...] = jnp.zeros_like(sum_ref)

    sum_ref[0:1, :] += total_rows(d_first * normal)
    sum_ref[1:2, :] += total_rows(d_first)
    low[...] = d_first.astype(LOW)
    begin = 0
    for size, ref in zip(out_sizes, out_refs):
        for i in range(size // rows):
            r = begin // rows + i

            @pl.when(step == r // 2)
            def _():
                ref[i * rows : (i + 1) * rows, :] = low[row_slot(r % 2, core, rows), :]

        begin += size


def mix_grad_kernel(at_ref, *refs):
    turned_ref, mine_ref, give_ref, sum_ref, held, d = refs[-6:]
    for i, ref in enumerate(refs[:-6]):
        n = ref.shape[2]
        d[:, i * n : (i + 1) * n] = ref[0]
    sum_ref[...] = jnp.broadcast_to(total_rows(d[...].astype(FULL)), sum_ref.shape)
    held[...] = dot_nn(turned_ref[...], d[...])
    split_cores(at_ref[0] % 2, held, mine_ref, give_ref)


def block_out_kernel(at_ref, *refs, rows, terms):
    hid_ref, vec_ref, o0_ref, o1_ref = refs[terms:]
    core = at_ref[0] % 2
    for half, ref in enumerate((o0_ref, o1_ref)):
        value = hid_ref[row_slot(half, core, rows), :] + vec_ref[7:8, :]
        ref[...] = (value + half_sum(refs[:terms], half, rows)).astype(LOW)


def input_grad_kernel(at_ref, *refs, rows, terms):
    dh_ref, x_ref, vec_ref, o0_ref, o1_ref = refs[terms:]
    core = at_ref[0] % 2
    for half, ref in enumerate((o0_ref, o1_ref)):
        d_first = half_sum(refs[:terms], half, rows)
        normal, inverse = norm_parts(x_ref[half * rows : (half + 1) * rows, :].astype(FULL))
        back = norm_back(d_first, vec_ref[0:1, :], normal, inverse)
        ref[...] = dh_ref[row_slot(half, core, rows), :] + back


def body(
    seq_n,
    dp_n,
    inputs,
    segments,
    cotangent,
    mix_weight,
    merge_weight,
    expand_weight,
    shrink_weight,
    first_gain,
    first_bias,
    query_bias,
    value_bias,
    merge_bias,
    second_gain,
    second_bias,
    expand_bias,
    shrink_bias,
):
    micro, rows, width = inputs.shape
    length = segments.shape[1]
    dim = width // HEADS
    teams = seq_n // 2
    bits = teams.bit_length() - 1
    pieces = seq_n
    own_rows = 2 * rows
    feats = width // seq_n
    share = width // teams
    begins = [share * t // dim for t in range(teams)]
    heads = max(-(-share * (t + 1) // dim) - begins[t] for t in range(teams))
    starts = [dim * min(h, HEADS - heads) for h in begins]
    span = -(-heads * dim // (2 * LANES)) * 2 * LANES
    part = span // 2
    hidden_units = expand_weight.shape[1] * dp_n
    hr = hidden_units // dp_n // teams // 2
    hp = hr
    while hp % 16 or dp_n * hp % LANES:
        hp += 1
    half = dp_n * hp
    units = 2 * half
    whole_rows = feats % 8 == 0

    place = lax.axis_index("seq")
    core = place % 2
    team = place // 2
    at = jnp.concatenate([place[None].astype(jnp.int32), jnp.asarray(starts, jnp.int32)])

    def hop(v, mask):
        shape = v.shape
        if len(shape) == 2 and shape[0] % LANES == 0 and shape[1] % LANES:
            v = v.reshape(2, shape[0] // 2, shape[1])
        return lax.ppermute(v, "seq", [(i, i ^ mask) for i in range(seq_n)]).reshape(shape)

    def pick(v, index):
        return lax.dynamic_index_in_dim(v, index, 0, keepdims=False)

    def along(v):
        return lax.all_gather(v, "dp", axis=0)

    def scatter(v):
        return lax.psum_scatter(v, "dp", scatter_dimension=0)

    def by_core(mine, other):
        return jnp.where(core == 0, jnp.stack([mine, other]), jnp.stack([other, mine]))

    def tie(v, *others):
        return lax.optimization_barrier((v, *others))[0]

    def meet(kept, moved):
        both = lax.optimization_barrier((*kept, *moved))
        return both[: len(kept)], both[len(kept) :]

    def own_pair(v, *others):
        mine = pick(v, core)
        return jnp.concatenate([mine, hop(tie(pick(v, 1 - core), *others), 1)], axis=0)

    def gather_near(own):
        if teams == 4:
            return [own, hop(own, 2), hop(own, 4)]
        return exchange([own] * teams)

    def gather_far(near, *others):
        if teams == 4:
            x, y = tie(near[1][:rows], *others), tie(near[2][rows:], *others)
            return [*near, hop(x, 4), hop(y, 2)]
        return near

    def add_low(a, b):
        return (a.astype(FULL) + b.astype(FULL)).astype(LOW)

    def reduce_early(p):
        return [hop(p[1], 2), hop(p[4], 4)] if teams == 4 else exchange(p)[1:]

    def reduce_far(p):
        return [hop(p[5], 2), hop(p[6], 4)] if teams == 4 else []

    def reduce_late(p, far, after=()):
        if teams != 4:
            return [], ()
        folded = simple(
            fold_kernel, "fold", (p[2], p[3], *far), [((rows, width), LOW)] * 2, after=after
        )
        return [hop(folded[0], 2), hop(folded[1], 4)], folded

    def reduce_terms(p, early, late):
        if teams == 4:
            return [p[0], early[0], late[0], late[1], early[1]]
        return [p[0], *early]

    def exchange(parts):
        return [parts[0]] + [hop(parts[k], 2 * k) for k in range(1, teams)]

    def assemble(parts, extra=0):
        out = jnp.zeros((seq_n + extra,) + parts[0].shape, parts[0].dtype)
        for r in range(pieces):
            out = lax.dynamic_update_index_in_dim(out, parts[r], place ^ r, 0)
        return out.reshape((-1,) + parts[0].shape[1:])

    def swap_out(out0, out1):
        return by_core(out0, hop(out1, 1))

    def gather_small(v):
        cur = v[None]
        for b in range(bits + 1):
            got = hop(cur, 1 << b)
            bit = (place >> b) & 1
            cur = jnp.where(
                bit == 0, jnp.concatenate([cur, got]), jnp.concatenate([got, cur])
            )
        return cur

    def reduce_small(v, *others):
        for b in reversed(range(bits + 1)):
            half_n = v.shape[0] // 2
            bit = (place >> b) & 1
            mine = jnp.where(bit == 0, v[:half_n], v[half_n:])
            give = jnp.where(bit == 0, v[half_n:], v[:half_n])
            v = mine + hop(give, 1 << b)
        v = tie(v[0], *others)
        for b in range(dp_n.bit_length() - 1):
            v = v + lax.ppermute(v, "dp", [(i, i ^ (1 << b)) for i in range(dp_n)])
        return v

    def simple(kernel, name, operands, outs, scratch=(), flops=0, nbytes=None, after=(), **named):
        if nbytes is None:
            nbytes = sum(v.size * v.dtype.itemsize for v in operands)
            nbytes += sum(4 * functools.reduce(lambda a, b: a * b, s) for s, _ in outs)
        return call(
            functools.partial(kernel, **named),
            name,
            (1,),
            at,
            operands,
            [fixed(v.shape) for v in operands],
            outs,
            [fixed(s) for s, _ in outs],
            [pltpu.VMEM(s, d) for s, d in scratch],
            flops,
            nbytes,
            after=after,
        )

    each = mix_weight.shape[1]
    mix_local = jnp.concatenate([mix_weight, merge_weight], axis=1)
    mix_rows = along(mix_local)
    small = (
        first_gain,
        first_bias,
        query_bias,
        value_bias,
        merge_bias,
        second_gain,
        second_bias,
        shrink_bias,
        expand_bias,
    )
    packed = gather_small(jnp.concatenate([v.reshape(-1, feats) for v in small], axis=0))
    x_own = own_pair(inputs)
    x_near = gather_near(tie(x_own, packed))

    cols = shrink_weight.shape[1]
    e_shape, s_shape = (feats, teams * hr), (hr, teams // 2 * cols)
    ek, eg, sk, sg = simple(
        cut_feed_kernel,
        "cut_feed",
        (expand_weight, shrink_weight),
        [(e_shape, LOW), (e_shape, LOW), (s_shape, LOW), (s_shape, LOW)],
        after=(mix_local,),
        teams=teams,
        hr=hr,
    )
    feed_cut = ((2, hr, cols), LOW)
    feed_cuts = simple(
        join_feed_kernel,
        "join_feed",
        (ek, hop(eg, 1), sk, hop(sg, 1)),
        [feed_cut] * teams,
        teams=teams,
        hr=hr,
    )
    feed_cuts, x_near = meet(exchange(feed_cuts), x_near)
    x_pieces = gather_far(x_near)
    vec = packed[:, :8].transpose(1, 0, 2)
    vec = vec.reshape(8, width).astype(FULL)
    e_bias = packed[:, 8:].reshape(-1).astype(FULL)
    mix_cut = ((feats, 3 * span), LOW)
    *cuts, merge_rows = simple(
        cut_mix_kernel,
        "cut_mix",
        (mix_rows,),
        [mix_cut] * teams + [((feats, width), LOW)],
        [((feats, 3 * width + LANES), LOW)],
        after=(*feed_cuts, vec),
        teams=teams,
        dp_n=dp_n,
        each=each,
        span=span,
        starts=starts,
        width=width,
    )
    e_cut, s_cut = simple(
        lay_feed_kernel,
        "lay_feed",
        feed_cuts,
        [((hp, width), LOW), ((cols, half), LOW)],
        [((teams, 2, hr, cols), LOW)],
        after=(cuts[0],),
        teams=teams,
        hp=hp,
    )

    expand_mine = along(e_cut).reshape(half, width)
    shrink_mine = along(tie(s_cut, expand_mine[0])).reshape(width, half)

    start = at[1 + team]

    def windowed(row):
        return lax.dynamic_slice_in_dim(jnp.pad(vec[row], (0, 2 * LANES)), start, span, 0)

    blank = jnp.zeros((span,), FULL)
    mix_bias = jnp.concatenate([windowed(2), blank, windowed(3)])
    shrinking = jnp.where(jnp.arange(3 * span) < span, dim**-0.5, 1.0).astype(FULL)
    mix_bias = jnp.concatenate([mix_bias[None], shrinking[None], jnp.zeros((6, 3 * span), FULL)])

    act_bytes = length * width * 2
    piece_spec = fixed((rows, width))
    vec_spec = fixed((8, width))
    mix_spec = fixed((width, 3 * span))
    team_rows = lambda n: pl.BlockSpec((own_rows, n), lambda k, a: (k ^ (a[0] // 2), 0))
    kept, moved = meet((*cuts, merge_rows), x_pieces[3:])
    cuts, merge_rows, x_pieces = kept[:-1], kept[-1], [*x_near, *moved]
    x_sizes = [v.shape[0] for v in x_pieces]
    row_specs = lambda sizes: [fixed((n, width)) for n in sizes]
    first, first_t = call(
        functools.partial(norm_kernel, x_sizes, rows),
        "norm",
        (teams,),
        at,
        (*x_pieces, vec),
        row_specs(x_sizes) + [vec_spec],
        [((length, width), LOW), ((width, length), LOW)],
        [
            team_rows(width),
            pl.BlockSpec((width, own_rows), lambda k, a: (0, k ^ (a[0] // 2))),
        ],
        [pltpu.VMEM((own_rows, width), LOW)],
        length * width * 10,
        2 * act_bytes,
        after=(cuts[0],),
    )
    got = exchange(cuts)
    (first, first_t), moved = meet((first, first_t), got[1:])
    got = [got[0], *moved]
    merge_rows = tie(merge_rows, *got)
    mix = [v for g in got for v in (g, hop(g, 1))]
    extra = -(-max(0, starts[-1] + span - width) // feats)
    if not whole_rows:
        mix = [assemble(mix)]
    if teams == 4:
        near = [hop(merge_rows, 2), hop(merge_rows, 4)]
    else:
        near = exchange([merge_rows] * teams)[1:]
    merge_shape = (width + extra * feats, width)

    chip_rows = lambda n: pl.BlockSpec((own_rows, n), lambda k, a: (k, 0))
    mixed, mix = call(
        functools.partial(mix_kernel, len(mix)),
        "mix",
        (teams,),
        at,
        (*mix, first, mix_bias),
        [fixed(v.shape) for v in mix] + [chip_rows(width), fixed((8, 3 * span))],
        [((length, 3 * span), LOW), ((width, 3 * span), LOW)],
        [chip_rows(3 * span), mix_spec],
        [pltpu.VMEM((width, 3 * span), FULL)],
        2 * length * width * 3 * span,
        4 * act_bytes,
    )

    (mixed, mix), near = meet((mixed, mix), near)
    merge = [merge_rows, *near]
    g_own = own_pair(cotangent)
    g_near = gather_near(tie(g_own, mixed))

    seg = pick(segments, core)
    per = span // LANES
    runs = [(0, per // 2), (per // 2, per // 2)]
    seg_specs = [fixed((length, 1)), fixed((1, length))]
    segs = (seg.reshape(length, 1), seg.reshape(1, length))
    column = pl.BlockSpec((own_rows, LANES), lambda p, a: (0, p))

    def qkv_specs(base):
        return [
            pl.BlockSpec((length, LANES), lambda p, a, m=m: (0, m * per + base + p))
            for m in range(3)
        ]

    attended, wait = [], ()
    logs = []
    for base, count in runs:
        *got, log = call(
            functools.partial(attend_forward_kernel, teams, own_rows, dim, heads, base),
            "attend_forward",
            (count,),
            at,
            (mixed, mixed, mixed, *segs),
            qkv_specs(base) + seg_specs,
            [((own_rows, part), LOW)] * teams + [((length, part), FULL)],
            [column] * teams + [pl.BlockSpec((length, LANES), lambda p, a: (0, p))],
            [],
            length * length * dim * heads * 2,
            4 * length * part * 2,
            length * length * heads // 4,
            after=wait,
        )
        logs.append(log)
        if base == 0:
            other = [hop(v, 1) for v in merge]
            got, (*other, g_x, g_y) = meet(got, (*other, *g_near[1:3]))
            g_near = [g_own, g_x, g_y, *g_near[3:]]
            wait = (got[0],)
            attended = exchange(got)
            expand_other = hop(tie(expand_mine, got[0]), 1)
            if teams == 4:
                merge.append(hop(tie(merge[1], got[0]), 4))
        else:
            got, (expand_other, *moved) = meet(got, (expand_other, *attended, *merge[3:]))
            attended = [*moved[:teams], *exchange(got)]
            shrink_other = hop(tie(shrink_mine, got[0]), 1)
            merge = [*merge[:3], *moved[teams:]]
            other += [hop(v, 1) for v in merge[len(other) :]]
    merge = [v for both in zip(merge, other) for v in both]
    if not whole_rows:
        merge = [assemble(merge, extra)]

    weights = (expand_mine, shrink_mine, expand_other, shrink_other)
    wide = ((own_rows, width), FULL)
    wide_low = ((own_rows, width), LOW)
    piece = ((rows, width), LOW)
    g_half = [g_near[1][:rows], g_near[2][rows:]] if teams == 4 else []
    hidden, *second, merge = simple(
        merge_norm_kernel,
        "merge_norm",
        (*attended, *merge, x_own, vec),
        [wide, piece, piece, (merge_shape, LOW)],
        [wide_low, wide_low, (merge_shape, FULL)],
        2 * own_rows * width * span * teams,
        after=tuple(g_half),
        count=teams,
        rows=rows,
        span=span,
        share=share,
        dim=dim,
        parts=len(merge),
    )
    near = [hop(v, 2 * k) for k in range(1, teams) if teams != 4 or k < 3 for v in second]
    second = [*second, *near]
    g_pieces = g_near

    e_row = e_bias.reshape(dp_n, teams, 2, hr).transpose(1, 2, 0, 3)
    e_row = pick(e_row, team)
    e_row = jnp.stack([pick(e_row, core), pick(e_row, 1 - core)])
    e_row = jnp.pad(e_row, ((0, 0), (0, 0), (0, hp - hr))).reshape(1, units)

    groups = [[0], [1, 2], [3, 4]] if teams == 4 else [[k] for k in range(teams)]
    halves = [[0, 1], [2, 3, 4, 5], [6, 7]] if teams == 4 else [[2 * k, 2 * k + 1] for k in range(teams)]
    acts, d_pres, e_sums, d_second, out = [], [], [], [], []
    for group, halved in zip(groups, halves):
        sizes = [x_sizes[i] for i in group]
        out_sizes = sizes if len(sizes) == 1 else [rows] * (sum(sizes) // rows)
        n, m = len(out_sizes), sum(sizes)
        half_spec = pl.BlockSpec((m, half), lambda f, a: (0, f))
        res = call(
            functools.partial(feed_kernel, rows, sizes, out_sizes),
            "feed",
            (2,),
            at,
            (*[second[i] for i in halved], *[g_pieces[i] for i in group], *weights, e_row),
            [piece_spec] * len(halved)
            + row_specs(sizes)
            + [pl.BlockSpec(memory_space=pl.ANY)] * 4
            + [pl.BlockSpec((1, half), lambda f, a: (0, f))],
            [((m, units), LOW)] * 2
            + [((8, units), FULL)]
            + [((size, width), LOW) for size in out_sizes] * 2,
            [half_spec, half_spec, pl.BlockSpec((8, half), lambda f, a: (0, f))]
            + row_specs(out_sizes) * 2,
            [pltpu.VMEM((m, width), LOW)] * 2
            + [pltpu.VMEM((m, width), FULL)] * 2
            + [
                pltpu.VMEM((2, half, width), LOW),
                pltpu.VMEM((2, width, half), LOW),
                pltpu.SemaphoreType.DMA((4,)),
            ],
            8 * m * width * units,
            4 * width * units + 12 * m * width,
            m * units,
            after=tuple(acts[-1:]),
        )
        if len(acts) == 0:
            res, moved = meet(res, second[2:])
            second = [*second[:2], *moved]
            if teams == 4:
                second += [hop(moved[0], 4), hop(moved[3], 2)]
                x, y = (tie(v, *moved) for v in g_half)
                g_pieces = [*g_pieces, hop(x, 4), hop(y, 2)]
        elif len(acts) == 1 and teams == 4:
            res, moved = meet(res, (*second[6:], *g_pieces[3:]))
            second, g_pieces = [*second[:6], *moved[:2]], [*g_pieces[:3], *moved[2:]]
            early = reduce_early([None, *res[3 : 3 + n]])
        elif teams == 4:
            res, early = meet(res, early)
        acts.append(res[0])
        d_pres.append(res[1])
        e_sums.append(res[2])
        d_second += res[3 : 3 + n]
        out += res[3 + n :]

    sizes = [v.shape[0] for v in acts]
    def feed_grad(name, parts, units_of, turned, after):
        shape = (width, half) if turned else (half, width)
        return call(
            functools.partial(feed_grad_kernel, [v.shape[0] for v in parts], sizes, turned),
            name,
            (2,),
            at,
            (*parts, *units_of),
            [pl.BlockSpec(memory_space=pl.ANY)] * len(parts)
            + [pl.BlockSpec((s, half), lambda f, a: (0, 1 - f)) for s in sizes],
            [(shape, LOW)] * 2,
            [fixed(shape)] * 2,
            [
                pltpu.VMEM((length, width), LOW),
                pltpu.VMEM((length, half), LOW),
                pltpu.SemaphoreType.DMA((len(parts),)),
            ],
            2 * length * width * units,
            2 * act_bytes + 2 * width * units,
            after=after,
        )

    if teams != 4:
        early = reduce_early(d_second)
    far = reduce_far(d_second)
    sm, sg = feed_grad("shrink_grad", g_pieces, acts, True, ())
    (sm, sg), far = meet((sm, sg), far)
    late, folded = reduce_late(d_second, far)
    s_got = hop(sg, 1)
    out_early = reduce_early([tie(v, *folded[:1]) for v in out])
    em, eg = feed_grad("expand_grad", second, d_pres, False, (sm, *folded))
    (em, eg), (s_got, *late) = meet((em, eg), (s_got, *late))
    d_second = reduce_terms(d_second, early, late)
    s_sum = add_low(sm, s_got)
    e_got = hop(eg, 1)
    g_shrink = scatter(s_sum.reshape(dp_n, cols, half))

    terms = len(d_second)
    window = ((own_rows, span), LOW)
    d_hidden, d_branch, second_sums, *d_attended = simple(
        second_back_kernel,
        "second_back",
        (*d_second, hidden, g_own, merge, vec),
        [wide, wide_low, ((8, width), FULL)] + [window] * teams,
        [wide, wide_low],
        2 * own_rows * width * span * teams,
        after=(s_sum,),
        count=teams,
        rows=rows,
        span=span,
        dim=dim,
        terms=terms,
    )
    d_attended = exchange(d_attended)

    step = min(span, CHUNK)
    feat_block = ((teams, feats, width), LOW)
    mine, give = simple(
        merge_grad_kernel,
        "merge_grad",
        (*attended, d_branch),
        [feat_block, feat_block],
        [(merge_shape, FULL), ((teams * (span // step), own_rows, step), LOW)],
        2 * own_rows * width * span * teams,
        count=teams,
        span=span,
        share=share,
        dim=dim,
        step=step,
    )

    (mine, give), (e_got, *moved) = meet((mine, give), (e_got, *d_attended, *out_early))
    d_attended, out_early = moved[:teams], moved[teams:]
    e_sum = add_low(em, e_got)
    g_expand = scatter(e_sum.reshape(dp_n, hp, width))

    def core_parts(mine, got):
        return simple(
            add_parts_kernel,
            "add_parts",
            (mine, got),
            [(mine.shape[1:], LOW)] * teams,
        )

    g_merge = core_parts(mine, hop(give, 1))
    merge_near = exchange([tie(v, *d_attended) for v in g_merge])[1:]

    d_parts, wait = [], (e_sum, mixed, g_merge[0])
    for base, count in runs:
        (d_part,) = call(
            functools.partial(attend_backward_kernel, teams, own_rows, dim, heads, share, base),
            "attend_backward",
            (count,),
            at,
            (mixed, mixed, mixed, *d_attended, *segs, logs[len(d_parts)]),
            qkv_specs(base)
            + [pl.BlockSpec((own_rows, LANES), lambda p, a, base=base: (0, base + p))] * teams
            + seg_specs
            + [pl.BlockSpec((length, LANES), lambda p, a: (0, p))],
            [((3, length, part), LOW)],
            [pl.BlockSpec((3, length, LANES), lambda p, a: (0, 0, p))],
            [
                pltpu.VMEM((length, dim), FULL),
                pltpu.VMEM((length, dim), FULL),
                pltpu.VMEM((length, LANES), LOW),
                pltpu.VMEM((LANES, length), FULL),
            ],
            5 * length * length * dim * heads,
            8 * length * part * 2,
            length * length * heads // 4,
            after=wait,
        )
        if base == 0:
            (d_part,), merge_near = meet((d_part,), merge_near)
            out_far = reduce_far([*out[:5], *[tie(v, d_part) for v in out[5:]]])
            wait = (d_part,)
        else:
            (d_part,), out_far = meet((d_part,), out_far)
            out_late, folded = reduce_late(out, out_far)
        d_parts.append(d_part)

    mix_block = ((teams, feats, 3 * span), LOW)
    mine, give, mix_sums = call(
        mix_grad_kernel,
        "mix_grad",
        (3,),
        at,
        (*d_parts, first_t),
        [pl.BlockSpec((1, length, part), lambda c, a: (c, 0, 0))] * 2 + [fixed((width, length))],
        [mix_block, mix_block, ((8, 3 * span), FULL)],
        [pl.BlockSpec((teams, feats, span), lambda c, a: (0, 0, c))] * 2
        + [pl.BlockSpec((8, span), lambda c, a: (0, c))],
        [pltpu.VMEM((width, span), FULL), pltpu.VMEM((length, span), LOW)],
        2 * length * width * 3 * span,
        3 * act_bytes,
        after=tuple(folded[:1]),
    )
    mix_sums = mix_sums[0].reshape(3, span)
    (mine, give), out_late = meet((mine, give), out_late)
    mix_got = hop(give, 1)
    feed_cuts = simple(
        split_feed_kernel,
        "split_feed",
        (g_expand, g_shrink),
        [feed_cut] * teams,
        teams=teams,
        after=(give,),
        hp=hp,
    )
    out = reduce_terms(out, out_early, out_late)
    block_out = simple(
        block_out_kernel,
        "block_out",
        (*out, hidden, vec),
        [piece, piece],
        after=(give,),
        rows=rows,
        terms=terms,
    )
    g_merge = [g_merge[0], *merge_near]
    g_merge = functools.reduce(jnp.add, [v.astype(FULL) for v in g_merge]).astype(LOW)
    merge_each = width // dp_n
    g_merge = jnp.stack(
        [g_merge[:, d * merge_each : (d + 1) * merge_each] for d in range(dp_n)]
    )
    grad_merge = scatter(g_merge).astype(FULL)

    groups = [([3, 4], 3), ([1, 2], 1), ([0], 0)] if teams == 4 else [([k], k) for k in range(teams)]
    kept, (mix_got,) = meet((*block_out, *feed_cuts), (mix_got,))
    block_out, feed_cuts = kept[:2], kept[2:]
    g_mix = core_parts(mine, mix_got)
    d_first, first_sums, wait = [], [], (g_mix[0], g_merge)
    feed_cuts, g_mix = exchange(feed_cuts), exchange(g_mix)
    block_out = swap_out(*block_out)
    far = early = ()
    for group, low in groups:
        sizes = [x_sizes[i] for i in group]
        out_sizes = sizes if len(sizes) == 1 else [rows] * (sum(sizes) // rows)
        n = sum(sizes) // own_rows
        sums, *got = call(
            functools.partial(first_back_kernel, sizes, out_sizes, rows, span),
            "first_back",
            (n,),
            at,
            (*d_parts, *[x_pieces[i] for i in group], mix),
            [
                pl.BlockSpec(
                    (3, own_rows, part), lambda i, a, low=low: (0, (i + low) ^ (a[0] // 2), 0)
                )
            ]
            * 2
            + row_specs(sizes)
            + [fixed((width, 3 * span))],
            [((8, width), FULL)] + [((size, width), LOW) for size in out_sizes],
            [vec_spec] + row_specs(out_sizes),
            [
                pltpu.VMEM((own_rows, width), LOW),
                pltpu.VMEM((own_rows, width), LOW),
                pltpu.VMEM((own_rows, 3 * span), LOW),
            ],
            2 * n * own_rows * width * 3 * span,
            n * own_rows * width * 8,
            after=wait,
        )
        first_sums.append(sums)
        if not d_first:
            got, moved = meet(got, feed_cuts[1:])
            feed_cuts = [feed_cuts[0], *moved]
            wait = (sums,)
            far = reduce_far([None] * 5 + list(got))
        elif len(first_sums) == 2:
            got, moved = meet(got, g_mix[1:])
            g_mix = [g_mix[0], *moved]
            wait = (sums,)
            if teams == 4:
                early = reduce_early([None, *got])
        else:
            got, far = meet(got, far)
        d_first.append(got)
    (g_mix,) = simple(
        join_mix_kernel,
        "join_mix",
        g_mix,
        [((dp_n, feats, each), LOW)],
        [((teams, feats, 3 * span), LOW), ((feats, 3 * width), LOW)],
        teams=teams,
        dp_n=dp_n,
        each=each,
        span=span,
        starts=starts,
        width=width,
    )
    grad_mix = scatter(g_mix).astype(FULL)
    first_sums = functools.reduce(jnp.add, first_sums)
    if teams == 4:
        d_first = [*d_first[2], *d_first[1], *d_first[0]]
    else:
        d_first = [v for got in d_first for v in got]
        early = reduce_early(d_first)
    ek, eg, sk, sg = simple(
        part_feed_kernel,
        "part_feed",
        feed_cuts,
        [(e_shape, LOW), (e_shape, LOW), (s_shape, LOW), (s_shape, LOW)],
        [((teams, 2, hr, cols), LOW)],
        teams=teams,
    )
    late, folded = reduce_late(d_first, far, (g_mix, ek))
    def spread(v):
        return lax.dynamic_update_slice_in_dim(
            jnp.zeros((width + 2 * LANES,), FULL), v, start, 0
        )[:width]

    d_e = functools.reduce(jnp.add, [s[0] for s in e_sums]).reshape(2, dp_n, hp)[:, :, :hr]
    d_e = jnp.where(core == 0, d_e, d_e[::-1]).transpose(1, 0, 2)
    d_e = lax.dynamic_update_slice_in_dim(
        jnp.zeros((dp_n, teams, 2, hr), FULL), d_e[:, None], team, 1
    )
    partial = (
        first_sums[0],
        first_sums[1],
        spread(mix_sums[0]),
        spread(mix_sums[2]),
        second_sums[2],
        second_sums[0],
        second_sums[1],
        second_sums[3],
        d_e.reshape(-1),
    )
    partial = jnp.concatenate([v.reshape(seq_n, -1) for v in partial], axis=1)
    total = reduce_small(tie(partial, *folded[:1]))
    (ek, sk), (total, *early) = meet((ek, sk), (total, *early))
    d_first = reduce_terms(d_first, early, late)
    grad_expand, grad_shrink = simple(
        end_feed_kernel,
        "end_feed",
        (ek, hop(eg, 1), sk, hop(sg, 1)),
        [(expand_weight.shape, FULL), (shrink_weight.shape, FULL)],
        teams=teams,
        hr=hr,
    )

    piece_full = ((rows, width), FULL)
    input_grad = simple(
        input_grad_kernel,
        "input_grad",
        (*d_first, d_hidden, x_own, vec),
        [piece_full, piece_full],
        after=(grad_expand,),
        rows=rows,
        terms=terms,
    )
    input_grad = swap_out(*input_grad)

    ends = [total[i * feats : (i + 1) * feats] for i in range(8)]
    vectors = (*ends[:7], total[8 * feats :], ends[7])
    return (block_out, input_grad, grad_mix, grad_merge, grad_expand, grad_shrink, *vectors)


def solution(mesh):
    rows = P("dp", "seq", None)
    matrix = P("seq", "dp")
    vector = P("seq")
    return jax.shard_map(
        functools.partial(body, mesh.shape["seq"], mesh.shape["dp"]),
        mesh=mesh,
        in_specs=(rows, P("dp", None), rows) + (matrix,) * 4 + (vector,) * 9,
        out_specs=(rows, rows) + (matrix,) * 4 + (vector,) * 9,
        check_vma=False,
    )
```
